32 devices in a mesh: rows: 4 (over y, x), bytes: 8 (over z, core).
Axes of the slice: x: 2, y: 2, z: 4, core: 2. Of those that a mesh axis runs over, the one named last changes fastest.
Arguments:
- tokens: bfloat16 [8, 1024, 1024], P('rows', 'bytes'), may hold values from -6 to 6
- boundaries: int32 [8, 16], P('rows'), may hold values from 1 to 1024, as said below
- norm_gain: float32 [2, 1024], replicated, may hold values from 0.25 to 1.75
- in_weight: bfloat16 [2, 4096, 1024], P(None, ('rows', 'bytes')), may hold values from -0.1875 to 0.1875
- out_weight: bfloat16 [2, 2048, 1024], P(None, ('rows', 'bytes')), may hold values from -0.375 to 0.375
- conv_weight: float32 [2, 4, 2048], P(None, None, 'bytes'), may hold values from -3 to 3
- conv_bias: float32 [2, 2048], P(None, 'bytes'), may hold values from -0.5 to 0.5
- xproj_weight: bfloat16 [2, 2048, 96], P(None, 'bytes'), may hold values from -0.25 to 0.25
- dtproj_weight: bfloat16 [2, 64, 2048], P(None, None, 'bytes'), may hold values from -0.75 to 0.75
- dt_bias: float32 [2, 2048], P(None, 'bytes'), may hold values from -5 to -3
- decay_log: float32 [2, 16, 2048], P(None, None, 'bytes'), may hold values from -11 to 0.5
- skip_gain: float32 [2, 2048], P(None, 'bytes'), may hold values from 0.5 to 1.5
- cotangent: bfloat16 [8, 1024, 1024], P('rows', 'bytes'), may hold values from -6 to 6
Outputs:
- activations: float32 [8, 1024, 1024], P('rows', 'bytes')
- grad_tokens: float32 [8, 1024, 1024], P('rows', 'bytes')
- grad_norm_gain: float32 [2, 1024], replicated
- grad_in_weight: float32 [2, 4096, 1024], P(None, ('rows', 'bytes'))
- grad_out_weight: float32 [2, 2048, 1024], P(None, ('rows', 'bytes'))
- grad_conv_weight: float32 [2, 4, 2048], P(None, None, 'bytes')
- grad_conv_bias: float32 [2, 2048], P(None, 'bytes')
- grad_xproj_weight: float32 [2, 2048, 96], P(None, 'bytes')
- grad_dtproj_weight: float32 [2, 64, 2048], P(None, None, 'bytes')
- grad_dt_bias: float32 [2, 2048], P(None, 'bytes')
- grad_decay_log: float32 [2, 16, 2048], P(None, None, 'bytes')
- grad_skip_gain: float32 [2, 2048], P(None, 'bytes')
The draws below stay inside these ranges and needn't reach their ends.
Inputs may be any that keep to these rules, and one draw needn't show every extreme that they name: `boundaries`: each row lists the first positions of its later segments in rising order, repeats allowed, then 1024 in unused slots; in every aligned group of 2 rows exactly one row holds 1024 only.
All inputs are finite; a program needn't handle non-finite values.
Results may differ from the reference program's by a relative error of at most 0.02385.
Values may be sent and summed in bfloat16 or wider, within the bound.
A program may use at most 768 MiB of HBM per device.

```python
import jax
import jax.numpy as jnp
from jax import lax

D = 1024
DI = 2048
NS = 16
KERNEL = 4
RANK = 64
LAYERS = 2
NBND = 16
SEQ_DEV = 2
SEQS = 8
LEN = 1024


def draw_boundaries(key, part):
    key = jax.random.fold_in(key, 11)
    key_pos, key_count, key_whole = jax.random.split(key, 3)
    places = jax.random.randint(key_pos, (SEQS, NBND), 1, LEN)
    counts = jax.random.randint(key_count, (SEQS, 1), 1, NBND + 1)
    in_use = jnp.arange(NBND)[None, :] < counts
    picked = jax.random.randint(key_whole, (SEQS // SEQ_DEV,), 0, SEQ_DEV)
    whole_row = jnp.arange(SEQS) % SEQ_DEV == jnp.repeat(picked, SEQ_DEV)
    in_use = in_use & jnp.logical_not(whole_row)[:, None]
    return jnp.sort(jnp.where(in_use, places, LEN), axis=1).astype(jnp.int32)


def block_scale(own_key, dims, shards, low, top_value):
    gain = 1.0
    for dim, shards_of in shards:
        steps = jax.random.uniform(jax.random.fold_in(jax.random.fold_in(own_key, 6), dim), (shards_of,), jnp.float32, low / len(shards), top_value / len(shards))
        gain = gain * jnp.repeat(jnp.exp(steps), dims[dim] // shards_of).reshape((-1,) + (1,) * (len(dims) - 1 - dim))
    return gain


def bell_draw(stream_key, extent, spread, most, cuts=(), held_as=jnp.bfloat16):
    factor_of = block_scale(stream_key, extent, cuts, -0.22, 0.18) if cuts else 1.0
    values = jax.random.normal(stream_key, extent, jnp.float32) * spread * factor_of
    return jnp.minimum(jnp.maximum(values, -most), most).astype(held_as)


def setup_inputs(seed: int = 0) -> dict:
    seeds = jax.random.split(jax.random.key(seed), 14)
    tokens = bell_draw(seeds[0], (SEQS, LEN, D), 1.0, 6.0, ((0, 4), (1, 8)))
    boundaries = draw_boundaries(jax.random.fold_in(seeds[13], 71), 0)
    norm_gain = jnp.clip(1.0 + 0.15 * jax.random.normal(seeds[2], (LAYERS, D), jnp.float32), 0.25, 1.75)
    in_weight = bell_draw(seeds[3], (LAYERS, 2 * DI, D), D ** -0.5, 0.1875, ((1, 32),))
    out_weight = bell_draw(seeds[4], (LAYERS, DI, D), (DI // 8) ** -0.5, 0.375, ((1, 32),))
    conv_weight = bell_draw(seeds[5], (LAYERS, KERNEL, DI), KERNEL ** -0.5, 3.0, ((2, 8),), jnp.float32)
    conv_bias = jnp.clip(jax.random.uniform(seeds[6], (LAYERS, DI), jnp.float32, -0.5, 0.5) * block_scale(seeds[6], (LAYERS, DI), ((1, 8),), -0.4, 0.0), -0.5, 0.5)
    xproj_weight = bell_draw(seeds[7], (LAYERS, DI, RANK + 2 * NS), (DI // 4) ** -0.5, 0.25, ((1, 8),))
    dtproj_weight = bell_draw(seeds[8], (LAYERS, RANK, DI), RANK ** -0.5, 0.75, ((2, 8),))
    dt_bias = jnp.clip(-5.0 + 2.0 * jax.random.uniform(seeds[9], (LAYERS, DI), jnp.float32) ** block_scale(seeds[9], (LAYERS, DI), ((1, 8),), -0.2, 0.2), -5.0, -3.0)
    decay_log = jnp.clip(-11.0 + 11.5 * jax.random.uniform(seeds[10], (LAYERS, NS, DI), jnp.float32) ** block_scale(seeds[10], (LAYERS, NS, DI), ((2, 8),), -0.2, 0.2), -11.0, 0.5)
    skip_gain = jnp.clip(0.5 + 1.0 * jax.random.uniform(seeds[11], (LAYERS, DI), jnp.float32) ** block_scale(seeds[11], (LAYERS, DI), ((1, 8),), -0.2, 0.2), 0.5, 1.5)
    cotangent = bell_draw(seeds[12], (SEQS, LEN, D), 1.0, 6.0, ((0, 4), (1, 8)))
    return dict(tokens=tokens, boundaries=boundaries, norm_gain=norm_gain, in_weight=in_weight, out_weight=out_weight, conv_weight=conv_weight, conv_bias=conv_bias, xproj_weight=xproj_weight, dtproj_weight=dtproj_weight, dt_bias=dt_bias, decay_log=decay_log, skip_gain=skip_gain, cotangent=cotangent)


norm_eps = 1e-05
highest = lax.Precision.HIGHEST

@jax.custom_vjp
def low(v):
    return lax.optimization_barrier(v.astype(jnp.bfloat16)).astype(jnp.float32)

@jax.custom_vjp
def low_back(v):
    return v

def low_keep(v):
    return (low(v), None)

def low_pass(kept, grad):
    return (grad,)

def back_keep(v):
    return (v, None)

def back_low(kept, grad):
    return (low(grad),)
low.defvjp(low_keep, low_pass)
low_back.defvjp(back_keep, back_low)

def segment_marks(bounds, length):
    places = jnp.arange(length, dtype=jnp.int32)
    reached = bounds[None, :] <= places[:, None]
    starts = lax.optimization_barrier(jnp.max(jnp.where(reached, bounds[None, :], 0), axis=1)).astype(jnp.int32)
    renewed = jnp.any(bounds[None, :] == places[:, None], axis=1)
    survive = jnp.where(renewed, 0.0, 1.0).astype(jnp.float32)
    return (starts, survive)

def causal_conv(signal, kernel, offset, starts):
    length = signal.shape[0]
    places = jnp.arange(length, dtype=jnp.int32)
    tap_count = kernel.shape[0]
    summed = offset[None, :] + kernel[tap_count - 1][None, :] * signal
    for lag_steps in range(1, tap_count):
        delayed = jnp.concatenate([jnp.zeros((lag_steps, signal.shape[1]), signal.dtype), signal[:-lag_steps]], axis=0)
        inside = jnp.where(places - lag_steps >= starts, 1.0, 0.0).astype(signal.dtype)
        summed = summed + kernel[tap_count - 1 - lag_steps][None, :] * delayed * inside[:, None]
    return jax.nn.silu(summed)

def combine_steps(earlier, later):
    return (earlier[0] * later[0], later[0] * earlier[1] + later[1])

def selective_scan(signal, project, dt_weight, dt_offset, decay_log, skip_gain, survive, block_len):
    rank_len = dt_weight.shape[0]
    state_len = decay_log.shape[0]
    low_rank = project[:, :rank_len]
    input_map = project[:, rank_len:rank_len + state_len]
    output_map = project[:, rank_len + state_len:]
    step_size = jax.nn.softplus(jnp.dot(low_rank, dt_weight, precision=highest) + dt_offset[None, :])
    decay_rates = -jnp.exp(decay_log)
    length, channel_len = signal.shape
    blocks = length // block_len
    pieces = (step_size.reshape(blocks, block_len, channel_len), (step_size * signal).reshape(blocks, block_len, channel_len), input_map.reshape(blocks, block_len, state_len), output_map.reshape(blocks, block_len, state_len), survive.reshape(blocks, block_len))

    def advance(carried, block_in):
        step_part, drive_in, enter_map, leave_map, kept_mask = block_in
        fading = jnp.exp(step_part[:, None, :] * decay_rates[None]) * kept_mask[:, None, None]
        pushes = drive_in[:, None, :] * enter_map[:, :, None]
        fade_all, push_all = lax.associative_scan(combine_steps, (fading, pushes), axis=0)
        states = push_all + fade_all * carried[None]
        return (states[-1], lax.optimization_barrier(jnp.sum(states * leave_map[:, :, None], axis=1)))
    last_state, outputs = lax.scan(jax.checkpoint(advance), jnp.zeros((state_len, channel_len), signal.dtype), pieces)
    return outputs.reshape(length, channel_len) + skip_gain[None, :] * signal

def forward(start_rows, params, starts, survive):
    gains, in_full, out_full, kernels, offsets, proj_weights, step_weights, step_bias, decays, skips = params
    current = start_rows
    for depth_no in range(LAYERS):
        scale = lax.rsqrt(lax.optimization_barrier(jnp.mean(current * current, axis=1, keepdims=True)) + norm_eps)
        normed = low(current * scale * gains[depth_no][None, :])
        projected = jnp.dot(normed, in_full[depth_no].T, precision=highest)
        signal = low_back(low(projected[:, :DI]))
        gate_in = low_back(projected[:, DI:])
        activated = causal_conv(signal, kernels[depth_no], offsets[depth_no], starts)
        project = jnp.dot(activated, proj_weights[depth_no], precision=highest)
        scanned = selective_scan(activated, project, step_weights[depth_no], step_bias[depth_no], decays[depth_no], skips[depth_no], survive, min(128, LEN))
        scanned = low_back(low(scanned))
        gated = low(scanned * jax.nn.silu(gate_in))
        branch = low_back(jnp.dot(gated, out_full[depth_no], precision=highest))
        current = current + branch
    return current

def reference(tokens, boundaries, norm_gain, in_weight, out_weight, conv_weight, conv_bias, xproj_weight, dtproj_weight, dt_bias, decay_log, skip_gain, cotangent):
    weights = tuple((item.astype(jnp.float32) for item in (norm_gain, in_weight, out_weight, conv_weight, conv_bias, xproj_weight, dtproj_weight, dt_bias, decay_log, skip_gain)))
    zero_grads = tuple((jnp.zeros_like(item) for item in weights))

    def one_sequence(totals, inputs):
        row_tokens, bounds, row_cot = inputs
        starts, survive = segment_marks(bounds, LEN)

        def run_rows(start_rows, *params):
            return forward(start_rows, params, starts, survive)
        result, pull = jax.vjp(run_rows, row_tokens.astype(jnp.float32), *weights)
        grads = pull(row_cot.astype(jnp.float32))
        totals = tuple((left + right for left, right in zip(totals, grads[1:])))
        return (totals, (result, grads[0]))
    totals, (outputs, input_grads) = lax.scan(one_sequence, zero_grads, (tokens, boundaries, cotangent))
    return (outputs, input_grads, totals[0], totals[1], totals[2], totals[3], totals[4], totals[5], totals[6], totals[7], totals[8], totals[9])
```

```python
import functools

import jax
import jax.numpy as jnp
from jax import lax
from jax.experimental import pallas as pl
from jax.experimental.pallas import tpu as pltpu
from jax.sharding import PartitionSpec as P

norm_eps = 1e-05
f32 = jnp.float32
bf16 = jnp.bfloat16
STEPS = 8
CB = 256
KILL = 1e30
LOG2E = 1.4426950408889634
VMEM = 48 * 2**20

NT = (((1,), (1,)), ((), ()))


def dot(a, b):
    return jnp.dot(a, b, preferred_element_type=f32)


def dot_nt(a, b):
    return lax.dot_general(a, b, NT, preferred_element_type=f32)


def halves(v):
    high = v.astype(bf16)
    return high, (v - high.astype(f32)).astype(bf16)


def wide(v, width):
    return jnp.concatenate([v] * (width // v.shape[1]), axis=1)


def sigmoid(v):
    return 1.0 / (1.0 + jnp.exp(-v))


def conv_sum(x, halo, kernel, offset, masks, rows):
    length = x.shape[0] // rows
    taps = kernel.shape[0]
    outs = []
    for s in range(rows):
        ext = jnp.concatenate([halo[8 * s : 8 * s + 8], x[s * length : (s + 1) * length]], axis=0)
        total = offset + kernel[taps - 1 : taps] * ext[8:]
        for lag in range(1, taps):
            moved = pltpu.roll(ext, lag, 0)[8:]
            m = masks[lag - 1][s * length : (s + 1) * length]
            total = total + kernel[taps - 1 - lag : taps - lag] * moved * m
        outs.append(total)
    return jnp.concatenate(outs, axis=0)


def conv_kernel(rows, x_ref, halo_ref, kern_ref, off_ref, mask_ref, xp_ref, act_ref, proj_ref):
    @pl.when(pl.program_id(0) == 0)
    def _():
        proj_ref[...] = jnp.zeros_like(proj_ref)

    x = x_ref[...].astype(bf16).astype(f32)
    cb = x.shape[1]
    masks = [wide(mask_ref[i], cb) for i in range(mask_ref.shape[0])]
    pre = conv_sum(x, halo_ref[...].astype(f32), kern_ref[...], off_ref[...], masks, rows)
    act = pre * sigmoid(pre)
    act_ref[...] = act
    high, low = halves(act)
    weight = xp_ref[...]
    proj_ref[...] += dot_nt(high, weight) + dot_nt(low, weight)


def step_sizes(rank2_ref, dtw_ref, bias_ref):
    weight = dtw_ref[...]
    pre = dot(rank2_ref[...], jnp.concatenate([weight, weight], axis=0)) + bias_ref[...]
    return jnp.maximum(pre, 0.0) + jnp.log1p(jnp.exp(-jnp.abs(pre)))


def chunked(v):
    return v.reshape(v.shape[0] // STEPS, STEPS, v.shape[1])


def tokens_of(ref, rows, k):
    per = ref.shape[0] // rows
    return jnp.concatenate([ref[s * per + k] for s in range(rows)], axis=0)


def drive_of(bd_ref, u_ref, rows, k):
    high, low = halves(tokens_of(u_ref, rows, k))
    return dot(bd_ref[k], jnp.concatenate([high, low, high], axis=0))


def ends_kernel(rows, act_ref, rank2_ref, dtw_ref, bias_ref, kill_ref, rate_ref, bd_ref,
                delta_ref, end_ref, sum_ref, eff_s, u_s, drive_s):
    delta = step_sizes(rank2_ref, dtw_ref, bias_ref)
    cb = delta.shape[1]
    delta_ref[...] = delta
    eff = delta + wide(kill_ref[...], cb)
    eff_s[...] = chunked(eff)
    u_s[...] = chunked(delta * act_ref[...])
    length = eff.shape[0] // rows
    sum_ref[...] = jnp.concatenate(
        [jnp.sum(eff[s * length : (s + 1) * length], axis=0, keepdims=True) for s in range(rows)], axis=0
    )
    rate = rate_ref[...] * LOG2E
    ns = rate.shape[0]
    chunks = length // STEPS

    def chunk(k, state):
        state = list(state)
        drive_s[...] = drive_of(bd_ref, u_s, rows, k)
        for t in range(STEPS):
            for s in range(rows):
                at = (s * STEPS + t) * ns
                fade = jnp.exp2(rate * eff_s[s * chunks + k, t : t + 1, :])
                state[s] = fade * state[s] + drive_s[at : at + ns, :]
        return tuple(state)

    zero = jnp.zeros((ns, cb), f32)
    state = lax.fori_loop(0, chunks, chunk, (zero,) * rows)
    for s in range(rows):
        end_ref[s * ns : (s + 1) * ns, :] = state[s]


def scan_kernel(rows, act_ref, delta_ref, z_ref, kill_ref, rate_ref, skip_ref, bd_ref, cd_ref, start_ref,
                y_ref, gated_ref, keep_ref, eff_s, u_s, drive_s, state_s, y_s):
    delta = delta_ref[...]
    cb = delta.shape[1]
    eff_s[...] = chunked(delta + wide(kill_ref[...], cb))
    u_s[...] = chunked(delta * act_ref[...])
    rate = rate_ref[...] * LOG2E
    ns = rate.shape[0]
    length = delta.shape[0] // rows
    chunks = length // STEPS

    def chunk(k, state):
        state = list(state)
        for s in range(rows):
            keep_ref[k, s * ns : (s + 1) * ns, :] = state[s]
        drive_s[...] = drive_of(bd_ref, u_s, rows, k)
        for t in range(STEPS):
            for s in range(rows):
                at = (s * STEPS + t) * ns
                fade = jnp.exp2(rate * eff_s[s * chunks + k, t : t + 1, :])
                state[s] = fade * state[s] + drive_s[at : at + ns, :]
                state_s[at : at + ns, :] = state[s].astype(bf16)
        y = dot(cd_ref[k], state_s[...])
        for s in range(rows):
            y_s[s * chunks + k] = y[s * STEPS : (s + 1) * STEPS]
        return tuple(state)

    lax.fori_loop(0, chunks, chunk, tuple(start_ref[s * ns : (s + 1) * ns, :] for s in range(rows)))
    y = (y_s[...].reshape(delta.shape) + skip_ref[...] * act_ref[...]).astype(bf16)
    y_ref[...] = y
    z = z_ref[...]
    gated_ref[...] = (y.astype(f32) * (z * sigmoid(z))).astype(bf16)


def back_ends_kernel(rows, gg_ref, z_ref, y_ref, delta_ref, kill_ref, rate_ref, cg_ref,
                     gy_ref, gz_ref, end_ref, eff_s, gy_s, push_s):
    z = z_ref[...]
    gg = gg_ref[...]
    sig = sigmoid(z)
    gy = (gg * z * sig).astype(bf16)
    gy_ref[...] = gy
    gz_ref[...] = (gg * y_ref[...].astype(f32) * sig * (1.0 + z * (1.0 - sig))).astype(bf16)
    cb = z.shape[1]
    eff_s[...] = chunked(delta_ref[...] + wide(kill_ref[...], cb))
    gy_s[...] = chunked(gy.astype(f32))
    rate = rate_ref[...] * LOG2E
    ns = rate.shape[0]
    length = z.shape[0] // rows
    chunks = length // STEPS

    def chunk(i, flow):
        k = chunks - 1 - i
        flow = list(flow)
        g16 = tokens_of(gy_s, rows, k).astype(bf16)
        push_s[...] = dot(cg_ref[k], jnp.concatenate([g16, g16], axis=0))
        for t in reversed(range(STEPS)):
            for s in range(rows):
                at = (s * STEPS + t) * ns
                fade = jnp.exp2(rate * eff_s[s * chunks + k, t : t + 1, :])
                flow[s] = fade * (flow[s] + push_s[at : at + ns, :])
        return tuple(flow)

    zero = jnp.zeros((ns, cb), f32)
    flow = lax.fori_loop(0, chunks, chunk, (zero,) * rows)
    for s in range(rows):
        end_ref[s * ns : (s + 1) * ns, :] = flow[s]


def back_kernel(rows, act_ref, delta_ref, gy_ref, kill_ref, rate_ref, skip_ref, dtw_ref, rank_t_ref,
                bd_ref, cg_ref, bt_ref, ones_ref, keep_ref, start_ref,
                gact_ref, gc_ref, gb_ref, grank_ref, gdtw_ref, gbias_ref, grate_ref, gskip_ref,
                eff_s, u_s, gy_s, drive_s, push_s, fade_s, held_s, state_s, grad_s, wa_s, gu_s, gd_s):
    @pl.when(pl.program_id(0) == 0)
    def _():
        gc_ref[...] = jnp.zeros_like(gc_ref)
        gb_ref[...] = jnp.zeros_like(gb_ref)
        grank_ref[...] = jnp.zeros_like(grank_ref)

    delta = delta_ref[...]
    act = act_ref[...]
    gy = gy_ref[...].astype(f32)
    cb = delta.shape[1]
    eff_s[...] = chunked(delta + wide(kill_ref[...], cb))
    u_s[...] = chunked(delta * act)
    gy_s[...] = chunked(gy)
    rate_n = rate_ref[...]
    rate = rate_n * LOG2E
    ns = rate.shape[0]
    length = delta.shape[0] // rows
    chunks = length // STEPS

    def chunk(i, carry):
        flow, total = list(carry[0]), carry[1]
        k = chunks - 1 - i
        g16 = tokens_of(gy_s, rows, k).astype(bf16)
        u16 = tokens_of(u_s, rows, k)
        drive_s[...] = drive_of(bd_ref, u_s, rows, k)
        push_s[...] = dot(cg_ref[k], jnp.concatenate([g16, g16], axis=0))
        state = [keep_ref[k, s * ns : (s + 1) * ns, :] for s in range(rows)]
        for t in range(STEPS):
            for s in range(rows):
                at = (s * STEPS + t) * ns
                fade = jnp.exp2(rate * eff_s[s * chunks + k, t : t + 1, :])
                held = fade * state[s]
                fade_s[at : at + ns, :] = fade
                held_s[at : at + ns, :] = held
                state[s] = held + drive_s[at : at + ns, :]
                state_s[at : at + ns, :] = state[s].astype(bf16)
        gc_ref[k] += dot_nt(g16, state_s[...])
        for t in reversed(range(STEPS)):
            for s in range(rows):
                at = (s * STEPS + t) * ns
                grad = flow[s] + push_s[at : at + ns, :]
                grad_s[at : at + ns, :] = grad.astype(bf16)
                w = grad * held_s[at : at + ns, :]
                step = eff_s[s * chunks + k, t : t + 1, :]
                total = total + w * step
                wa_s[at : at + ns, :] = (w * rate_n).astype(bf16)
                flow[s] = fade_s[at : at + ns, :] * grad
        g_all = grad_s[...]
        gb_ref[k] += dot_nt(u16.astype(bf16), g_all)
        gu = dot(bt_ref[k], g_all)
        gd = dot(ones_ref[...], wa_s[...])
        for s in range(rows):
            gu_s[s * chunks + k] = gu[s * STEPS : (s + 1) * STEPS]
            gd_s[s * chunks + k] = gd[s * STEPS : (s + 1) * STEPS]
        return tuple(flow), total

    first = tuple(start_ref[s * ns : (s + 1) * ns, :] for s in range(rows))
    _, total = lax.fori_loop(0, chunks, chunk, (first, jnp.zeros((ns, cb), f32)))
    grate_ref[...] = total * rate_n
    gu = gu_s[...].reshape(delta.shape)
    gact_ref[...] = gu * delta + skip_ref[...] * gy
    gskip_ref[...] = jnp.sum(gy * act, axis=0, keepdims=True)
    gpre = (gu * act + gd_s[...].reshape(delta.shape)) * (1.0 - jnp.exp(-delta))
    gbias_ref[...] = jnp.sum(gpre, axis=0, keepdims=True)
    gpre16 = gpre.astype(bf16)
    gdtw_ref[...] = dot(rank_t_ref[...], gpre16)
    grank_ref[...] += dot_nt(gpre16, dtw_ref[...])


def conv_back_kernel(rows, x_ref, halo_ref, kern_ref, off_ref, mask_ref, act_ref, gact_ref, gproj_ref,
                     gproj_t_ref, xp_ref, gx_ref, edge_ref, gxp_ref, gkern_ref, goff_ref):
    x = x_ref[...].astype(bf16).astype(f32)
    cb = x.shape[1]
    halo = halo_ref[...].astype(f32)
    kernel = kern_ref[...]
    taps = kernel.shape[0]
    masks = [wide(mask_ref[i], cb) for i in range(taps - 1)]
    pre = conv_sum(x, halo, kernel, off_ref[...], masks, rows)
    sig = sigmoid(pre)
    act16 = act_ref[...].astype(bf16)
    gxp_ref[...] = dot(gproj_t_ref[...], act16)
    g_act = gact_ref[...] + dot(gproj_ref[...], xp_ref[...])
    gpre = g_act * sig * (1.0 + pre * (1.0 - sig))
    goff_ref[...] = jnp.sum(gpre, axis=0, keepdims=True)
    length = x.shape[0] // rows
    place = lax.broadcasted_iota(jnp.int32, (length, cb), 0)
    gk = [jnp.zeros((1, cb), f32) for _ in range(taps)]
    for s in range(rows):
        here = slice(s * length, (s + 1) * length)
        g = gpre[here]
        ext = jnp.concatenate([halo[8 * s : 8 * s + 8], x[here]], axis=0)
        gk[taps - 1] = gk[taps - 1] + jnp.sum(g * x[here], axis=0, keepdims=True)
        gx = kernel[taps - 1 : taps] * g
        edge = jnp.zeros((length, cb), f32)
        for lag in range(1, taps):
            gm = g * masks[lag - 1][here]
            moved = pltpu.roll(ext, lag, 0)[8:]
            j = taps - 1 - lag
            gk[j] = gk[j] + jnp.sum(gm * moved, axis=0, keepdims=True)
            up = pltpu.roll(kernel[j : j + 1] * gm, length - lag, 0)
            inside = place < length - lag
            gx = gx + jnp.where(inside, up, 0.0)
            edge = edge + jnp.where(inside, 0.0, up)
        gx_ref[here, :] = gx
        edge_ref[8 * s : 8 * s + 8, :] = edge[length - 8 :]
    gkern_ref[...] = jnp.concatenate(gk, axis=0)


def col(rows, cb, shift=0):
    return pl.BlockSpec((rows, cb), lambda j: (0, j + shift))


def whole(*shape):
    return pl.BlockSpec(shape, lambda j: (0,) * len(shape))


def call(body, blocks, ins, outs, scratch, args):
    return pl.pallas_call(
        body,
        grid=(blocks,),
        in_specs=ins,
        out_specs=[spec for spec, _, _ in outs],
        out_shape=[jax.ShapeDtypeStruct(shape, kind) for _, shape, kind in outs],
        scratch_shapes=scratch,
        compiler_params=pltpu.CompilerParams(
            dimension_semantics=("arbitrary",), vmem_limit_bytes=VMEM
        ),
    )(*args)


class Mixer:
    def __init__(self, rows, length, channels, ns, rank, taps):
        self.rows, self.length, self.c, self.ns, self.rank, self.taps = rows, length, channels, ns, rank, taps
        self.tokens = rows * length
        self.blocks = channels // CB
        self.chunks = length // STEPS
        self.pairs = rows * STEPS
        self.inner = self.pairs * ns
        self.width = rank + 2 * ns

    def conv(self, projected, halo, p, masks):
        t, c = self.tokens, self.c
        return call(
            functools.partial(conv_kernel, self.rows), self.blocks,
            [col(t, CB), col(8 * self.rows, CB), col(self.taps, CB), col(1, CB), whole(*masks.shape), col(self.width, CB)],
            [(col(t, CB), (t, c), f32), (whole(t, self.width), (t, self.width), f32)],
            [], (projected, halo, p["conv_w"], p["conv_b"], masks, p["xproj"]),
        )

    def maps(self, proj):
        r, b, c = proj[:, : self.rank], proj[:, self.rank : self.rank + self.ns], proj[:, self.rank + self.ns :]
        eye = jnp.eye(self.pairs, dtype=f32)

        def per_chunk(v):
            return (
                v.reshape(self.rows, self.chunks, STEPS, self.ns)
                .transpose(1, 0, 2, 3)
                .reshape(self.chunks, self.pairs, self.ns)
            )

        def tall(v):
            return (per_chunk(v)[:, :, :, None] * eye[None, :, None, :]).reshape(self.chunks, self.inner, self.pairs)

        def flat(v):
            return (per_chunk(v)[:, None, :, :] * eye[None, :, :, None]).reshape(self.chunks, self.pairs, self.inner)

        bh, bl = halves(tall(b))
        ch, cl = halves(tall(c))
        rh, rl = halves(r)
        return dict(
            rank2=jnp.concatenate([rh, rl], axis=1),
            rank_t=rh.T,
            bd=jnp.concatenate([bh, bh, bl], axis=2),
            cg=jnp.concatenate([ch, cl], axis=2),
            bt=flat(b).astype(bf16),
            cd=flat(c).astype(bf16),
        )

    def unmap(self, raw):
        eye = jnp.eye(self.pairs, dtype=f32)
        v = raw.reshape(self.chunks, self.pairs, self.pairs, self.ns)
        v = jnp.sum(v * eye[None, :, :, None], axis=1)
        return v.reshape(self.chunks, self.rows, STEPS, self.ns).transpose(1, 0, 2, 3).reshape(self.tokens, self.ns)

    def scratch3(self):
        return pltpu.VMEM((self.tokens // STEPS, STEPS, CB), f32)

    def wide_scratch(self, kind):
        return pltpu.VMEM((self.inner, CB), kind)

    def ends(self, act, m, p, kill):
        t, c, sn = self.tokens, self.c, self.rows * self.ns
        return call(
            functools.partial(ends_kernel, self.rows), self.blocks,
            [col(t, CB), whole(*m["rank2"].shape), col(self.rank, CB), col(1, CB), whole(*kill.shape), col(self.ns, CB),
             whole(*m["bd"].shape)],
            [(col(t, CB), (t, c), f32), (col(sn, CB), (sn, c), f32), (col(self.rows, CB), (self.rows, c), f32)],
            [self.scratch3(), self.scratch3(), self.wide_scratch(f32)],
            (act, m["rank2"], p["dtproj"], p["dt_b"], kill, p["rate"], m["bd"]),
        )

    def scan(self, act, delta, projected, m, p, kill, start):
        t, c, sn = self.tokens, self.c, self.rows * self.ns
        keep = pl.BlockSpec((self.chunks, sn, CB), lambda j: (0, 0, j))
        return call(
            functools.partial(scan_kernel, self.rows), self.blocks,
            [col(t, CB), col(t, CB), col(t, CB, self.blocks), whole(*kill.shape), col(self.ns, CB), col(1, CB),
             whole(*m["bd"].shape), whole(*m["cd"].shape), col(sn, CB)],
            [(col(t, CB), (t, c), bf16), (col(t, CB), (t, c), bf16), (keep, (self.chunks, sn, c), f32)],
            [self.scratch3(), self.scratch3(), self.wide_scratch(f32), self.wide_scratch(bf16), self.scratch3()],
            (act, delta, projected, kill, p["rate"], p["skip"], m["bd"], m["cd"], start),
        )

    def back_ends(self, gg, projected, y, delta, m, p, kill):
        t, c, sn = self.tokens, self.c, self.rows * self.ns
        return call(
            functools.partial(back_ends_kernel, self.rows), self.blocks,
            [col(t, CB), col(t, CB, self.blocks), col(t, CB), col(t, CB), whole(*kill.shape), col(self.ns, CB),
             whole(*m["cg"].shape)],
            [(col(t, CB), (t, c), bf16), (col(t, CB), (t, c), bf16), (col(sn, CB), (sn, c), f32)],
            [self.scratch3(), self.scratch3(), self.wide_scratch(f32)],
            (gg, projected, y, delta, kill, p["rate"], m["cg"]),
        )

    def back(self, act, delta, gy, m, p, kill, keep, start):
        t, c, sn, ns = self.tokens, self.c, self.rows * self.ns, self.ns
        kept = pl.BlockSpec((self.chunks, sn, CB), lambda j: (0, 0, j))
        raw = (self.chunks, self.pairs, self.inner)
        ones = jnp.repeat(jnp.eye(self.pairs, dtype=bf16), ns, axis=1)
        return call(
            functools.partial(back_kernel, self.rows), self.blocks,
            [col(t, CB), col(t, CB), col(t, CB), whole(*kill.shape), col(ns, CB), col(1, CB), col(self.rank, CB),
             whole(*m["rank_t"].shape), whole(*m["bd"].shape), whole(*m["cg"].shape), whole(*m["bt"].shape),
             whole(*ones.shape), kept, col(sn, CB)],
            [(col(t, CB), (t, c), f32), (whole(*raw), raw, f32), (whole(*raw), raw, f32),
             (whole(t, self.rank), (t, self.rank), f32), (col(self.rank, CB), (self.rank, c), f32),
             (col(1, CB), (1, c), f32), (col(ns, CB), (ns, c), f32), (col(1, CB), (1, c), f32)],
            [self.scratch3()] * 3 + [self.wide_scratch(f32)] * 4 + [self.wide_scratch(bf16)] * 3 + [self.scratch3()] * 2,
            (act, delta, gy, kill, p["rate"], p["skip"], p["dtproj"], m["rank_t"], m["bd"], m["cg"], m["bt"], ones,
             keep, start),
        )

    def conv_back(self, projected, halo, p, masks, act, gact, gproj):
        t, c = self.tokens, self.c
        g16 = gproj.astype(bf16)
        return call(
            functools.partial(conv_back_kernel, self.rows), self.blocks,
            [col(t, CB), col(8 * self.rows, CB), col(self.taps, CB), col(1, CB), whole(*masks.shape), col(t, CB),
             col(t, CB), whole(t, self.width), whole(self.width, t), col(self.width, CB)],
            [(col(t, CB), (t, c), f32), (col(8 * self.rows, CB), (8 * self.rows, c), f32),
             (col(self.width, CB), (self.width, c), f32), (col(self.taps, CB), (self.taps, c), f32),
             (col(1, CB), (1, c), f32)],
            [], (projected, halo, p["conv_w"], p["conv_b"], masks, act, gact, g16, g16.T, p["xproj"]),
        )


def carried_in(ends, sums, rate, axis, backward):
    n = lax.axis_size(axis)
    rows = sums.shape[0]
    ns = rate.shape[0]

    def fade(total):
        return jnp.exp(total[:, None, :] * rate[None])

    def moved(v, shift):
        if backward:
            pairs = [(i, i - shift) for i in range(shift, n)]
        else:
            pairs = [(i, i + shift) for i in range(n - shift)]
        return lax.ppermute(v, axis, pairs)

    def shifted(e, s, shift):
        return moved(e.astype(bf16), shift).astype(f32), moved(s, shift)

    ends = ends.reshape(rows, ns, -1)
    ends, sums = shifted(ends, sums, 1)
    shift = 1
    while shift < n - 1:
        e, s = shifted(ends, sums, shift)
        ends = fade(sums) * e + ends
        sums = sums + s
        shift *= 2
    return ends.reshape(rows * ns, -1)


def body(
    tokens, boundaries, norm_gain, in_weight, out_weight, conv_weight, conv_bias, xproj_weight,
    dtproj_weight, dt_bias, decay_log, skip_gain, cotangent,
):
    rows, length, d = tokens.shape
    layers = norm_gain.shape[0]
    both = ("rows", "bytes")
    n = rows * length
    place = lax.axis_index("bytes") * length + jnp.arange(length, dtype=jnp.int32)
    reached = boundaries[:, None, :] <= place[None, :, None]
    starts = jnp.max(jnp.where(reached, boundaries[:, None, :], 0), axis=2)
    renewed = jnp.any(boundaries[:, None, :] == place[None, :, None], axis=2)
    kill = jnp.broadcast_to(jnp.where(renewed, KILL, 0.0).reshape(n, 1), (n, 128)).astype(f32)
    taps = conv_weight.shape[1]
    masks = jnp.stack(
        [
            jnp.broadcast_to((place[None, :] - lag >= starts).astype(f32).reshape(n, 1), (n, 128))
            for lag in range(1, taps)
        ]
    )
    half = jnp.concatenate([xproj_weight.transpose(0, 2, 1), dtproj_weight], axis=1)
    full = jnp.concatenate(
        [conv_weight, conv_bias[:, None], dt_bias[:, None], skip_gain[:, None], -jnp.exp(decay_log)], axis=1
    )
    half = lax.all_gather(half, "bytes", axis=2, tiled=True)
    full = lax.all_gather(full, "bytes", axis=2, tiled=True)
    ns = decay_log.shape[1]
    rank = dtproj_weight.shape[1]
    width = xproj_weight.shape[2]
    channels = full.shape[2]
    mixer = Mixer(rows, length, channels, ns, rank, taps)
    params = []
    for i in range(layers):
        params.append(
            dict(
                xproj=half[i, :width], dtproj=half[i, width:], conv_w=full[i, :taps], conv_b=full[i, taps : taps + 1],
                dt_b=full[i, taps + 1 : taps + 2], skip=full[i, taps + 2 : taps + 3], rate=full[i, taps + 3 :],
            )
        )
    weights = [
        (
            lax.all_gather(in_weight[i], both, axis=0, tiled=True),
            lax.all_gather(out_weight[i], both, axis=0, tiled=True),
        )
        for i in range(layers)
    ]
    size = lax.axis_size("bytes")
    ahead = [(i, i + 1) for i in range(size - 1)]
    behind = [(i + 1, i) for i in range(size - 1)]
    current = tokens.astype(f32).reshape(n, d)
    saved = []
    for i in range(layers):
        p = params[i]
        in_full, out_full = weights[i]
        normed = (
            current * lax.rsqrt(jnp.mean(current * current, axis=-1, keepdims=True) + norm_eps) * norm_gain[i]
        ).astype(bf16)
        projected = dot_nt(normed, in_full)
        tail = projected.reshape(rows, length, -1)[:, length - 8 :, :channels].astype(bf16)
        halo = lax.ppermute(tail, "bytes", ahead).reshape(8 * rows, channels)
        act, proj = mixer.conv(projected, halo, p, masks)
        m = mixer.maps(proj)
        delta, end, total = mixer.ends(act, m, p, kill)
        start = carried_in(end, total, p["rate"], "bytes", False)
        y, gated, keep = mixer.scan(act, delta, projected, m, p, kill, start)
        saved.append((current, normed, projected, halo, act, m, delta, total, y, gated, keep))
        current = current + dot(gated, out_full)
    flowing = cotangent.astype(f32).reshape(n, d)
    big, small, gains = [], [], []
    for i in reversed(range(layers)):
        p = params[i]
        in_full, out_full = weights[i]
        before, normed, projected, halo, act, m, delta, total, y, gated, keep = saved[i]
        down = flowing.astype(bf16)
        grad_out = lax.dot_general(gated, down, (((0,), (0,)), ((), ())), preferred_element_type=f32).astype(bf16)
        gg = dot_nt(down, out_full)
        gy, gz, gend = mixer.back_ends(gg, projected, y, delta, m, p, kill)
        gstart = carried_in(gend, total, p["rate"], "bytes", True)
        gact, graw_c, graw_b, grank, gdtw, gbias, grate, gskip = mixer.back(
            act, delta, gy, m, p, kill, keep, gstart
        )
        gproj = jnp.concatenate([grank, mixer.unmap(graw_b), mixer.unmap(graw_c)], axis=1)
        gx, edge, gxp, gkern, goff = mixer.conv_back(projected, halo, p, masks, act, gact, gproj)
        late = lax.ppermute(edge.astype(bf16), "bytes", behind).astype(f32).reshape(rows, 8, channels)
        gx = (
            (gx.reshape(rows, length, channels) + jnp.pad(late, ((0, 0), (length - 8, 0), (0, 0))))
            .reshape(n, channels)
            .astype(bf16)
        )
        mixed = jnp.concatenate([gx, gz], axis=1)
        grad_in = lax.dot_general(mixed, normed, (((0,), (0,)), ((), ())), preferred_element_type=f32).astype(bf16)
        gn = dot(mixed, in_full)
        inv = lax.rsqrt(jnp.mean(before * before, axis=-1, keepdims=True) + norm_eps)
        scaled = before * inv
        gains.append(jnp.sum(gn * scaled, axis=0))
        gs = gn * norm_gain[i]
        flowing = flowing + inv * (gs - scaled * jnp.mean(gs * scaled, axis=-1, keepdims=True))
        big.append(
            (
                lax.psum_scatter(grad_in, both, scatter_dimension=0, tiled=True).astype(f32),
                lax.psum_scatter(grad_out, both, scatter_dimension=0, tiled=True).astype(f32),
            )
        )
        small.append(jnp.concatenate([gxp, gdtw, grate, gkern, goff, gbias, gskip], axis=0))
    big, small, gains = big[::-1], small[::-1], gains[::-1]
    packed = jnp.stack(small).astype(bf16)
    packed = lax.psum_scatter(packed, "bytes", scatter_dimension=2, tiled=True)
    packed = lax.psum(packed, "rows").astype(f32)
    cuts = [width, rank, ns, taps, 1, 1, 1]
    parts, at = [], 0
    for cut in cuts:
        parts.append(packed[:, at : at + cut])
        at += cut
    gain_total = lax.psum(jnp.stack(gains), both)
    return (
        current.reshape(rows, length, d),
        flowing.reshape(rows, length, d),
        gain_total,
        jnp.stack([b[0] for b in big]),
        jnp.stack([b[1] for b in big]),
        parts[3],
        parts[4][:, 0],
        parts[0].transpose(0, 2, 1),
        parts[1],
        parts[5][:, 0],
        parts[2],
        parts[6][:, 0],
    )


def solution(mesh):
    split = P("rows", "bytes", None)
    shared = P(None, ("rows", "bytes"), None)
    in_specs = (
        split, P("rows", None), P(), shared, shared, P(None, None, "bytes"), P(None, "bytes"),
        P(None, "bytes", None), P(None, None, "bytes"), P(None, "bytes"), P(None, None, "bytes"),
        P(None, "bytes"), split,
    )
    out_specs = (
        split, split, P(), shared, shared, P(None, None, "bytes"), P(None, "bytes"), P(None, "bytes", None),
        P(None, None, "bytes"), P(None, "bytes"), P(None, None, "bytes"), P(None, "bytes"),
    )
    return jax.shard_map(body, mesh=mesh, in_specs=in_specs, out_specs=out_specs, check_vma=False)
```

```python
import functools

import jax
import jax.numpy as jnp
from jax import lax
from jax.experimental import pallas as pl
from jax.experimental.pallas import tpu as pltpu
from jax.sharding import PartitionSpec as P

norm_eps = 1e-05
f32 = jnp.float32
bf16 = jnp.bfloat16
STEPS = 8
CB = 256
CB_ENDS = 512
CB_SCAN = 512
CB_BACK = 512
KILL = 1e30
LOG2E = 1.4426950408889634
VMEM = 58 * 2**20
FORWARD_ONE = (8, 15, 16, 17, 18, 18, 19, 20, 21)
FORWARD_EARLY = (8, 16, 17, 19, 20, 20, 20, 22, 23)
BACKWARD_STEPS = (0, 2, 4, 4, 4, 4, 4, 5, 6, 7, 8)

NT = (((1,), (1,)), ((), ()))


def dot(a, b):
    return jnp.dot(a, b, preferred_element_type=f32)


def dot_nt(a, b):
    return lax.dot_general(a, b, NT, preferred_element_type=f32)


def halves(v):
    high = v.astype(bf16)
    return high, (v - high.astype(f32)).astype(bf16)


def wide(v, width):
    return jnp.concatenate([v] * (width // v.shape[1]), axis=1)


def sigmoid(v):
    return 1.0 / (1.0 + jnp.exp(-v))


def conv_sum(x, halo, kernel, offset, masks, rows):
    length = x.shape[0] // rows
    taps = kernel.shape[0]
    outs = []
    for s in range(rows):
        ext = jnp.concatenate([halo[8 * s : 8 * s + 8], x[s * length : (s + 1) * length]], axis=0)
        total = offset + kernel[taps - 1 : taps] * ext[8:]
        for lag in range(1, taps):
            moved = pltpu.roll(ext, lag, 0)[8:]
            m = masks[lag - 1][s * length : (s + 1) * length]
            total = total + kernel[taps - 1 - lag : taps - lag] * moved * m
        outs.append(total)
    return jnp.concatenate(outs, axis=0)


class Packed:
    def __init__(self, rank, ns, taps):
        self.rank, self.ns, self.taps = rank, ns, taps
        self.width = rank + 2 * ns

    def rate(self, ref):
        return ref.at[0 : self.ns]

    def kernel(self, ref):
        return ref.at[self.ns : self.ns + self.taps]

    def row(self, ref, i):
        return ref.at[self.ns + self.taps + i : self.ns + self.taps + i + 1]

    def offset(self, ref):
        return self.row(ref, 0)

    def bias(self, ref):
        return self.row(ref, 1)

    def skip(self, ref):
        return self.row(ref, 2)

    def xproj(self, ref):
        return ref.at[0 : self.width]

    def dtproj(self, ref):
        return ref.at[self.width : self.width + self.rank]


def maps_part(rows, rank, ns, proj, rank2_ref, rank_t_ref, bb_ref, cc_ref, cd_ref):
    tokens = proj.shape[0]
    high, low = halves(proj[:, :rank])
    rank2_ref[...] = jnp.concatenate([high, low], axis=1)
    turned = proj.T
    rank_t_ref[...] = turned[:rank].astype(bf16)
    per = tokens // rows // STEPS
    for s in range(rows):
        for k in range(per):
            for t in range(STEPS):
                tok = (s * per + k) * STEPS + t
                at = ((k * rows + s) * STEPS + t) * ns
                bb_ref[at : at + ns, :] = jnp.broadcast_to(turned[rank : rank + ns, tok : tok + 1], (ns, 128))
                cc_ref[at : at + ns, :] = jnp.broadcast_to(turned[rank + ns :, tok : tok + 1], (ns, 128))
    inner = cd_ref.shape[-1]
    tile = (
        lax.broadcasted_iota(jnp.int32, (ns, inner), 0) == lax.broadcasted_iota(jnp.int32, (ns, inner), 1) % ns
    ).astype(bf16)
    spread = dot(proj[:, rank + ns :].astype(bf16), tile)
    tok = lax.broadcasted_iota(jnp.int32, (tokens, inner), 0)
    own = (tok // (tokens // rows)) * STEPS + tok % STEPS
    cd = jnp.where(own == lax.broadcasted_iota(jnp.int32, (tokens, inner), 1) // ns, spread, 0.0)
    cd_ref[...] = cd.reshape(cd_ref.shape)


def conv_part(rows, x, halo, kern_ref, off_ref, mask_ref, xp_ref, proj_s):
    cb = x.shape[1]
    masks = [wide(mask_ref[i], cb) for i in range(mask_ref.shape[0])]
    pre = conv_sum(x, halo, kern_ref[...], off_ref[...], masks, rows)
    act = pre * sigmoid(pre)
    high, low = halves(act)
    weight = xp_ref[...]
    proj_s[...] += dot_nt(high, weight) + dot_nt(low, weight)
    return act


def conv_kernel(rows, sizes, x_ref, halo_ref, kern_ref, off_ref, mask_ref, xp_ref,
                act_ref, rank2_ref, rank_t_ref, bb_ref, cc_ref, cd_ref, proj_s):
    block = pl.program_id(0)

    @pl.when(block == 0)
    def _():
        proj_s[...] = jnp.zeros_like(proj_s)

    act_ref[...] = conv_part(
        rows, x_ref[...].astype(bf16).astype(f32), halo_ref[...].astype(f32), kern_ref, off_ref, mask_ref, xp_ref, proj_s
    )

    @pl.when(block == pl.num_programs(0) - 1)
    def _():
        maps_part(rows, *sizes, proj_s[...], rank2_ref, rank_t_ref, bb_ref, cc_ref, cd_ref)


def step_sizes(rank2_ref, dtw_ref, bias_ref):
    weight = dtw_ref[...]
    pre = dot(rank2_ref[...], jnp.concatenate([weight, weight], axis=0)) + bias_ref[...]
    return jnp.maximum(pre, 0.0) + jnp.log1p(jnp.exp(-jnp.abs(pre)))


def chunked(v):
    return v.reshape(v.shape[0] // STEPS, STEPS, v.shape[1])


def tile_rows(ref, k, at, ns, inner, cb):
    v = ref[pl.ds(pl.multiple_of(k * inner, inner) + at, ns), :]
    return jnp.concatenate([v] * (cb // v.shape[1]), axis=1)


def lane_sum(v):
    out = v[:, :128]
    for i in range(1, v.shape[1] // 128):
        out = out + v[:, 128 * i : 128 * (i + 1)]
    return out


def ends_part(rows, act, rank2_ref, dtw_ref, bias_ref, kill_ref, rate_ref, bb_ref, eff_s, u_s):
    delta = step_sizes(rank2_ref, dtw_ref, bias_ref)
    cb = delta.shape[1]
    eff = delta + wide(kill_ref[...], cb)
    eff_s[...] = chunked(eff)
    u_s[...] = chunked(delta * act)
    length = eff.shape[0] // rows
    sums = jnp.concatenate(
        [jnp.sum(eff[s * length : (s + 1) * length], axis=0, keepdims=True) for s in range(rows)], axis=0
    )
    rate = rate_ref[...] * LOG2E
    ns = rate.shape[0]
    chunks = length // STEPS
    inner = rows * STEPS * ns

    def chunk(k, state):
        state = list(state)
        for t in range(STEPS):
            for s in range(rows):
                fade = jnp.exp2(rate * eff_s[s * chunks + k, t : t + 1, :])
                drive = u_s[s * chunks + k, t : t + 1, :] * tile_rows(bb_ref, k, (s * STEPS + t) * ns, ns, inner, cb)
                state[s] = fade * state[s] + drive
        return tuple(state)

    zero = jnp.zeros((ns, cb), f32)
    state = lax.fori_loop(0, chunks, chunk, (zero,) * rows)
    return delta, sums, jnp.concatenate(state, axis=0)


def scan_part(rows, delta, act, z, kill_ref, rate_ref, skip_ref, bb_ref, cd_ref, start,
              y_ref, gated_ref, keep_ref, eff_s, u_s, sa, sb, y_s):
    cb = delta.shape[1]
    eff_s[...] = chunked(delta + wide(kill_ref[...], cb))
    u_s[...] = chunked(delta * act)
    rate = rate_ref[...] * LOG2E
    ns = rate.shape[0]
    length = delta.shape[0] // rows
    chunks = length // STEPS
    inner = rows * STEPS * ns

    def scan(k, state, held):
        state = list(state)
        for s in range(rows):
            keep_ref[k, s * ns : (s + 1) * ns, :] = state[s]
        for t in range(STEPS):
            for s in range(rows):
                at = (s * STEPS + t) * ns
                fade = jnp.exp2(rate * eff_s[s * chunks + k, t : t + 1, :])
                drive = u_s[s * chunks + k, t : t + 1, :] * tile_rows(bb_ref, k, at, ns, inner, cb)
                state[s] = fade * state[s] + drive
                held[at : at + ns, :] = state[s].astype(bf16)
        return tuple(state)

    def leave(k, held):
        left = jnp.concatenate([cd_ref[s * chunks + k] for s in range(rows)], axis=0).astype(bf16)
        y = dot(left, held[...])
        for s in range(rows):
            y_s[s * chunks + k] = y[s * STEPS : (s + 1) * STEPS]

    sb[...] = jnp.zeros_like(sb)

    def two(i, state):
        k = 2 * i
        leave(jnp.maximum(k - 1, 0), sb)
        state = scan(k, state, sa)
        leave(k, sa)
        return scan(k + 1, state, sb)

    lax.fori_loop(0, chunks // 2, two, tuple(start[s * ns : (s + 1) * ns] for s in range(rows)))
    leave(chunks - 1, sb)
    y = (y_s[...].reshape(delta.shape) + skip_ref[...] * act).astype(bf16)
    y_ref[...] = y
    gated_ref[...] = (y.astype(f32) * (z * sigmoid(z))).astype(bf16)


def forward_kernel(rows, layer_of, sizes, *refs):
    n = len(layer_of)
    rank, ns, taps, narrow, blocks = sizes
    (h_ref, gain_ref, wx_ref, wz_ref, full_n, half_n, mask_ref, half_w, kill_ref, full_w, full_ref), refs = refs[:11], refs[11:]
    cut = Packed(rank, ns, taps)
    kern_ref, off_ref, xp_ref = cut.kernel(full_n), cut.offset(full_n), cut.xproj(half_n)
    dtw_ref, bias_ref, rate_ref = cut.dtproj(half_w), cut.bias(full_w), cut.rate(full_w)
    skip_ref, rates_ref = cut.skip(full_w), cut.rate(full_ref)
    srcs, refs = refs[:n], refs[n:]
    (normed_ref, x_ref, z_ref, halo_ref, act_ref, rank_t_ref, bb_ref, cc_ref, delta_ref, sum_ref, y_ref, gated_ref,
     keep_ref), refs = refs[:13], refs[13:]
    dsts, refs = refs[:n], refs[n:]
    (proj_s, x_s, tail_s, halo_s, act_s, z_s, rank2_s, cd_s, eff_s, u_s, sa, sb, y_s, delta_s, end_s, start_s,
     sum_s), refs = refs[:17], refs[17:]
    exch, (send, recv, hsend, hrecv) = refs[:10], refs[10:]
    here = Place()
    block = pl.program_id(0)
    front = 2 * narrow
    nb, cb = x_s.shape[2], eff_s.shape[2]
    per = cb // nb

    def halo(j):
        return push(tail_s.at[j], halo_s.at[j], hsend, hrecv, j, here.ring(1))

    @pl.when(block == 0)
    def _():
        greet(here.partners() + [here.ring(1), here.ring(-1)])
        proj_s[...] = jnp.zeros_like(proj_s)
        h = h_ref[...]
        normed_ref[...] = (
            h * lax.rsqrt(jnp.mean(h * h, axis=1, keepdims=True) + norm_eps) * gain_ref[...]
        ).astype(bf16)

    jobs = [
        Gather(here, src.at[layer], dst, send, recv, GATHER_SEMS * i)
        for i, (src, dst, layer) in enumerate(zip(srcs, dsts, layer_of))
    ]
    plans = [FORWARD_ONE if src.shape[1] * 32 < h_ref.shape[1] * 4 else FORWARD_EARLY for src in srcs]
    for job, plan in zip(jobs, plans):
        beside(job, block, plan)

    @pl.when(block < narrow)
    def _():
        normed = normed_ref[...]
        x = dot_nt(normed, wx_ref[...])
        z = dot_nt(normed, wz_ref[...])
        z_ref[...] = z
        z_s[block // per, :, pl.ds(pl.multiple_of(lax.rem(block, per) * nb, nb), nb)] = z
        x16 = x.astype(bf16)
        x_ref[...] = x16
        x_s[block] = x16
        length = x.shape[0] // rows
        tail_s[block] = jnp.concatenate([x[(s + 1) * length - 8 : (s + 1) * length] for s in range(rows)], axis=0).astype(bf16)
        halo(block).start()

    @pl.when((block >= narrow) & (block < front))
    def _():
        j = block - narrow
        halo(j).wait()
        before = halo_s[j]
        halo_ref[...] = before
        act = conv_part(
            rows, x_s[j].astype(f32), before.astype(f32), kern_ref, off_ref, mask_ref, xp_ref, proj_s
        )
        act_ref[...] = act
        act_s[j // per, :, pl.ds(pl.multiple_of(lax.rem(j, per) * nb, nb), nb)] = act

    @pl.when(block == front - 1)
    def _():
        maps_part(rows, rank, ns, proj_s[...], rank2_s, rank_t_ref, bb_ref, cc_ref, cd_s)

    @pl.when((block >= front) & (block < front + blocks))
    def _():
        j = block - front
        delta, sums, ends = ends_part(
            rows, act_s[j], rank2_s, dtw_ref, bias_ref, kill_ref, rate_ref, bb_ref, eff_s, u_s
        )
        cols = pl.ds(pl.multiple_of(j * cb, cb), cb)
        delta_ref[...] = delta
        delta_s[j] = delta
        sum_s[:, cols] = sums
        end_s[:, cols] = ends

    @pl.when(block == front + blocks - 1)
    def _():
        sum_ref[...] = sum_s[...]
        exchange(here, False, rows, end_s, sum_s, rates_ref, start_s, exch)

    @pl.when(block >= front + blocks)
    def _():
        j = block - front - blocks
        cols = pl.ds(pl.multiple_of(j * cb, cb), cb)
        scan_part(rows, delta_s[j], act_s[j], z_s[j], kill_ref, rate_ref, skip_ref, bb_ref, cd_s,
                  start_s[:, cols], y_ref, gated_ref, keep_ref, eff_s, u_s, sa, sb, y_s)

    @pl.when(block == pl.num_programs(0) - 1)
    def _():
        for job, plan in reversed(list(zip(jobs, plans))):
            for phase in job.phases[len(plan) :]:
                phase()


def back_ends_part(rows, gg_ref, z_ref, y_ref, delta_ref, kill_ref, rate_ref, cc_ref, gz_ref, eff_s, gy_s):
    z = z_ref[...]
    gg = gg_ref[...]
    sig = sigmoid(z)
    gy = (gg * z * sig).astype(bf16)
    gz_ref[...] = (gg * y_ref[...].astype(f32) * sig * (1.0 + z * (1.0 - sig))).astype(bf16)
    cb = z.shape[1]
    eff_s[...] = chunked(delta_ref[...] + wide(kill_ref[...], cb))
    gy_s[...] = chunked(gy.astype(f32))
    rate = rate_ref[...] * LOG2E
    ns = rate.shape[0]
    length = z.shape[0] // rows
    chunks = length // STEPS
    inner = rows * STEPS * ns

    def chunk(i, flow):
        k = chunks - 1 - i
        flow = list(flow)
        for t in reversed(range(STEPS)):
            for s in range(rows):
                fade = jnp.exp2(rate * eff_s[s * chunks + k, t : t + 1, :])
                push = gy_s[s * chunks + k, t : t + 1, :] * tile_rows(cc_ref, k, (s * STEPS + t) * ns, ns, inner, cb)
                flow[s] = fade * (flow[s] + push)
        return tuple(flow)

    zero = jnp.zeros((ns, cb), f32)
    flow = lax.fori_loop(0, chunks, chunk, (zero,) * rows)
    return gy, jnp.concatenate(flow, axis=0)


def back_part(rows, act_ref, delta_ref, gy, kill_ref, rate_ref, skip_ref, dtw_ref, rank_t_ref, bb_ref, cc_ref, keep_ref,
              start, gact_ref, gdtw_ref, gbias_ref, grate_ref, gskip_ref,
              eff_s, u_s, gy_s, fade_s, held_s, sa, sb, gu_s, gd_s, gb_s, gc_s, grank_s):
    delta = delta_ref[...]
    act = act_ref[...]
    cb = delta.shape[1]
    eff_s[...] = chunked(delta + wide(kill_ref[...], cb))
    u_s[...] = chunked(delta * act)
    gy_s[...] = chunked(gy)
    rate_n = rate_ref[...]
    rate = rate_n * LOG2E
    ns = rate.shape[0]
    length = delta.shape[0] // rows
    chunks = length // STEPS
    pairs = rows * STEPS
    inner = pairs * ns
    half = ns // 2
    side = pairs * half
    pick = (
        lax.broadcasted_iota(jnp.int32, (2 * pairs, 2 * side), 0)
        == lax.broadcasted_iota(jnp.int32, (2 * pairs, 2 * side), 1) // half
    ).astype(bf16)

    def scan(k, carry, sums):
        flow, total = list(carry[0]), carry[1]
        state = [keep_ref[k, s * ns : (s + 1) * ns, :] for s in range(rows)]
        base = pl.multiple_of(k * inner, inner)
        for t in range(STEPS):
            for s in range(rows):
                at = (s * STEPS + t) * ns
                fade = jnp.exp2(rate * eff_s[s * chunks + k, t : t + 1, :])
                held = fade * state[s]
                fade_s[at : at + ns, :] = fade
                held_s[at : at + ns, :] = held
                drive = u_s[s * chunks + k, t : t + 1, :] * tile_rows(bb_ref, k, at, ns, inner, cb)
                state[s] = held + drive
                gc_s[pl.ds(base + at, ns), :] += lane_sum(state[s] * gy_s[s * chunks + k, t : t + 1, :])
        for t in reversed(range(STEPS)):
            for s in range(rows):
                at = (s * STEPS + t) * ns
                push = gy_s[s * chunks + k, t : t + 1, :] * tile_rows(cc_ref, k, at, ns, inner, cb)
                grad = flow[s] + push
                gb_s[pl.ds(base + at, ns), :] += lane_sum(grad * u_s[s * chunks + k, t : t + 1, :])
                w = grad * held_s[at : at + ns, :]
                total = total + w * eff_s[s * chunks + k, t : t + 1, :]
                gu = grad * tile_rows(bb_ref, k, at, ns, inner, cb)
                wa = w * rate_n
                low = (s * STEPS + t) * half
                sums[low : low + half, :] = gu[:half] + gu[half:]
                sums[side + low : side + low + half, :] = wa[:half] + wa[half:]
                flow[s] = fade_s[at : at + ns, :] * grad
        return tuple(flow), total

    def leave(k, sums):
        out = dot(pick, sums[...].astype(bf16))
        for s in range(rows):
            gu_s[s * chunks + k] = out[s * STEPS : (s + 1) * STEPS]
            gd_s[s * chunks + k] = out[pairs + s * STEPS : pairs + (s + 1) * STEPS]

    sb[...] = jnp.zeros_like(sb)

    def two(i, carry):
        k = chunks - 1 - 2 * i
        leave(jnp.minimum(k + 1, chunks - 1), sb)
        carry = scan(k, carry, sa)
        leave(k, sa)
        return scan(k - 1, carry, sb)

    first = tuple(start[s * ns : (s + 1) * ns] for s in range(rows))
    _, total = lax.fori_loop(0, chunks // 2, two, (first, jnp.zeros((ns, cb), f32)))
    leave(0, sb)
    grate_ref[...] = total * rate_n
    gu = gu_s[...].reshape(delta.shape)
    gact_ref[...] = gu * delta + skip_ref[...] * gy
    gskip_ref[...] = jnp.sum(gy * act, axis=0, keepdims=True)
    gpre = (gu * act + gd_s[...].reshape(delta.shape)) * (1.0 - jnp.exp(-delta))
    gbias_ref[...] = jnp.sum(gpre, axis=0, keepdims=True)
    gpre16 = gpre.astype(bf16)
    gdtw_ref[...] = dot(rank_t_ref[...], gpre16)
    grank_s[...] += dot_nt(gpre16, dtw_ref[...])


def fold_part(rows, ns, gproj_ref, gproj_t_ref, gb_s, gc_s, grank_s):
    pairs = rows * STEPS
    inner = pairs * ns
    chunks = gb_s.shape[0] // inner
    ones = jnp.ones((128, 128), bf16)
    lane = lax.broadcasted_iota(jnp.int32, (pairs, ns, 128), 2)
    spot = lax.broadcasted_iota(jnp.int32, (pairs, ns, 128), 1)
    rank = grank_s.shape[1]

    def fold(ref, k):
        high, low = halves(ref[k * inner : (k + 1) * inner, :])
        v = (dot(high, ones) + dot(low, ones)).reshape(pairs, ns, 128)
        return jnp.sum(jnp.where(lane == spot, v, 0.0), axis=1)[:, :ns]

    for k in range(chunks):
        gb, gc = fold(gb_s, k), fold(gc_s, k)
        for s in range(rows):
            here = slice((s * chunks + k) * STEPS, (s * chunks + k + 1) * STEPS)
            mine = slice(s * STEPS, (s + 1) * STEPS)
            gproj_ref[here, :] = jnp.concatenate([grank_s[here, :], gb[mine], gc[mine]], axis=1)
    gproj_t_ref[...] = gproj_ref[...].T


def backward_kernel(rows, n, sizes, *refs):
    blocks, narrow, rank, ns, taps = sizes
    (gg_ref, z_ref, y_ref, wdelta_ref, full_w, kill_ref, full_ref, sum_ref, act_ref, delta_ref, full_n,
     half_n, rank_t_ref, bb_ref, cc_ref, keep_ref, x_ref, halo_ref, mask_ref) = refs[:19]
    refs = refs[19:]
    cut = Packed(rank, ns, taps)
    wrate_ref, rates_ref, rate_ref, skip_ref = cut.rate(full_w), cut.rate(full_ref), cut.rate(full_n), cut.skip(full_n)
    dtw_ref, xp_ref, kern_ref, off_ref = cut.dtproj(half_n), cut.xproj(half_n), cut.kernel(full_n), cut.offset(full_n)
    srcs, refs = refs[:n], refs[n:]
    (mixed_ref, packed_ref), refs = refs[:2], refs[2:]
    sums, refs = refs[:n], refs[n:]
    (weff_s, wgy_s, gyall_s, end_s, start_s, gz_s, gact_s, gproj_s, gproj_t_s, gend_s, edge_s, late_s, gdtw_s, gbias_s, grate_s,
     gskip_s, gxp_s, gkern_s, goff_s), refs = refs[:19], refs[19:]
    (eff_s, u_s, gy_s, fade_s, held_s, sa, sb, gu_s, gd_s, gb_s, gc_s, grank_s), refs = refs[:12], refs[12:]
    exch, (esend, erecv), refs = refs[:10], refs[10:12], refs[12:]
    here = Place()
    block = pl.program_id(0)
    wide_cb, cb = gg_ref.shape[1], act_ref.shape[1]
    c = wide_cb * blocks

    def edge(j):
        return push(edge_s.at[j], late_s.at[j], esend, erecv, j, here.ring(-1))

    @pl.when(block == 0)
    def _():
        greet(here.partners() + [here.ring(1), here.ring(-1)])
        gc_s[...] = jnp.zeros_like(gc_s)
        gb_s[...] = jnp.zeros_like(gb_s)
        grank_s[...] = jnp.zeros_like(grank_s)

    beside(Reduces(srcs, sums, refs), block, BACKWARD_STEPS)

    @pl.when(block < blocks)
    def _():
        gy, flow = back_ends_part(
            rows, gg_ref, z_ref, y_ref, wdelta_ref, kill_ref, wrate_ref, cc_ref, gz_s, weff_s, wgy_s
        )
        cols = pl.ds(pl.multiple_of(block * wide_cb, wide_cb), wide_cb)
        mixed_ref[:, pl.ds(pl.multiple_of(c + block * wide_cb, wide_cb), wide_cb)] = gz_s[...]
        gyall_s[:, cols] = gy.astype(f32)
        end_s[:, cols] = flow

    @pl.when(block == blocks - 1)
    def _():
        exchange(here, True, rows, end_s, sum_ref, rates_ref, start_s, exch)

    @pl.when((block >= blocks) & (block < blocks + narrow))
    def _():
        j = block - blocks
        cols = pl.ds(pl.multiple_of(j * cb, cb), cb)
        back_part(rows, act_ref, delta_ref, gyall_s[:, cols], kill_ref, rate_ref, skip_ref, dtw_ref, rank_t_ref,
                  bb_ref, cc_ref, keep_ref, start_s[:, cols], gact_s.at[j], gdtw_s.at[j], gbias_s.at[j], grate_s.at[j], gskip_s.at[j],
                  eff_s, u_s, gy_s, fade_s, held_s, sa, sb, gu_s, gd_s, gb_s, gc_s, grank_s)

    @pl.when(block == blocks + narrow - 1)
    def _():
        fold_part(rows, rate_ref.shape[0], gproj_s, gproj_t_s, gb_s, gc_s, grank_s)

    @pl.when(block >= blocks + narrow)
    def _():
        j = block - blocks - narrow
        cols = pl.ds(pl.multiple_of(j * cb, cb), cb)
        gx, edges = conv_back_part(
            rows, x_ref, halo_ref, kern_ref, off_ref, mask_ref, act_ref, gact_s[j], gproj_s, gproj_t_s, xp_ref,
            gxp_s, gkern_s, goff_s
        )
        rows_of = [gxp_s[...], gdtw_s[j], grate_s[j], gkern_s[...], goff_s[...], gbias_s[j], gskip_s[j]]
        count = sum(v.shape[0] for v in rows_of)
        rows_of.append(jnp.zeros((packed_ref.shape[0] - count, cb), f32))
        packed_ref[...] = jnp.concatenate(rows_of, axis=0).astype(bf16)
        edge_s[j] = edges.astype(bf16)
        edge(j).start()
        mixed_ref[:, cols] = gx.astype(bf16)
        length = gx.shape[0] // rows
        gend_s[j] = jnp.concatenate([gx[(s + 1) * length - 16 : (s + 1) * length] for s in range(rows)], axis=0)

    @pl.when(block == pl.num_programs(0) - 1)
    def _():
        more = jnp.where((here.z == 3) & (here.c == 1), 0.0, 1.0)
        length = mixed_ref.shape[0] // rows
        for j in range(narrow):
            edge(j).wait()
            late = late_s[j].astype(f32) * more
            for s in range(rows):
                end = gend_s[j, 16 * s : 16 * s + 16]
                fixed = jnp.concatenate([end[:8], end[8:] + late[8 * s : 8 * s + 8]], axis=0)
                mixed_ref[(s + 1) * length - 16 : (s + 1) * length, j * cb : (j + 1) * cb] = fixed.astype(bf16)
        Reduces(srcs, sums, refs).run(-1)


def ends_kernel(rows, act_ref, rank2_ref, dtw_ref, bias_ref, kill_ref, rate_ref, bb_ref,
                delta_ref, end_ref, sum_ref, eff_s, u_s):
    delta_ref[...], sum_ref[...], end_ref[...] = ends_part(
        rows, act_ref[...], rank2_ref, dtw_ref, bias_ref, kill_ref, rate_ref, bb_ref, eff_s, u_s
    )


def scan_kernel(rows, act_ref, delta_ref, z_ref, kill_ref, rate_ref, skip_ref, bb_ref, cd_ref, start_ref, *refs):
    scan_part(rows, delta_ref[...], act_ref[...], z_ref[...], kill_ref, rate_ref, skip_ref, bb_ref, cd_ref, start_ref[...], *refs)


def back_ends_kernel(rows, gg_ref, z_ref, y_ref, delta_ref, kill_ref, rate_ref, cc_ref,
                     gy_ref, gz_ref, end_ref, eff_s, gy_s):
    gy_ref[...], end_ref[...] = back_ends_part(
        rows, gg_ref, z_ref, y_ref, delta_ref, kill_ref, rate_ref, cc_ref, gz_ref, eff_s, gy_s
    )


def back_kernel(rows, act_ref, delta_ref, gy_ref, kill_ref, rate_ref, skip_ref, dtw_ref, rank_t_ref,
                bb_ref, cc_ref, keep_ref, start_ref,
                gact_ref, gproj_ref, gproj_t_ref, gdtw_ref, gbias_ref, grate_ref, gskip_ref, *scratch):
    gb_s, gc_s, grank_s = scratch[-3:]

    @pl.when(pl.program_id(0) == 0)
    def _():
        gc_s[...] = jnp.zeros_like(gc_s)
        gb_s[...] = jnp.zeros_like(gb_s)
        grank_s[...] = jnp.zeros_like(grank_s)

    back_part(rows, act_ref, delta_ref, gy_ref[...].astype(f32), kill_ref, rate_ref, skip_ref, dtw_ref, rank_t_ref,
              bb_ref, cc_ref, keep_ref, start_ref[...], gact_ref, gdtw_ref, gbias_ref, grate_ref, gskip_ref, *scratch)

    @pl.when(pl.program_id(0) == pl.num_programs(0) - 1)
    def _():
        fold_part(rows, rate_ref.shape[0], gproj_ref, gproj_t_ref, gb_s, gc_s, grank_s)


def conv_back_part(rows, x_ref, halo_ref, kern_ref, off_ref, mask_ref, act_ref, gact, gproj_ref,
                   gproj_t_ref, xp_ref, gxp_ref, gkern_ref, goff_ref):
    x = x_ref[...].astype(bf16).astype(f32)
    cb = x.shape[1]
    halo = halo_ref[...].astype(f32)
    kernel = kern_ref[...]
    taps = kernel.shape[0]
    masks = [wide(mask_ref[i], cb) for i in range(taps - 1)]
    pre = conv_sum(x, halo, kernel, off_ref[...], masks, rows)
    sig = sigmoid(pre)
    act16 = act_ref[...].astype(bf16)
    gxp_ref[...] = dot(gproj_t_ref[...].astype(bf16), act16)
    g_act = gact + dot(gproj_ref[...].astype(bf16), xp_ref[...])
    gpre = g_act * sig * (1.0 + pre * (1.0 - sig))
    goff_ref[...] = jnp.sum(gpre, axis=0, keepdims=True)
    length = x.shape[0] // rows
    place = lax.broadcasted_iota(jnp.int32, (length, cb), 0)
    gk = [jnp.zeros((1, cb), f32) for _ in range(taps)]
    gxs, edges = [], []
    for s in range(rows):
        here = slice(s * length, (s + 1) * length)
        g = gpre[here]
        ext = jnp.concatenate([halo[8 * s : 8 * s + 8], x[here]], axis=0)
        gk[taps - 1] = gk[taps - 1] + jnp.sum(g * x[here], axis=0, keepdims=True)
        gx = kernel[taps - 1 : taps] * g
        edge = jnp.zeros((length, cb), f32)
        for lag in range(1, taps):
            gm = g * masks[lag - 1][here]
            moved = pltpu.roll(ext, lag, 0)[8:]
            j = taps - 1 - lag
            gk[j] = gk[j] + jnp.sum(gm * moved, axis=0, keepdims=True)
            up = pltpu.roll(kernel[j : j + 1] * gm, length - lag, 0)
            inside = place < length - lag
            gx = gx + jnp.where(inside, up, 0.0)
            edge = edge + jnp.where(inside, 0.0, up)
        gxs.append(gx)
        edges.append(edge[length - 8 :])
    gkern_ref[...] = jnp.concatenate(gk, axis=0)
    return jnp.concatenate(gxs, axis=0), jnp.concatenate(edges, axis=0)


def conv_back_kernel(rows, x_ref, halo_ref, kern_ref, off_ref, mask_ref, act_ref, gact_ref, gproj_ref,
                     gproj_t_ref, xp_ref, gx_ref, edge_ref, *outs):
    gx_ref[...], edge_ref[...] = conv_back_part(
        rows, x_ref, halo_ref, kern_ref, off_ref, mask_ref, act_ref, gact_ref[...], gproj_ref, gproj_t_ref, xp_ref, *outs
    )


def col(rows, cb, shift=0):
    return pl.BlockSpec((rows, cb), lambda j: (0, j + shift))


def whole(*shape):
    return pl.BlockSpec(shape, lambda j: (0,) * len(shape))


def call(body, blocks, ins, outs, scratch, args, ident=None):
    more = {} if ident is None else dict(collective_id=ident, has_side_effects=True)
    return pl.pallas_call(
        body,
        grid=(blocks,),
        in_specs=ins,
        out_specs=[spec for spec, _, _ in outs],
        out_shape=[jax.ShapeDtypeStruct(shape, kind) for _, shape, kind in outs],
        scratch_shapes=scratch,
        compiler_params=pltpu.CompilerParams(
            dimension_semantics=("arbitrary",), vmem_limit_bytes=VMEM, **more
        ),
    )(*args)


class Mixer:
    def __init__(self, layers, rows, length, channels, ns, rank, taps):
        self.layers = layers
        self.rows, self.length, self.c, self.ns, self.rank, self.taps = rows, length, channels, ns, rank, taps
        self.tokens = rows * length
        self.chunks = length // STEPS
        self.pairs = rows * STEPS
        self.inner = self.pairs * ns
        self.width = rank + 2 * ns

    def conv(self, projected, halo, p, masks):
        t, c, cb = self.tokens, self.c, CB
        tall = (t * self.ns, 128)
        out = call(
            functools.partial(conv_kernel, self.rows, (self.rank, self.ns)), c // cb,
            [col(t, cb), col(8 * self.rows, cb), col(self.taps, cb), col(1, cb), whole(*masks.shape), col(self.width, cb)],
            [(col(t, cb), (t, c), f32), (whole(t, 2 * self.rank), (t, 2 * self.rank), bf16),
             (whole(self.rank, t), (self.rank, t), bf16), (whole(*tall), tall, f32), (whole(*tall), tall, f32),
             (whole(t, self.inner), (t, self.inner), f32)],
            [pltpu.VMEM((t, self.width), f32)], (projected, halo, p["conv_w"], p["conv_b"], masks, p["xproj"]),
        )
        m = dict(zip(("rank2", "rank_t", "bb", "cc", "cd"), out[1:]))
        m["cd"] = m["cd"].reshape(-1, STEPS, self.inner)
        return out[0], m

    def scratch3(self, cb):
        return pltpu.VMEM((self.tokens // STEPS, STEPS, cb), f32)

    def wide_scratch(self, kind, cb):
        return pltpu.VMEM((self.inner, cb), kind)

    def forward(self, i, h, gain, in_full, half, full, masks, kill, gathers, ident):
        t, c, sn, cb, nb, ns, d = self.tokens, self.c, self.rows * self.ns, CB_SCAN, CB, self.ns, h.shape[1]
        narrow, blocks = c // nb, c // cb
        front = 2 * narrow
        hn, fn = half.shape[0] // self.layers, full.shape[0] // self.layers

        def first(rows):
            return pl.BlockSpec((rows, nb), lambda j: (0, jnp.minimum(j, narrow - 1)))

        def second(rows):
            return pl.BlockSpec((rows, nb), lambda j: (0, jnp.clip(j - narrow, 0, narrow - 1)))

        def early(rows):
            return pl.BlockSpec((rows, cb), lambda j: (0, jnp.clip(j - front, 0, blocks - 1)))

        def both(rows):
            return pl.BlockSpec((rows, cb), lambda j: (0, lax.rem(jnp.maximum(j - front, 0), blocks)))

        def late(rows):
            return pl.BlockSpec((rows, cb), lambda j: (0, jnp.maximum(j - front - blocks, 0)))

        def at(spec):
            return pl.BlockSpec(spec.block_shape, lambda j: (i, spec.index_map(j)[1]))

        wx = pl.BlockSpec((nb, d), lambda j: (jnp.minimum(j, narrow - 1), 0))
        wz = pl.BlockSpec((nb, d), lambda j: (jnp.minimum(j, narrow - 1) + narrow, 0))
        n = len(gathers)
        keep = pl.BlockSpec((self.chunks, sn, cb), lambda j: (0, 0, jnp.maximum(j - front - blocks, 0)))
        sems = [pltpu.SemaphoreType.DMA((GATHER_SEMS * max(n, 1),))] * 2 + [pltpu.SemaphoreType.DMA((narrow,))] * 2
        tall = (t * ns, 128)
        hr = 8 * self.rows
        out = call(
            functools.partial(forward_kernel, self.rows, [k for _, k in gathers], (self.rank, ns, self.taps, narrow, blocks)), front + 2 * blocks,
            [whole(t, d), whole(1, d), wx, wz, at(second(fn)), at(second(hn)), whole(*masks.shape), at(early(hn)),
             whole(*kill.shape), at(both(fn)), pl.BlockSpec((fn, c), lambda j: (i, 0))] + [ANY] * n,
            [(whole(t, d), (t, d), bf16), (first(t), (t, c), bf16), (first(t), (t, c), f32), (second(hr), (hr, c), bf16),
             (second(t), (t, c), f32), (whole(self.rank, t), (self.rank, t), bf16), (whole(*tall), tall, f32),
             (whole(*tall), tall, f32), (early(t), (t, c), f32), (whole(self.rows, c), (self.rows, c), f32),
             (late(t), (t, c), bf16), (late(t), (t, c), bf16), (keep, (self.chunks, sn, c), f32)]
            + [(ANY, (2, 2, 4, 2) + g.shape[1:], g.dtype) for g, _ in gathers],
            [pltpu.VMEM((t, self.width), f32), pltpu.VMEM((narrow, t, nb), bf16), pltpu.VMEM((narrow, hr, nb), bf16),
             pltpu.VMEM((narrow, hr, nb), bf16), pltpu.VMEM((blocks, t, cb), f32), pltpu.VMEM((blocks, t, cb), f32),
             pltpu.VMEM((t, 2 * self.rank), bf16), pltpu.VMEM((t // STEPS, STEPS, self.inner), f32),
             self.scratch3(cb), self.scratch3(cb), self.wide_scratch(bf16, cb), self.wide_scratch(bf16, cb),
             self.scratch3(cb), pltpu.VMEM((blocks, t, cb), f32), pltpu.VMEM((sn, c), f32), pltpu.VMEM((sn, c), f32),
             pltpu.VMEM((self.rows, c), f32)] + exchange_scratch(self.rows, sn, c) + sems,
            (h, gain, in_full, in_full, full, half, masks, half, kill, full, full, *[g for g, _ in gathers]),
            ident,
        )
        return out[:13], [g.reshape(-1, g.shape[-1]) for g in out[13:]]

    def backward(self, i, gg, x, z, halo, y, act, delta, total, m, half, full, masks, kill, keep, sums, ident):
        t, c, sn, ns, cb, wcb = self.tokens, self.c, self.rows * self.ns, self.ns, CB_BACK, CB_ENDS
        blocks, narrow = c // wcb, c // cb

        def early(rows):
            return pl.BlockSpec((rows, wcb), lambda j: (0, jnp.minimum(j, blocks - 1)))

        def late(rows):
            return pl.BlockSpec((rows, cb), lambda j: (0, jnp.clip(j - blocks, 0, narrow - 1)))

        def last(rows):
            return pl.BlockSpec((rows, cb), lambda j: (0, jnp.maximum(j - blocks - narrow, 0)))

        def twice(rows):
            return pl.BlockSpec((rows, cb), lambda j: (0, lax.rem(jnp.maximum(j - blocks, 0), narrow)))

        def at(spec):
            return pl.BlockSpec(spec.block_shape, lambda j: (i, spec.index_map(j)[1]))

        hn, fn = half.shape[0] // self.layers, full.shape[0] // self.layers
        kept = pl.BlockSpec((self.chunks, sn, cb), lambda j: (0, 0, jnp.clip(j - blocks, 0, narrow - 1)))
        tall = m["bb"].shape
        hr = 8 * self.rows
        pack = self.width + self.rank + ns + self.taps + 3
        pack += -pack % 64
        more_in, more_out, more_scratch = reduce_parts(sums)
        sems = [pltpu.SemaphoreType.DMA((narrow,))] * 2
        out = call(
            functools.partial(backward_kernel, self.rows, len(sums), (blocks, narrow, self.rank, ns, self.taps)), blocks + 2 * narrow,
            [early(t), early(t), early(t), early(t), at(early(fn)), whole(*kill.shape), pl.BlockSpec((fn, c), lambda j: (i, 0)),
             whole(self.rows, c), twice(t), late(t), at(twice(fn)), at(twice(hn)), whole(*m["rank_t"].shape), whole(*tall),
             whole(*tall), kept, last(t), last(hr), whole(*masks.shape)] + [ANY] * len(sums),
            [(whole(t, 2 * c), (t, 2 * c), bf16), (last(pack), (pack, c), bf16)]
            + [(whole(*v.shape), v.shape, f32) for v in more_out],
            [self.scratch3(wcb)] * 2 + [pltpu.VMEM((t, c), f32), pltpu.VMEM((sn, c), f32), pltpu.VMEM((sn, c), f32)]
            + [pltpu.VMEM((t, wcb), bf16), pltpu.VMEM((narrow, t, cb), f32), pltpu.VMEM((t, self.width), f32),
               pltpu.VMEM((self.width, t), f32), pltpu.VMEM((narrow, 2 * hr, cb), f32), pltpu.VMEM((narrow, hr, cb), bf16),
               pltpu.VMEM((narrow, hr, cb), bf16)]
            + [pltpu.VMEM((narrow, k, cb), f32) for k in (self.rank, 1, ns, 1)]
            + [pltpu.VMEM((k, cb), f32) for k in (self.width, self.taps, 1)]
            + [self.scratch3(cb)] * 3 + [self.wide_scratch(f32, cb)] * 4 + [self.scratch3(cb)] * 2
            + [pltpu.VMEM(tall, f32)] * 2 + [pltpu.VMEM((t, self.rank), f32)] + exchange_scratch(self.rows, sn, c)
            + sems + more_scratch,
            (gg, z, y, delta, full, kill, full, total, act, delta, full, half, m["rank_t"], m["bb"], m["cc"], keep, x, halo,
             masks, *more_in),
            ident,
        )
        return out[:2], out[2:]

    def ends(self, act, m, p, kill):
        t, c, sn, cb = self.tokens, self.c, self.rows * self.ns, CB_ENDS
        return call(
            functools.partial(ends_kernel, self.rows), c // cb,
            [col(t, cb), whole(*m["rank2"].shape), col(self.rank, cb), col(1, cb), whole(*kill.shape), col(self.ns, cb),
             whole(*m["bb"].shape)],
            [(col(t, cb), (t, c), f32), (col(sn, cb), (sn, c), f32), (col(self.rows, cb), (self.rows, c), f32)],
            [self.scratch3(cb), self.scratch3(cb)],
            (act, m["rank2"], p["dtproj"], p["dt_b"], kill, p["rate"], m["bb"]),
        )

    def scan(self, act, delta, projected, m, p, kill, start):
        t, c, sn, cb = self.tokens, self.c, self.rows * self.ns, CB_SCAN
        keep = pl.BlockSpec((self.chunks, sn, cb), lambda j: (0, 0, j))
        return call(
            functools.partial(scan_kernel, self.rows), c // cb,
            [col(t, cb), col(t, cb), col(t, cb, c // cb), whole(*kill.shape), col(self.ns, cb), col(1, cb),
             whole(*m["bb"].shape), whole(*m["cd"].shape), col(sn, cb)],
            [(col(t, cb), (t, c), bf16), (col(t, cb), (t, c), bf16), (keep, (self.chunks, sn, c), f32)],
            [self.scratch3(cb), self.scratch3(cb), self.wide_scratch(bf16, cb), self.wide_scratch(bf16, cb),
             self.scratch3(cb)],
            (act, delta, projected, kill, p["rate"], p["skip"], m["bb"], m["cd"], start),
        )

    def back_ends(self, gg, projected, y, delta, m, p, kill):
        t, c, sn, cb = self.tokens, self.c, self.rows * self.ns, CB_ENDS
        return call(
            functools.partial(back_ends_kernel, self.rows), c // cb,
            [col(t, cb), col(t, cb, c // cb), col(t, cb), col(t, cb), whole(*kill.shape), col(self.ns, cb),
             whole(*m["cc"].shape)],
            [(col(t, cb), (t, c), bf16), (col(t, cb), (t, c), bf16), (col(sn, cb), (sn, c), f32)],
            [self.scratch3(cb), self.scratch3(cb)],
            (gg, projected, y, delta, kill, p["rate"], m["cc"]),
        )

    def back(self, act, delta, gy, m, p, kill, keep, start):
        t, c, sn, ns, cb = self.tokens, self.c, self.rows * self.ns, self.ns, CB_BACK
        kept = pl.BlockSpec((self.chunks, sn, cb), lambda j: (0, 0, j))
        tall = m["bb"].shape
        return call(
            functools.partial(back_kernel, self.rows), c // cb,
            [col(t, cb), col(t, cb), col(t, cb), whole(*kill.shape), col(ns, cb), col(1, cb), col(self.rank, cb),
             whole(*m["rank_t"].shape), whole(*tall), whole(*tall), kept, col(sn, cb)],
            [(col(t, cb), (t, c), f32), (whole(t, self.width), (t, self.width), f32),
             (whole(self.width, t), (self.width, t), f32), (col(self.rank, cb), (self.rank, c), f32),
             (col(1, cb), (1, c), f32), (col(ns, cb), (ns, c), f32), (col(1, cb), (1, c), f32)],
            [self.scratch3(cb)] * 3 + [self.wide_scratch(f32, cb)] * 4 + [self.scratch3(cb)] * 2
            + [pltpu.VMEM(tall, f32)] * 2 + [pltpu.VMEM((t, self.rank), f32)],
            (act, delta, gy, kill, p["rate"], p["skip"], p["dtproj"], m["rank_t"], m["bb"], m["cc"], keep, start),
        )

    def conv_back(self, projected, halo, p, masks, act, gact, gproj, gproj_t):
        t, c, cb = self.tokens, self.c, CB
        return call(
            functools.partial(conv_back_kernel, self.rows), c // cb,
            [col(t, cb), col(8 * self.rows, cb), col(self.taps, cb), col(1, cb), whole(*masks.shape), col(t, cb),
             col(t, cb), whole(t, self.width), whole(self.width, t), col(self.width, cb)],
            [(col(t, cb), (t, c), f32), (col(8 * self.rows, cb), (8 * self.rows, c), f32),
             (col(self.width, cb), (self.width, c), f32), (col(self.taps, cb), (self.taps, c), f32),
             (col(1, cb), (1, c), f32)],
            [], (projected, halo, p["conv_w"], p["conv_b"], masks, act, gact, gproj, gproj_t, p["xproj"]),
        )


MESH = pl.DeviceIdType.MESH
ANY = pl.BlockSpec(memory_space=pl.ANY)
INV = pl.BlockSpec(memory_space=pltpu.VMEM)


class Place:
    def __init__(self):
        r, b = lax.axis_index("rows"), lax.axis_index("bytes")
        self.y, self.x, self.z, self.c = r // 2, lax.rem(r, 2), b // 2, lax.rem(b, 2)

    def at(self, y=None, x=None, z=None, c=None):
        y = self.y if y is None else y
        x = self.x if x is None else x
        z = self.z if z is None else z
        c = self.c if c is None else c
        return (y * 2 + x, z * 2 + c)

    def over(self, k):
        return lax.rem(self.z + k, 4)

    def ring(self, step):
        b = lax.rem(self.z * 2 + self.c + 8 + step, 8)
        return self.at(z=b // 2, c=lax.rem(b, 2))

    def partners(self):
        return [self.at(c=1 - self.c), self.at(x=1 - self.x), self.at(y=1 - self.y)] + [
            self.at(z=self.over(k)) for k in (1, 2, 3)
        ]


def greet(partners):
    barrier = pltpu.get_barrier_semaphore()
    for p in partners:
        pl.semaphore_signal(barrier, inc=1, device_id=p, device_id_type=MESH)
    pl.semaphore_wait(barrier, len(partners))


def push(src, dst, send, recv, i, device):
    return pltpu.make_async_remote_copy(
        src_ref=src, dst_ref=dst, send_sem=send.at[i], recv_sem=recv.at[i], device_id=device, device_id_type=MESH
    )


GATHER_SEMS = 36
TURN = (1, 3, 2)


class Gather:
    def __init__(self, here, src, dst, send, recv, base):
        self.here, self.src, self.dst, self.send, self.recv, self.base = here, src, dst, send, recv, base
        self.h = src.shape[0] // 2
        part = functools.partial
        self.phases = [self.begin, part(self.side, 0), part(self.come, 1), part(self.come, 3), part(self.side, 1),
                       part(self.come, 2), part(self.side, 3), part(self.side, 2), self.cross, self.last]

    def source(self, k):
        return lax.rem(self.here.z + 4 - k, 4)

    def own(self):
        h = self.here
        return pltpu.make_async_copy(self.src, self.dst.at[h.y, h.x, h.z, h.c], self.send.at[self.base + 35])

    def push(self, src, dst, i, device):
        return push(src, dst, self.send, self.recv, self.base + i, device)

    def line(self, k):
        h = self.here
        return self.push(self.src, self.dst.at[h.y, h.x, h.z, h.c], k - 1, h.at(z=h.over(k)))

    def sides(self, k):
        h = self.here
        dst = self.dst.at[h.y, h.x, self.source(k), h.c]
        src = self.src if k == 0 else dst
        return [
            self.push(src, dst, 3 + k, h.at(x=1 - h.x)),
            self.push(src, dst, 7 + k, h.at(y=1 - h.y)),
        ]

    def across(self, k):
        h, z = self.here, self.source(k)
        top, low = pl.ds(0, self.h), pl.ds(self.h, self.h)
        u, v = self.dst.at[1 - h.y, h.x, z, h.c, top], self.dst.at[h.y, 1 - h.x, z, h.c, low]
        return [
            self.push(u, u, 11 + k, h.at(x=1 - h.x)),
            self.push(v, v, 15 + k, h.at(y=1 - h.y)),
        ]

    def core(self, k, part):
        h, z = self.here, self.source(k)
        y, x = ((h.y, h.x), (h.y, 1 - h.x), (1 - h.y, h.x), (1 - h.y, 1 - h.x))[part]
        dst = self.dst.at[y, x, z, h.c]
        src = self.src if (k == 0 and part == 0) else dst
        return self.push(src, dst, 19 + 4 * k + part, h.at(c=1 - h.c))

    def begin(self):
        self.own().start()
        for k in TURN:
            self.line(k).start()
        for copy in self.sides(0):
            copy.start()
        self.core(0, 0).start()

    def come(self, k):
        self.line(k).wait_recv()
        for copy in self.sides(k):
            copy.start()
        self.core(k, 0).start()

    def side(self, k):
        for copy in self.sides(k):
            copy.wait_recv()
        for copy in self.across(k):
            copy.start()
        self.core(k, 1).start()
        self.core(k, 2).start()

    def cross(self):
        for k in (0,) + TURN:
            for copy in self.across(k):
                copy.wait_recv()
            self.core(k, 3).start()

    def last(self):
        self.own().wait()
        for k in TURN:
            self.line(k).wait_send()
        for k in range(4):
            for copy in self.sides(k) + self.across(k):
                copy.wait_send()
            for part in range(4):
                self.core(k, part).wait()


class GatherBytes:
    def __init__(self, here, src, dst, send, recv, base):
        self.here, self.src, self.dst, self.send, self.recv, self.base = here, src, dst, send, recv, base
        self.w = src.shape[1]
        self.q = src.shape[0] // 4
        self.phases = [self.begin, self.second, self.third, self.fourth, self.last]

    def spot(self, z, c, q=None, n=1):
        cols = pl.ds(pl.multiple_of((z * 2 + c) * self.w, self.w), self.w)
        if q is None:
            return self.dst.at[:, cols]
        return self.dst.at[pl.ds(pl.multiple_of(q * self.q, self.q), n * self.q), cols]

    def source(self, k):
        return lax.rem(self.here.z + 4 - k, 4)

    def push(self, src, dst, i, device):
        return push(src, dst, self.send, self.recv, self.base + i, device)

    def own(self):
        h = self.here
        return pltpu.make_async_copy(self.src, self.spot(h.z, h.c), self.send.at[self.base + 13])

    def line(self, k):
        h = self.here
        q = h.y * 2 + h.x
        src = self.src.at[pl.ds(pl.multiple_of(q * self.q, self.q), self.q)]
        return self.push(src, self.spot(h.z, h.c, q), k - 1, h.at(z=h.over(k)))

    def over_x(self, k):
        h = self.here
        u = self.spot(self.source(k), h.c, h.y * 2 + h.x)
        return self.push(u, u, 2 + k, h.at(x=1 - h.x))

    def over_y(self, k):
        h = self.here
        u = self.spot(self.source(k), h.c, h.y * 2, 2)
        return self.push(u, u, 5 + k, h.at(y=1 - h.y))

    def core(self, k):
        h = self.here
        u = self.spot(self.source(k), h.c)
        src = self.src if k == 0 else u
        return self.push(src, u, 9 + k, h.at(c=1 - h.c))

    def begin(self):
        self.own().start()
        for k in TURN:
            self.line(k).start()
        self.core(0).start()

    def second(self):
        for k in TURN:
            self.line(k).wait_recv()
            self.over_x(k).start()

    def third(self):
        for k in TURN:
            self.over_x(k).wait_recv()
            self.over_y(k).start()

    def fourth(self):
        for k in TURN:
            self.over_y(k).wait_recv()
            self.core(k).start()

    def last(self):
        self.own().wait()
        for k in TURN:
            self.line(k).wait_send()
            self.over_x(k).wait_send()
            self.over_y(k).wait_send()
        for k in range(4):
            self.core(k).wait()


def run_phases(jobs, plans):
    for step in range(max(plan[-1] for plan in plans) + 1):
        for job, plan in zip(jobs, plans):
            for phase, at in zip(job.phases, plan):
                if at == step:
                    phase()


GATHER_PLAN = (0, 2, 4, 6, 8, 10, 12, 14, 16, 18)
NEXT_PLAN = (0, 3, 7, 9, 11, 13, 15, 17, 19, 20)
SMALL_PLAN = (0, 3, 6, 9, 15)
REDUCE_PLAN = (0, 1, 2, 3, 4, 5, 6, 7, 8, 9, 10, 11)
SIDES_PLAN = (8, 10)
ALL_PLAN = (6, 8, 9, 10, 11)
SMALL_REDUCE = (0, 1, 2, 2, 2, 2, 2, 5, 5, 5, 5, 7)


def gather_kernel(xp_ref, dtw_ref, rate_ref, kern_ref, off_ref, bias_ref, skip_ref, in_ref, out_ref,
                  half_ref, full_ref, win_ref, wout_ref, half_s, full_s, send, recv):
    here = Place()
    greet(here.partners())
    layers = xp_ref.shape[0]
    hn, fn = half_s.shape[0] // layers, full_s.shape[0] // layers
    for i in range(layers):
        wt = xp_ref[i].astype(f32).T.astype(bf16)
        half_s[i * hn : i * hn + wt.shape[0], :] = wt
        half_s[i * hn + wt.shape[0] : (i + 1) * hn, :] = dtw_ref[i]
        parts = [-jnp.exp(rate_ref[i]), kern_ref[i], off_ref[i : i + 1], bias_ref[i : i + 1], skip_ref[i : i + 1]]
        rest = fn - sum(v.shape[0] for v in parts)
        full_s[i * fn : (i + 1) * fn, :] = jnp.concatenate(parts + [jnp.zeros((rest, full_s.shape[1]), f32)], axis=0)
    jobs = [
        GatherBytes(here, half_s, half_ref, send, recv, 0),
        GatherBytes(here, full_s, full_ref, send, recv, GATHER_SEMS),
        Gather(here, in_ref.at[0], win_ref, send, recv, 2 * GATHER_SEMS),
        Gather(here, out_ref.at[0], wout_ref, send, recv, 3 * GATHER_SEMS),
    ]
    run_phases(jobs, [SMALL_PLAN, SMALL_PLAN, GATHER_PLAN, NEXT_PLAN])


def gather_all(xp, dtw, decay, kern, off, bias, skip, in_weight, out_weight, ident):
    layers, w, width = xp.shape
    half = (layers * (width + dtw.shape[1]), w)
    rows = decay.shape[1] + kern.shape[1] + 3
    full = (layers * (rows + -rows % 32), w)
    sems = pltpu.SemaphoreType.DMA((GATHER_SEMS * 4,))
    outs = [jax.ShapeDtypeStruct((half[0], 8 * w), bf16), jax.ShapeDtypeStruct((full[0], 8 * w), f32)]
    outs += [jax.ShapeDtypeStruct((2, 2, 4, 2) + a.shape[1:], bf16) for a in (in_weight, out_weight)]
    half, full, win, wout = pl.pallas_call(
        gather_kernel,
        out_shape=outs,
        in_specs=[INV] * 7 + [ANY] * 2,
        out_specs=[ANY] * 4,
        scratch_shapes=[pltpu.VMEM(half, bf16), pltpu.VMEM(full, f32), sems, sems],
        compiler_params=pltpu.CompilerParams(collective_id=ident, has_side_effects=True, vmem_limit_bytes=VMEM),
    )(xp, dtw, decay, kern, off, bias, skip, in_weight, out_weight)
    return half, full, win.reshape(-1, win.shape[-1]), wout.reshape(-1, wout.shape[-1])


REDUCE_SEMS = 27
FAR = (2, 1, 3, 0)


def reduce_scratch(rows, d):
    def buf(*lead, r=rows):
        return pltpu.VMEM(lead + (r, d), bf16)

    return [buf(2, 2, 4), buf(2, 2, 4), buf(4, r=rows // 2), buf(4, r=rows // 2), buf(4), buf(4), buf(3)]


class Reduce:
    def __init__(self, here, src, out, bufs, send, recv, base):
        self.here, self.src, self.out, self.send, self.recv, self.base = here, src, out, send, recv, base
        self.acc, self.rc, self.da, self.db, self.rx, self.ry, self.rz = bufs
        self.h = src.shape[4] // 2
        h = here
        self.parts = [(1 - h.y, 1 - h.x), (1 - h.y, h.x), (h.y, 1 - h.x), (h.y, h.x)]
        self.phases = (
            [self.begin, self.cross, self.pairs]
            + [functools.partial(self.side, k) for k in FAR]
            + [functools.partial(self.mine, k) for k in FAR]
            + [self.last]
        )

    def push(self, src, dst, i, device):
        return push(src, dst, self.send, self.recv, self.base + i, device)

    def own(self, part):
        y, x = self.parts[part]
        return pltpu.make_async_copy(
            self.src.at[y, x, :, self.here.c], self.acc.at[y, x], self.send.at[self.base + 23 + part]
        )

    def cores(self, part):
        y, x = self.parts[part]
        return self.push(
            self.src.at[y, x, :, 1 - self.here.c], self.rc.at[y, x], 19 + part, self.here.at(c=1 - self.here.c)
        )

    def across(self, k):
        h, z = self.here, self.here.over(k)
        block = self.acc.at[1 - h.y, 1 - h.x, z]
        return [
            self.push(block.at[pl.ds(0, self.h)], self.da.at[z], 3 + k, h.at(x=1 - h.x)),
            self.push(block.at[pl.ds(self.h, self.h)], self.db.at[z], 7 + k, h.at(y=1 - h.y)),
        ]

    def sides(self, k):
        h, z = self.here, self.here.over(k)
        return [
            self.push(self.acc.at[h.y, 1 - h.x, z], self.rx.at[z], 11 + k, h.at(x=1 - h.x)),
            self.push(self.acc.at[1 - h.y, h.x, z], self.ry.at[z], 15 + k, h.at(y=1 - h.y)),
        ]

    def line(self, k):
        h = self.here
        return self.push(self.acc.at[h.y, h.x, h.over(k)], self.rz.at[k - 1], k - 1, h.at(z=h.over(k)))

    def pair(self, part):
        y, x = self.parts[part]
        self.own(part).wait()
        self.cores(part).wait_recv()

        @pl.loop(0, 4)
        def _(z):
            self.acc[y, x, z] = self.acc[y, x, z] + self.rc[y, x, z]

    def begin(self):
        for part in range(4):
            self.cores(part).start()
            self.own(part).start()

    def cross(self):
        self.pair(0)
        for k in FAR:
            for copy in self.across(k):
                copy.start()

    def pairs(self):
        for part in (1, 2, 3):
            self.pair(part)

    def side(self, k):
        h, a, n = self.here, self.acc, self.h
        z = h.over(k)
        for copy in self.across(k):
            copy.wait_recv()
        a[1 - h.y, h.x, z, :n] = a[1 - h.y, h.x, z, :n] + self.da[z]
        a[h.y, 1 - h.x, z, n:] = a[h.y, 1 - h.x, z, n:] + self.db[z]
        for copy in self.sides(k):
            copy.start()

    def mine(self, k):
        h, a = self.here, self.acc
        z = h.over(k)
        for copy in self.sides(k):
            copy.wait_recv()
        a[h.y, h.x, z] = a[h.y, h.x, z] + self.rx[z] + self.ry[z]
        if k:
            self.line(k).start()

    def last(self):
        h = self.here
        total = self.acc[h.y, h.x, h.z].astype(f32)
        for k in (1, 3, 2):
            self.line(k).wait()
            total = total + self.rz[k - 1].astype(f32)
        self.out[...] = total
        for k in range(4):
            for copy in self.across(k) + self.sides(k):
                copy.wait_send()
            self.cores(k).wait_send()


class Reduces:
    def __init__(self, srcs, outs, scratch):
        per = len(reduce_scratch(16, 128))
        self.here = Place()
        self.jobs = [
            Reduce(self.here, src, out, scratch[per * i : per * (i + 1)], scratch[-2], scratch[-1], REDUCE_SEMS * i)
            for i, (src, out) in enumerate(zip(srcs, outs))
        ]

        self.phases = [functools.partial(self.run, i) for i in range(12)]

    def run(self, phase):
        for job in self.jobs:
            job.phases[phase]()


def reduce_parts(arrays):
    arrays = [a.reshape(2, 2, 4, 2, a.shape[0] // 32, a.shape[1]) for a in arrays]
    scratch = []
    for a in arrays:
        scratch += reduce_scratch(*a.shape[4:])
    if arrays:
        sems = pltpu.SemaphoreType.DMA((REDUCE_SEMS * len(arrays),))
        scratch += [sems, sems]
    return arrays, [jax.ShapeDtypeStruct(a.shape[4:], f32) for a in arrays], scratch


def beside(work, block, steps):
    for step in sorted(set(steps)):

        @pl.when(block == step)
        def _(step=step):
            for phase, at in enumerate(steps):
                if at == step:
                    work.phases[phase]()


SIDE_SEMS = 4


class Sides:
    def __init__(self, here, src, dst, send, recv, base):
        self.here, self.src, self.dst, self.send, self.recv, self.base = here, src, dst, send, recv, base
        self.phases = [self.begin, self.last]

    def copies(self):
        h = self.here
        dst = self.dst.at[h.y, h.x]
        to = [h.at(x=1 - h.x), h.at(y=1 - h.y), h.at(x=1 - h.x, y=1 - h.y)]
        return [push(self.src, dst, self.send, self.recv, self.base + i, p) for i, p in enumerate(to)]

    def begin(self):
        for copy in self.copies():
            copy.start()
        self.dst[self.here.y, self.here.x] = self.src[...]

    def last(self):
        for copy in self.copies():
            copy.wait()


ALL_SEMS = 6


class AllSum:
    def __init__(self, here, src, out, got, send, recv, base):
        self.here, self.src, self.out, self.got, self.send, self.recv, self.base = here, src, out, got, send, recv, base
        self.phases = [self.begin, functools.partial(self.turn, 0), functools.partial(self.turn, 1), self.along, self.last]

    def copy(self, i):
        h = self.here
        p = h.partners()[i]
        return push(self.got.at[6 + min(i, 3)], self.got.at[i], self.send, self.recv, self.base + i, p)

    def begin(self):
        self.got[6] = self.src[...]
        self.copy(0).start()

    def turn(self, i):
        self.copy(i).wait()
        self.got[7 + i] = self.got[6 + i] + self.got[i]
        self.copy(i + 1).start()

    def along(self):
        self.copy(2).wait()
        self.got[9] = self.got[8] + self.got[2]
        for i in (3, 4, 5):
            self.copy(i).start()

    def last(self):
        for i in (3, 4, 5):
            self.copy(i).wait()
        self.out[...] = self.got[9] + self.got[3] + self.got[4] + self.got[5]


def finish_kernel(cuts, small_ref, big_ref, w_ref, mixed_ref, before_ref, flow_ref, gain_ref, upper_ref,
                  flow_out, in_out, gain_out, *refs):
    outs, refs = refs[: len(cuts)], refs[len(cuts) :]
    per = len(reduce_scratch(16, 128))
    one, two, refs = refs[:per], refs[per : 2 * per], refs[2 * per :]
    w_s, gn_s, mine_s, plane_s, gains_s, got_s, send, recv, wsem = refs
    here = Place()
    greet(here.partners() + [here.at(x=1 - here.x, y=1 - here.y)])
    load = pltpu.make_async_copy(w_ref, w_s, wsem)
    load.start()
    base = 2 * REDUCE_SEMS
    small = Reduce(here, small_ref, mine_s, one, send, recv, 0)
    big = Reduce(here, big_ref, in_out, two, send, recv, REDUCE_SEMS)
    gains = AllSum(here, gains_s, gain_out, got_s, send, recv, base)
    plane = Sides(here, mine_s, plane_s, send, recv, base + ALL_SEMS)

    class Norm:
        def run(self):
            load.wait()
            depth = 512
            gn_s[...] = jnp.zeros_like(gn_s)

            @pl.loop(0, mixed_ref.shape[1] // depth)
            def _(k):
                at = pl.ds(pl.multiple_of(k * depth, depth), depth)
                gn_s[...] += dot(mixed_ref[:, at], w_s[at, :])

            gn, before, gain = gn_s[...], before_ref[...], gain_ref[...]
            inv = lax.rsqrt(jnp.mean(before * before, axis=1, keepdims=True) + norm_eps)
            scaled = before * inv
            gs = gn * gain
            flow_out[...] = flow_ref[...] + inv * (gs - scaled * jnp.mean(gs * scaled, axis=1, keepdims=True))
            gains_s[0:1, :] = jnp.sum(gn * scaled, axis=0, keepdims=True)
            gains_s[1:, :] = upper_ref[...]

        def __init__(self):
            self.phases = [self.run]

    run_phases(
        [small, big, Norm(), gains, plane],
        [SMALL_REDUCE, REDUCE_PLAN, (6,), ALL_PLAN, SIDES_PLAN],
    )
    rows, d = mine_s.shape
    layers = upper_ref.shape[0] + 1
    whole_sum = plane_s[...].reshape(4 * rows, d)
    per_layer = 4 * rows // layers
    for layer in range(layers):
        at = layer * per_layer
        for i, (cut, out) in enumerate(zip(cuts, outs)):
            v = whole_sum[at : at + cut]
            if i == 0:
                out[layer] = v.T
            elif len(out.shape) == 2:
                out[layer : layer + 1, :] = v
            else:
                out[layer] = v
            at += cut


def finish(packed, grad_in, in_full, mixed, before, flowing, gain, upper, cuts, ident):
    arrays = [a.reshape(2, 2, 4, 2, a.shape[0] // 32, a.shape[1]) for a in (packed, grad_in)]
    (rows, w), d = arrays[0].shape[4:], before.shape[1]
    layers = upper.shape[0] + 1
    outs = [jax.ShapeDtypeStruct(before.shape, f32), jax.ShapeDtypeStruct(arrays[1].shape[4:], f32),
            jax.ShapeDtypeStruct((layers, d), f32), jax.ShapeDtypeStruct((layers, w, cuts[0]), f32)]
    outs += [jax.ShapeDtypeStruct((layers, cut, w) if cut > 1 else (layers, w), f32) for cut in cuts[1:]]
    scratch = reduce_scratch(rows, w) + reduce_scratch(*arrays[1].shape[4:])
    scratch += [pltpu.VMEM(in_full.shape, bf16), pltpu.VMEM(before.shape, f32), pltpu.VMEM((rows, w), f32),
                pltpu.VMEM((2, 2, rows, w), f32), pltpu.VMEM((layers, d), f32), pltpu.VMEM((10, layers, d), f32)]
    sems = pltpu.SemaphoreType.DMA((REDUCE_SEMS * 2 + ALL_SEMS + SIDE_SEMS,))
    return pl.pallas_call(
        functools.partial(finish_kernel, cuts),
        out_shape=outs,
        in_specs=[ANY] * 3 + [INV] * 5,
        out_specs=[INV] * len(outs),
        scratch_shapes=scratch + [sems, sems, pltpu.SemaphoreType.DMA],
        compiler_params=pltpu.CompilerParams(collective_id=ident, has_side_effects=True, vmem_limit_bytes=VMEM),
    )(*arrays, in_full, mixed, before, flowing, gain, upper)


EXCHANGE_SEMS = 10


def exchange_scratch(rows, sn, c):
    h = c // 2
    sems = pltpu.SemaphoreType.DMA((EXCHANGE_SEMS,))
    return [pltpu.VMEM((sn, h), bf16)] * 4 + [
        pltpu.VMEM((rows, h), f32), pltpu.VMEM((1, rows, h), f32), pltpu.VMEM((4, sn, h), bf16),
        pltpu.VMEM((4, rows, h), f32), sems, sems,
    ]


def exchange(here, backward, rows, end_ref, sum_ref, rate_ref, out_ref, scratch):
    sent, back, got, late, gsum, msum, line, lsum, send, recv = scratch
    half = end_ref.shape[1] // 2
    mine = pl.ds(pl.multiple_of(here.c * half, half), half)
    theirs = pl.ds(pl.multiple_of((1 - here.c) * half, half), half)
    other = here.at(c=1 - here.c)
    sent[...] = end_ref[:, theirs].astype(bf16)
    msum[0] = sum_ref[:, theirs]
    one = [push(sent, got, send, recv, 0, other), push(msum.at[0], gsum, send, recv, 1, other)]
    for copy in one:
        copy.start()
    rate = rate_ref[:, mine]

    def fade(total):
        return jnp.concatenate([jnp.exp(rate * total[s : s + 1]) for s in range(rows)], axis=0)

    for copy in one:
        copy.wait()
    e_me, d_me = end_ref[:, mine], sum_ref[:, mine]
    e_it, d_it = got[...].astype(f32), gsum[...]
    first = here.c == 0
    e0, e1 = jnp.where(first, e_me, e_it), jnp.where(first, e_it, e_me)
    d0, d1 = jnp.where(first, d_me, d_it), jnp.where(first, d_it, d_me)
    chip = e0 + fade(d0) * e1 if backward else fade(d1) * e0 + e1
    line[3] = chip.astype(bf16)
    lsum[3] = d0 + d1
    two = []
    for k in (1, 2, 3):
        two.append(push(line.at[3], line.at[k - 1], send, recv, 2 + 2 * k, here.at(z=here.over(k))))
        two.append(push(lsum.at[3], lsum.at[k - 1], send, recv, 3 + 2 * k, here.at(z=here.over(k))))
    for copy in two:
        copy.start()
    for copy in two:
        copy.wait()
    state = jnp.zeros_like(chip)
    for k in (1, 2, 3) if backward else (3, 2, 1):
        at = lax.rem(here.z + 4 - k, 4)
        e, d = line[k - 1].astype(f32), lsum[k - 1]
        use = at > here.z if backward else at < here.z
        state = jnp.where(use, fade(d) * state + e, state)
    if backward:
        s1, s0 = state, e1 + fade(d1) * state
    else:
        s0, s1 = state, fade(d0) * state + e0
    out_ref[:, mine] = jnp.where(first, s0, s1)
    back[...] = jnp.where(first, s1, s0).astype(bf16)
    three = push(back, late, send, recv, 2, other)
    three.start()
    three.wait()
    out_ref[:, theirs] = late[...].astype(f32)


def carried_in(ends, sums, rate, axis, backward):
    n = lax.axis_size(axis)
    rows = sums.shape[0]
    ns = rate.shape[0]

    def fade(total):
        return jnp.exp(total[:, None, :] * rate[None])

    def moved(v, shift):
        if backward:
            pairs = [(i, i - shift) for i in range(shift, n)]
        else:
            pairs = [(i, i + shift) for i in range(n - shift)]
        return lax.ppermute(v, axis, pairs)

    def shifted(e, s, shift):
        return moved(e.astype(bf16), shift).astype(f32), moved(s, shift)

    ends = ends.reshape(rows, ns, -1)
    ends, sums = shifted(ends, sums, 1)
    shift = 1
    while shift < n - 1:
        e, s = shifted(ends, sums, shift)
        ends = fade(sums) * e + ends
        sums = sums + s
        shift *= 2
    return ends.reshape(rows * ns, -1)


def body(
    tokens, boundaries, norm_gain, in_weight, out_weight, conv_weight, conv_bias, xproj_weight,
    dtproj_weight, dt_bias, decay_log, skip_gain, cotangent,
):
    rows, length, d = tokens.shape
    layers = norm_gain.shape[0]
    both = ("rows", "bytes")
    n = rows * length
    place = lax.axis_index("bytes") * length + jnp.arange(length, dtype=jnp.int32)
    reached = boundaries[:, None, :] <= place[None, :, None]
    starts = jnp.max(jnp.where(reached, boundaries[:, None, :], 0), axis=2)
    renewed = jnp.any(boundaries[:, None, :] == place[None, :, None], axis=2)
    kill = jnp.broadcast_to(jnp.where(renewed, KILL, 0.0).reshape(n, 1), (n, 128)).astype(f32)
    taps = conv_weight.shape[1]
    masks = jnp.stack(
        [
            jnp.broadcast_to((place[None, :] - lag >= starts).astype(f32).reshape(n, 1), (n, 128))
            for lag in range(1, taps)
        ]
    )
    fast = (lax.axis_size("rows"), lax.axis_size("bytes")) == (4, 8)
    if fast:
        half, full, first_in, first_out = gather_all(
            xproj_weight, dtproj_weight, decay_log, conv_weight, conv_bias, dt_bias, skip_gain, in_weight, out_weight, 1
        )
    else:
        half = jnp.concatenate([xproj_weight.transpose(0, 2, 1), dtproj_weight], axis=1)
        full = jnp.concatenate(
            [-jnp.exp(decay_log), conv_weight, conv_bias[:, None], dt_bias[:, None], skip_gain[:, None]], axis=1
        )
        half = lax.all_gather(half, "bytes", axis=2, tiled=True)
        full = lax.all_gather(full, "bytes", axis=2, tiled=True)
    ns = decay_log.shape[1]
    rank = dtproj_weight.shape[1]
    width = xproj_weight.shape[2]
    channels = full.shape[-1]
    mixer = Mixer(layers, rows, length, channels, ns, rank, taps)
    params = []
    for i in range(0 if fast else layers):
        rest = full[i, ns + taps :]
        params.append(
            dict(
                xproj=half[i, :width], dtproj=half[i, width:], conv_w=full[i, ns : ns + taps], conv_b=rest[:1],
                dt_b=rest[1:2], skip=rest[2:3], rate=full[i, :ns],
            )
        )
    if fast:
        in_fulls, out_fulls = {0: first_in}, {0: first_out}
    else:
        in_fulls = {i: lax.all_gather(in_weight[i], both, axis=0, tiled=True) for i in range(layers)}
        out_fulls = {i: lax.all_gather(out_weight[i], both, axis=0, tiled=True) for i in range(layers)}
    size = lax.axis_size("bytes")
    ahead = [(i, i + 1) for i in range(size - 1)]
    behind = [(i + 1, i) for i in range(size - 1)]
    current = tokens.astype(f32).reshape(n, d)
    saved = []
    for i in range(layers):
        p = None if fast else params[i]
        if fast:
            (normed, x, z, halo, act, rank_t, bb, cc, delta, total, y, gated, keep), whole_w = mixer.forward(
                i, current, norm_gain[i][None], in_fulls[i], half, full, masks, kill,
                ([(out_weight, i)] if i else []) + [(in_weight, j) for j in range(i + 1, min(i + 2, layers))], 2 + i,
            )
            m = dict(rank_t=rank_t, bb=bb, cc=cc)
            if i:
                out_fulls[i] = whole_w[0]
            if i + 1 < layers:
                in_fulls[i + 1] = whole_w[-1]
        else:
            normed = (
                current * lax.rsqrt(jnp.mean(current * current, axis=-1, keepdims=True) + norm_eps) * norm_gain[i]
            ).astype(bf16)
            projected = dot_nt(normed, in_fulls[i])
            tail = projected.reshape(rows, length, -1)[:, length - 8 :, :channels].astype(bf16)
            halo = lax.ppermute(tail, "bytes", ahead).reshape(8 * rows, channels)
            act, m = mixer.conv(projected, halo, p, masks)
            delta, end, total = mixer.ends(act, m, p, kill)
            start = carried_in(end, total, p["rate"], "bytes", False)
            y, gated, keep = mixer.scan(act, delta, projected, m, p, kill, start)
            x = z = projected
        saved.append((current, normed, x, z, halo, act, m, delta, total, y, gated, keep))
        current = current + dot(gated, out_fulls[i])
    flowing = cotangent.astype(f32).reshape(n, d)
    big, small, gains = [], [], []
    waiting, ready = [], []
    for i in reversed(range(layers)):
        p = None if fast else params[i]
        in_full, out_full = in_fulls[i], out_fulls[i]
        before, normed, x, z, halo, act, m, delta, total, y, gated, keep = saved[i]
        down = flowing.astype(bf16)
        grad_out = lax.dot_general(gated, down, (((0,), (0,)), ((), ())), preferred_element_type=f32).astype(bf16)
        gg = dot_nt(down, out_full)
        if fast:
            waiting.append(grad_out)
            (mixed, pieces), done = mixer.backward(
                i, gg, x, z, halo, y, act, delta, total, m, half, full, masks, kill, keep, waiting, 10 + i
            )
            ready += done
        else:
            gy, gz, gend = mixer.back_ends(gg, z, y, delta, m, p, kill)
            gstart = carried_in(gend, total, p["rate"], "bytes", True)
            gact, gproj, gproj_t, gdtw, gbias, grate, gskip = mixer.back(act, delta, gy, m, p, kill, keep, gstart)
            gx, edge, gxp, gkern, goff = mixer.conv_back(x, halo, p, masks, act, gact, gproj, gproj_t)
            late = lax.ppermute(edge.astype(bf16), "bytes", behind).astype(f32).reshape(rows, 8, channels)
            gx = (
                (gx.reshape(rows, length, channels) + jnp.pad(late, ((0, 0), (length - 8, 0), (0, 0))))
                .reshape(n, channels)
                .astype(bf16)
            )
            mixed = jnp.concatenate([gx, gz], axis=1)
            pieces = jnp.concatenate([gxp, gdtw, grate, gkern, goff, gbias, gskip], axis=0)
        grad_in = lax.dot_general(mixed, normed, (((0,), (0,)), ((), ())), preferred_element_type=f32).astype(bf16)
        small.append(pieces)
        waiting = [grad_in]
        if fast and i == 0:
            break
        gn = dot(mixed, in_full)
        inv = lax.rsqrt(jnp.mean(before * before, axis=-1, keepdims=True) + norm_eps)
        scaled = before * inv
        gains.append(jnp.sum(gn * scaled, axis=0))
        gs = gn * norm_gain[i]
        flowing = flowing + inv * (gs - scaled * jnp.mean(gs * scaled, axis=-1, keepdims=True))
        if not fast:
            big.append([lax.psum_scatter(g, both, scatter_dimension=0, tiled=True).astype(f32) for g in (grad_in, grad_out)])
    cuts = [width, rank, ns, taps, 1, 1, 1]
    if fast:
        packed = jnp.stack(small[::-1])
        packed = packed.reshape(4, layers * packed.shape[1] // 4, size, channels // size).transpose(0, 2, 1, 3)
        flowing, last_in, gain_total, *parts = finish(
            packed.reshape(-1, channels // size), grad_in, in_full, mixed, before, flowing, norm_gain[0][None],
            jnp.stack(gains[::-1]), cuts, 9,
        )
        ready.append(last_in)
        big = [(ready[2 * i + 1], ready[2 * i]) for i in range(layers)]
    else:
        packed = jnp.stack(small[::-1]).astype(bf16)
        packed = lax.psum_scatter(packed, "bytes", scatter_dimension=2, tiled=True)
        packed = lax.psum(packed, "rows").astype(f32)
        gain_total = lax.psum(jnp.stack(gains[::-1]), both)
        parts, at = [], 0
        for cut in cuts:
            parts.append(packed[:, at] if cut == 1 else packed[:, at : at + cut])
            at += cut
        parts[0] = parts[0].transpose(0, 2, 1)
    big = big[::-1]
    return (
        current.reshape(rows, length, d),
        flowing.reshape(rows, length, d),
        gain_total,
        jnp.stack([b[0] for b in big]),
        jnp.stack([b[1] for b in big]),
        parts[3],
        parts[4],
        parts[0],
        parts[1],
        parts[5],
        parts[2],
        parts[6],
    )


def solution(mesh):
    split = P("rows", "bytes", None)
    shared = P(None, ("rows", "bytes"), None)
    in_specs = (
        split, P("rows", None), P(), shared, shared, P(None, None, "bytes"), P(None, "bytes"),
        P(None, "bytes", None), P(None, None, "bytes"), P(None, "bytes"), P(None, None, "bytes"),
        P(None, "bytes"), split,
    )
    out_specs = (
        split, split, P(), shared, shared, P(None, None, "bytes"), P(None, "bytes"), P(None, "bytes", None),
        P(None, None, "bytes"), P(None, "bytes"), P(None, None, "bytes"), P(None, "bytes"),
    )
    return jax.shard_map(body, mesh=mesh, in_specs=in_specs, out_specs=out_specs, check_vma=False)
```

```python
import functools

import jax
import jax.numpy as jnp
from jax import lax
from jax.experimental import pallas as pl
from jax.experimental.pallas import tpu as pltpu
from jax.sharding import PartitionSpec as P

norm_eps = 1e-05
f32 = jnp.float32
bf16 = jnp.bfloat16
STEPS = 8
CB = 256
CB_ENDS = 512
CB_SCAN = 512
CB_BACK = 512
KILL = 1e30
LOG2E = 1.4426950408889634
VMEM = 58 * 2**20
FORWARD_ONE = (8, 15, 16, 17, 18, 18, 19, 20, 21)
FORWARD_EARLY = (8, 16, 17, 19, 20, 20, 20, 22, 23)
BACKWARD_STEPS = (0, 2, 4, 4, 4, 4, 4, 5, 6, 7, 8)

NT = (((1,), (1,)), ((), ()))


def dot(a, b):
    return jnp.dot(a, b, preferred_element_type=f32)


def dot_nt(a, b):
    return lax.dot_general(a, b, NT, preferred_element_type=f32)


def halves(v):
    high = v.astype(bf16)
    return high, (v - high.astype(f32)).astype(bf16)


def wide(v, width):
    return jnp.concatenate([v] * (width // v.shape[1]), axis=1)


def sigmoid(v):
    return 1.0 / (1.0 + jnp.exp(-v))


def conv_sum(x, halo, kernel, offset, masks, rows):
    length = x.shape[0] // rows
    taps = kernel.shape[0]
    outs = []
    for s in range(rows):
        ext = jnp.concatenate([halo[8 * s : 8 * s + 8], x[s * length : (s + 1) * length]], axis=0)
        total = offset + kernel[taps - 1 : taps] * ext[8:]
        for lag in range(1, taps):
            moved = pltpu.roll(ext, lag, 0)[8:]
            m = masks[lag - 1][s * length : (s + 1) * length]
            total = total + kernel[taps - 1 - lag : taps - lag] * moved * m
        outs.append(total)
    return jnp.concatenate(outs, axis=0)


class Packed:
    def __init__(self, rank, ns, taps):
        self.rank, self.ns, self.taps = rank, ns, taps
        self.width = rank + 2 * ns

    def rate(self, ref):
        return ref.at[0 : self.ns]

    def kernel(self, ref):
        return ref.at[self.ns : self.ns + self.taps]

    def row(self, ref, i):
        return ref.at[self.ns + self.taps + i : self.ns + self.taps + i + 1]

    def offset(self, ref):
        return self.row(ref, 0)

    def bias(self, ref):
        return self.row(ref, 1)

    def skip(self, ref):
        return self.row(ref, 2)

    def xproj(self, ref):
        return ref.at[0 : self.width]

    def dtproj(self, ref):
        return ref.at[self.width : self.width + self.rank]


def maps_part(rows, rank, ns, proj, rank2_ref, rank_t_ref, bb_ref, cc_ref, cd_ref):
    tokens = proj.shape[0]
    high, low = halves(proj[:, :rank])
    rank2_ref[...] = jnp.concatenate([high, low], axis=1)
    turned = proj.T
    rank_t_ref[...] = turned[:rank].astype(bf16)
    per = tokens // rows // STEPS
    for s in range(rows):
        for k in range(per):
            for t in range(STEPS):
                tok = (s * per + k) * STEPS + t
                at = ((k * rows + s) * STEPS + t) * ns
                bb_ref[at : at + ns, :] = jnp.broadcast_to(turned[rank : rank + ns, tok : tok + 1], (ns, 128))
                cc_ref[at : at + ns, :] = jnp.broadcast_to(turned[rank + ns :, tok : tok + 1], (ns, 128))
    inner = cd_ref.shape[-1]
    tile = (
        lax.broadcasted_iota(jnp.int32, (ns, inner), 0) == lax.broadcasted_iota(jnp.int32, (ns, inner), 1) % ns
    ).astype(bf16)
    spread = dot(proj[:, rank + ns :].astype(bf16), tile)
    tok = lax.broadcasted_iota(jnp.int32, (tokens, inner), 0)
    own = (tok // (tokens // rows)) * STEPS + tok % STEPS
    cd = jnp.where(own == lax.broadcasted_iota(jnp.int32, (tokens, inner), 1) // ns, spread, 0.0)
    cd_ref[...] = cd.reshape(cd_ref.shape)


def conv_part(rows, x, halo, kern_ref, off_ref, mask_ref, xp_ref, proj_s):
    cb = x.shape[1]
    masks = [wide(mask_ref[i], cb) for i in range(mask_ref.shape[0])]
    pre = conv_sum(x, halo, kern_ref[...], off_ref[...], masks, rows)
    act = pre * sigmoid(pre)
    high, low = halves(act)
    weight = xp_ref[...]
    proj_s[...] += dot_nt(high, weight) + dot_nt(low, weight)
    return act


def conv_kernel(rows, sizes, x_ref, halo_ref, kern_ref, off_ref, mask_ref, xp_ref,
                act_ref, rank2_ref, rank_t_ref, bb_ref, cc_ref, cd_ref, proj_s):
    block = pl.program_id(0)

    @pl.when(block == 0)
    def _():
        proj_s[...] = jnp.zeros_like(proj_s)

    act_ref[...] = conv_part(
        rows, x_ref[...].astype(bf16).astype(f32), halo_ref[...].astype(f32), kern_ref, off_ref, mask_ref, xp_ref, proj_s
    )

    @pl.when(block == pl.num_programs(0) - 1)
    def _():
        maps_part(rows, *sizes, proj_s[...], rank2_ref, rank_t_ref, bb_ref, cc_ref, cd_ref)


def step_sizes(rank2_ref, dtw_ref, bias_ref):
    weight = dtw_ref[...]
    pre = dot(rank2_ref[...], jnp.concatenate([weight, weight], axis=0)) + bias_ref[...]
    return jnp.maximum(pre, 0.0) + jnp.log1p(jnp.exp(-jnp.abs(pre)))


def chunked(v):
    return v.reshape(v.shape[0] // STEPS, STEPS, v.shape[1])


def tile_rows(ref, k, at, ns, inner, cb):
    v = ref[pl.ds(pl.multiple_of(k * inner, inner) + at, ns), :]
    return jnp.concatenate([v] * (cb // v.shape[1]), axis=1)


def lane_sum(v):
    out = v[:, :128]
    for i in range(1, v.shape[1] // 128):
        out = out + v[:, 128 * i : 128 * (i + 1)]
    return out


def ends_part(rows, act, rank2_ref, dtw_ref, bias_ref, kill_ref, rate_ref, bb_ref, eff_s, u_s):
    delta = step_sizes(rank2_ref, dtw_ref, bias_ref)
    cb = delta.shape[1]
    eff = delta + wide(kill_ref[...], cb)
    eff_s[...] = chunked(eff)
    u_s[...] = chunked(delta * act)
    length = eff.shape[0] // rows
    sums = jnp.concatenate(
        [jnp.sum(eff[s * length : (s + 1) * length], axis=0, keepdims=True) for s in range(rows)], axis=0
    )
    rate = rate_ref[...] * LOG2E
    ns = rate.shape[0]
    chunks = length // STEPS
    inner = rows * STEPS * ns

    def chunk(k, state):
        state = list(state)
        for t in range(STEPS):
            for s in range(rows):
                fade = jnp.exp2(rate * eff_s[s * chunks + k, t : t + 1, :])
                drive = u_s[s * chunks + k, t : t + 1, :] * tile_rows(bb_ref, k, (s * STEPS + t) * ns, ns, inner, cb)
                state[s] = fade * state[s] + drive
        return tuple(state)

    zero = jnp.zeros((ns, cb), f32)
    state = lax.fori_loop(0, chunks, chunk, (zero,) * rows)
    return delta, sums, jnp.concatenate(state, axis=0)


def scan_part(rows, delta, act, z, kill_ref, rate_ref, skip_ref, bb_ref, cd_ref, start,
              y_ref, gated_ref, keep_ref, eff_s, u_s, sa, sb, y_s):
    cb = delta.shape[1]
    eff_s[...] = chunked(delta + wide(kill_ref[...], cb))
    u_s[...] = chunked(delta * act)
    rate = rate_ref[...] * LOG2E
    ns = rate.shape[0]
    length = delta.shape[0] // rows
    chunks = length // STEPS
    inner = rows * STEPS * ns

    def scan(k, state, held):
        state = list(state)
        for s in range(rows):
            keep_ref[k, s * ns : (s + 1) * ns, :] = state[s]
        for t in range(STEPS):
            for s in range(rows):
                at = (s * STEPS + t) * ns
                fade = jnp.exp2(rate * eff_s[s * chunks + k, t : t + 1, :])
                drive = u_s[s * chunks + k, t : t + 1, :] * tile_rows(bb_ref, k, at, ns, inner, cb)
                state[s] = fade * state[s] + drive
                held[at : at + ns, :] = state[s].astype(bf16)
        return tuple(state)

    def leave(k, held):
        left = jnp.concatenate([cd_ref[s * chunks + k] for s in range(rows)], axis=0).astype(bf16)
        y = dot(left, held[...])
        for s in range(rows):
            y_s[s * chunks + k] = y[s * STEPS : (s + 1) * STEPS]

    sb[...] = jnp.zeros_like(sb)

    def two(i, state):
        k = 2 * i
        leave(jnp.maximum(k - 1, 0), sb)
        state = scan(k, state, sa)
        leave(k, sa)
        return scan(k + 1, state, sb)

    lax.fori_loop(0, chunks // 2, two, tuple(start[s * ns : (s + 1) * ns] for s in range(rows)))
    leave(chunks - 1, sb)
    y = (y_s[...].reshape(delta.shape) + skip_ref[...] * act).astype(bf16)
    y_ref[...] = y
    gated_ref[...] = (y.astype(f32) * (z * sigmoid(z))).astype(bf16)


def forward_kernel(rows, layer_of, sizes, *refs):
    n = len(layer_of)
    rank, ns, taps, narrow, blocks = sizes
    (h_ref, gain_ref, wx_ref, wz_ref, full_n, half_n, mask_ref, half_w, kill_ref, full_w, full_ref), refs = refs[:11], refs[11:]
    cut = Packed(rank, ns, taps)
    kern_ref, off_ref, xp_ref = cut.kernel(full_n), cut.offset(full_n), cut.xproj(half_n)
    dtw_ref, bias_ref, rate_ref = cut.dtproj(half_w), cut.bias(full_w), cut.rate(full_w)
    skip_ref, rates_ref = cut.skip(full_w), cut.rate(full_ref)
    srcs, refs = refs[:n], refs[n:]
    (normed_ref, x_ref, z_ref, halo_ref, act_ref, rank_t_ref, bb_ref, cc_ref, delta_ref, sum_ref, y_ref, gated_ref,
     keep_ref), refs = refs[:13], refs[13:]
    dsts, refs = refs[:n], refs[n:]
    (proj_s, x_s, tail_s, halo_s, act_s, z_s, rank2_s, cd_s, eff_s, u_s, sa, sb, y_s, delta_s, end_s, start_s,
     sum_s), refs = refs[:17], refs[17:]
    exch, (send, recv, hsend, hrecv) = refs[:10], refs[10:]
    here = Place()
    block = pl.program_id(0)
    front = 2 * narrow
    nb, cb = x_s.shape[2], eff_s.shape[2]
    per = cb // nb

    def halo(j):
        return push(tail_s.at[j], halo_s.at[j], hsend, hrecv, j, here.ring(1))

    @pl.when(block == 0)
    def _():
        greet(here.partners() + [here.ring(1), here.ring(-1)])
        proj_s[...] = jnp.zeros_like(proj_s)
        h = h_ref[...].astype(f32)
        normed_ref[...] = (
            h * lax.rsqrt(jnp.mean(h * h, axis=1, keepdims=True) + norm_eps) * gain_ref[...]
        ).astype(bf16)

    jobs = [
        Gather(here, src.at[layer], dst, send, recv, GATHER_SEMS * i)
        for i, (src, dst, layer) in enumerate(zip(srcs, dsts, layer_of))
    ]
    plans = [FORWARD_ONE if src.shape[1] * 32 < h_ref.shape[1] * 4 else FORWARD_EARLY for src in srcs]
    for job, plan in zip(jobs, plans):
        beside(job, block, plan)

    @pl.when(block < narrow)
    def _():
        normed = normed_ref[...]
        x = dot_nt(normed, wx_ref[...])
        z = dot_nt(normed, wz_ref[...])
        z_ref[...] = z
        z_s[block // per, :, pl.ds(pl.multiple_of(lax.rem(block, per) * nb, nb), nb)] = z
        x16 = x.astype(bf16)
        x_ref[...] = x16
        x_s[block] = x16
        length = x.shape[0] // rows
        tail_s[block] = jnp.concatenate([x[(s + 1) * length - 8 : (s + 1) * length] for s in range(rows)], axis=0).astype(bf16)
        halo(block).start()

    @pl.when((block >= narrow) & (block < front))
    def _():
        j = block - narrow
        halo(j).wait()
        before = halo_s[j]
        halo_ref[...] = before
        act = conv_part(
            rows, x_s[j].astype(f32), before.astype(f32), kern_ref, off_ref, mask_ref, xp_ref, proj_s
        )
        act_ref[...] = act
        act_s[j // per, :, pl.ds(pl.multiple_of(lax.rem(j, per) * nb, nb), nb)] = act

    @pl.when(block == front - 1)
    def _():
        maps_part(rows, rank, ns, proj_s[...], rank2_s, rank_t_ref, bb_ref, cc_ref, cd_s)

    @pl.when((block >= front) & (block < front + blocks))
    def _():
        j = block - front
        delta, sums, ends = ends_part(
            rows, act_s[j], rank2_s, dtw_ref, bias_ref, kill_ref, rate_ref, bb_ref, eff_s, u_s
        )
        cols = pl.ds(pl.multiple_of(j * cb, cb), cb)
        delta_ref[...] = delta
        delta_s[j] = delta
        sum_s[:, cols] = sums
        end_s[:, cols] = ends

    @pl.when(block == front + blocks - 1)
    def _():
        sum_ref[...] = sum_s[...]
        exchange(here, False, rows, end_s, sum_s, rates_ref, start_s, exch)

    @pl.when(block >= front + blocks)
    def _():
        j = block - front - blocks
        cols = pl.ds(pl.multiple_of(j * cb, cb), cb)
        scan_part(rows, delta_s[j], act_s[j], z_s[j], kill_ref, rate_ref, skip_ref, bb_ref, cd_s,
                  start_s[:, cols], y_ref, gated_ref, keep_ref, eff_s, u_s, sa, sb, y_s)

    @pl.when(block == pl.num_programs(0) - 1)
    def _():
        for job, plan in reversed(list(zip(jobs, plans))):
            for phase in job.phases[len(plan) :]:
                phase()


def back_ends_part(rows, gg_ref, z_ref, y_ref, delta_ref, kill_ref, rate_ref, cc_ref, gz_ref, eff_s, gy_s):
    z = z_ref[...]
    gg = gg_ref[...]
    sig = sigmoid(z)
    gy = (gg * z * sig).astype(bf16)
    gz_ref[...] = (gg * y_ref[...].astype(f32) * sig * (1.0 + z * (1.0 - sig))).astype(bf16)
    cb = z.shape[1]
    eff_s[...] = chunked(delta_ref[...] + wide(kill_ref[...], cb))
    gy_s[...] = chunked(gy.astype(f32))
    rate = rate_ref[...] * LOG2E
    ns = rate.shape[0]
    length = z.shape[0] // rows
    chunks = length // STEPS
    inner = rows * STEPS * ns

    def chunk(i, flow):
        k = chunks - 1 - i
        flow = list(flow)
        for t in reversed(range(STEPS)):
            for s in range(rows):
                fade = jnp.exp2(rate * eff_s[s * chunks + k, t : t + 1, :])
                push = gy_s[s * chunks + k, t : t + 1, :] * tile_rows(cc_ref, k, (s * STEPS + t) * ns, ns, inner, cb)
                flow[s] = fade * (flow[s] + push)
        return tuple(flow)

    zero = jnp.zeros((ns, cb), f32)
    flow = lax.fori_loop(0, chunks, chunk, (zero,) * rows)
    return gy, jnp.concatenate(flow, axis=0)


def back_part(rows, act_ref, delta_ref, gy, kill_ref, rate_ref, skip_ref, dtw_ref, rank_t_ref, bb_ref, cc_ref, keep_ref,
              start, gact_ref, gdtw_ref, gbias_ref, grate_ref, gskip_ref,
              eff_s, u_s, gy_s, fade_s, held_s, sa, sb, gu_s, gd_s, gb_s, gc_s, grank_s):
    delta = delta_ref[...]
    act = act_ref[...]
    cb = delta.shape[1]
    eff_s[...] = chunked(delta + wide(kill_ref[...], cb))
    u_s[...] = chunked(delta * act)
    gy_s[...] = chunked(gy)
    rate_n = rate_ref[...]
    rate = rate_n * LOG2E
    ns = rate.shape[0]
    length = delta.shape[0] // rows
    chunks = length // STEPS
    pairs = rows * STEPS
    inner = pairs * ns
    half = ns // 2
    side = pairs * half
    pick = (
        lax.broadcasted_iota(jnp.int32, (2 * pairs, 2 * side), 0)
        == lax.broadcasted_iota(jnp.int32, (2 * pairs, 2 * side), 1) // half
    ).astype(bf16)

    def scan(k, carry, sums):
        flow, total = list(carry[0]), carry[1]
        state = [keep_ref[k, s * ns : (s + 1) * ns, :] for s in range(rows)]
        base = pl.multiple_of(k * inner, inner)
        for t in range(STEPS):
            for s in range(rows):
                at = (s * STEPS + t) * ns
                fade = jnp.exp2(rate * eff_s[s * chunks + k, t : t + 1, :])
                held = fade * state[s]
                fade_s[at : at + ns, :] = fade
                held_s[at : at + ns, :] = held
                drive = u_s[s * chunks + k, t : t + 1, :] * tile_rows(bb_ref, k, at, ns, inner, cb)
                state[s] = held + drive
                gc_s[pl.ds(base + at, ns), :] += lane_sum(state[s] * gy_s[s * chunks + k, t : t + 1, :])
        for t in reversed(range(STEPS)):
            for s in range(rows):
                at = (s * STEPS + t) * ns
                push = gy_s[s * chunks + k, t : t + 1, :] * tile_rows(cc_ref, k, at, ns, inner, cb)
                grad = flow[s] + push
                gb_s[pl.ds(base + at, ns), :] += lane_sum(grad * u_s[s * chunks + k, t : t + 1, :])
                w = grad * held_s[at : at + ns, :]
                total = total + w * eff_s[s * chunks + k, t : t + 1, :]
                gu = grad * tile_rows(bb_ref, k, at, ns, inner, cb)
                wa = w * rate_n
                low = (s * STEPS + t) * half
                sums[low : low + half, :] = gu[:half] + gu[half:]
                sums[side + low : side + low + half, :] = wa[:half] + wa[half:]
                flow[s] = fade_s[at : at + ns, :] * grad
        return tuple(flow), total

    def leave(k, sums):
        out = dot(pick, sums[...].astype(bf16))
        for s in range(rows):
            gu_s[s * chunks + k] = out[s * STEPS : (s + 1) * STEPS]
            gd_s[s * chunks + k] = out[pairs + s * STEPS : pairs + (s + 1) * STEPS]

    sb[...] = jnp.zeros_like(sb)

    def two(i, carry):
        k = chunks - 1 - 2 * i
        leave(jnp.minimum(k + 1, chunks - 1), sb)
        carry = scan(k, carry, sa)
        leave(k, sa)
        return scan(k - 1, carry, sb)

    first = tuple(start[s * ns : (s + 1) * ns] for s in range(rows))
    _, total = lax.fori_loop(0, chunks // 2, two, (first, jnp.zeros((ns, cb), f32)))
    leave(0, sb)
    grate_ref[...] = total * rate_n
    gu = gu_s[...].reshape(delta.shape)
    gact_ref[...] = gu * delta + skip_ref[...] * gy
    gskip_ref[...] = jnp.sum(gy * act, axis=0, keepdims=True)
    gpre = (gu * act + gd_s[...].reshape(delta.shape)) * (1.0 - jnp.exp(-delta))
    gbias_ref[...] = jnp.sum(gpre, axis=0, keepdims=True)
    gpre16 = gpre.astype(bf16)
    gdtw_ref[...] = dot(rank_t_ref[...], gpre16)
    grank_s[...] += dot_nt(gpre16, dtw_ref[...])


def fold_part(rows, ns, gproj_ref, gproj_t_ref, gb_s, gc_s, grank_s):
    pairs = rows * STEPS
    inner = pairs * ns
    chunks = gb_s.shape[0] // inner
    ones = jnp.ones((128, 128), bf16)
    lane = lax.broadcasted_iota(jnp.int32, (pairs, ns, 128), 2)
    spot = lax.broadcasted_iota(jnp.int32, (pairs, ns, 128), 1)
    rank = grank_s.shape[1]

    def fold(ref, k):
        high, low = halves(ref[k * inner : (k + 1) * inner, :])
        v = (dot(high, ones) + dot(low, ones)).reshape(pairs, ns, 128)
        return jnp.sum(jnp.where(lane == spot, v, 0.0), axis=1)[:, :ns]

    for k in range(chunks):
        gb, gc = fold(gb_s, k), fold(gc_s, k)
        for s in range(rows):
            here = slice((s * chunks + k) * STEPS, (s * chunks + k + 1) * STEPS)
            mine = slice(s * STEPS, (s + 1) * STEPS)
            gproj_ref[here, :] = jnp.concatenate([grank_s[here, :], gb[mine], gc[mine]], axis=1)
    gproj_t_ref[...] = gproj_ref[...].T


def backward_kernel(rows, n, sizes, *refs):
    blocks, narrow, rank, ns, taps = sizes
    (gg_ref, z_ref, y_ref, wdelta_ref, full_w, kill_ref, full_ref, sum_ref, act_ref, delta_ref, full_n,
     half_n, rank_t_ref, bb_ref, cc_ref, keep_ref, x_ref, halo_ref, mask_ref) = refs[:19]
    refs = refs[19:]
    cut = Packed(rank, ns, taps)
    wrate_ref, rates_ref, rate_ref, skip_ref = cut.rate(full_w), cut.rate(full_ref), cut.rate(full_n), cut.skip(full_n)
    dtw_ref, xp_ref, kern_ref, off_ref = cut.dtproj(half_n), cut.xproj(half_n), cut.kernel(full_n), cut.offset(full_n)
    srcs, refs = refs[:n], refs[n:]
    (mixed_ref, packed_ref), refs = refs[:2], refs[2:]
    sums, refs = refs[:n], refs[n:]
    (weff_s, wgy_s, gyall_s, end_s, start_s, gz_s, gact_s, gproj_s, gproj_t_s, gend_s, edge_s, late_s, gdtw_s, gbias_s, grate_s,
     gskip_s, gxp_s, gkern_s, goff_s), refs = refs[:19], refs[19:]
    (eff_s, u_s, gy_s, fade_s, held_s, sa, sb, gu_s, gd_s, gb_s, gc_s, grank_s), refs = refs[:12], refs[12:]
    exch, (esend, erecv), refs = refs[:10], refs[10:12], refs[12:]
    here = Place()
    block = pl.program_id(0)
    wide_cb, cb = gg_ref.shape[1], act_ref.shape[1]
    c = wide_cb * blocks

    def edge(j):
        return push(edge_s.at[j], late_s.at[j], esend, erecv, j, here.ring(-1))

    @pl.when(block == 0)
    def _():
        greet(here.partners() + [here.ring(1), here.ring(-1)])
        gc_s[...] = jnp.zeros_like(gc_s)
        gb_s[...] = jnp.zeros_like(gb_s)
        grank_s[...] = jnp.zeros_like(grank_s)

    beside(Reduces(srcs, sums, refs), block, BACKWARD_STEPS)

    @pl.when(block < blocks)
    def _():
        gy, flow = back_ends_part(
            rows, gg_ref, z_ref, y_ref, wdelta_ref, kill_ref, wrate_ref, cc_ref, gz_s, weff_s, wgy_s
        )
        cols = pl.ds(pl.multiple_of(block * wide_cb, wide_cb), wide_cb)
        mixed_ref[:, pl.ds(pl.multiple_of(c + block * wide_cb, wide_cb), wide_cb)] = gz_s[...]
        gyall_s[:, cols] = gy.astype(f32)
        end_s[:, cols] = flow

    @pl.when(block == blocks - 1)
    def _():
        exchange(here, True, rows, end_s, sum_ref, rates_ref, start_s, exch)

    @pl.when((block >= blocks) & (block < blocks + narrow))
    def _():
        j = block - blocks
        cols = pl.ds(pl.multiple_of(j * cb, cb), cb)
        back_part(rows, act_ref, delta_ref, gyall_s[:, cols], kill_ref, rate_ref, skip_ref, dtw_ref, rank_t_ref,
                  bb_ref, cc_ref, keep_ref, start_s[:, cols], gact_s.at[j], gdtw_s.at[j], gbias_s.at[j], grate_s.at[j], gskip_s.at[j],
                  eff_s, u_s, gy_s, fade_s, held_s, sa, sb, gu_s, gd_s, gb_s, gc_s, grank_s)

    @pl.when(block == blocks + narrow - 1)
    def _():
        fold_part(rows, rate_ref.shape[0], gproj_s, gproj_t_s, gb_s, gc_s, grank_s)

    @pl.when(block >= blocks + narrow)
    def _():
        j = block - blocks - narrow
        cols = pl.ds(pl.multiple_of(j * cb, cb), cb)
        gx, edges = conv_back_part(
            rows, x_ref, halo_ref, kern_ref, off_ref, mask_ref, act_ref, gact_s[j], gproj_s, gproj_t_s, xp_ref,
            gxp_s, gkern_s, goff_s
        )
        rows_of = [gxp_s[...], gdtw_s[j], grate_s[j], gkern_s[...], goff_s[...], gbias_s[j], gskip_s[j]]
        count = sum(v.shape[0] for v in rows_of)
        rows_of.append(jnp.zeros((packed_ref.shape[0] - count, cb), f32))
        packed_ref[...] = jnp.concatenate(rows_of, axis=0).astype(bf16)
        edge_s[j] = edges.astype(bf16)
        edge(j).start()
        mixed_ref[:, cols] = gx.astype(bf16)
        length = gx.shape[0] // rows
        gend_s[j] = jnp.concatenate([gx[(s + 1) * length - 16 : (s + 1) * length] for s in range(rows)], axis=0)

    @pl.when(block == pl.num_programs(0) - 1)
    def _():
        more = jnp.where((here.z == 3) & (here.c == 1), 0.0, 1.0)
        length = mixed_ref.shape[0] // rows
        for j in range(narrow):
            edge(j).wait()
            late = late_s[j].astype(f32) * more
            for s in range(rows):
                end = gend_s[j, 16 * s : 16 * s + 16]
                fixed = jnp.concatenate([end[:8], end[8:] + late[8 * s : 8 * s + 8]], axis=0)
                mixed_ref[(s + 1) * length - 16 : (s + 1) * length, j * cb : (j + 1) * cb] = fixed.astype(bf16)
        Reduces(srcs, sums, refs).run(-1)


def ends_kernel(rows, act_ref, rank2_ref, dtw_ref, bias_ref, kill_ref, rate_ref, bb_ref,
                delta_ref, end_ref, sum_ref, eff_s, u_s):
    delta_ref[...], sum_ref[...], end_ref[...] = ends_part(
        rows, act_ref[...], rank2_ref, dtw_ref, bias_ref, kill_ref, rate_ref, bb_ref, eff_s, u_s
    )


def scan_kernel(rows, act_ref, delta_ref, z_ref, kill_ref, rate_ref, skip_ref, bb_ref, cd_ref, start_ref, *refs):
    scan_part(rows, delta_ref[...], act_ref[...], z_ref[...], kill_ref, rate_ref, skip_ref, bb_ref, cd_ref, start_ref[...], *refs)


def back_ends_kernel(rows, gg_ref, z_ref, y_ref, delta_ref, kill_ref, rate_ref, cc_ref,
                     gy_ref, gz_ref, end_ref, eff_s, gy_s):
    gy_ref[...], end_ref[...] = back_ends_part(
        rows, gg_ref, z_ref, y_ref, delta_ref, kill_ref, rate_ref, cc_ref, gz_ref, eff_s, gy_s
    )


def back_kernel(rows, act_ref, delta_ref, gy_ref, kill_ref, rate_ref, skip_ref, dtw_ref, rank_t_ref,
                bb_ref, cc_ref, keep_ref, start_ref,
                gact_ref, gproj_ref, gproj_t_ref, gdtw_ref, gbias_ref, grate_ref, gskip_ref, *scratch):
    gb_s, gc_s, grank_s = scratch[-3:]

    @pl.when(pl.program_id(0) == 0)
    def _():
        gc_s[...] = jnp.zeros_like(gc_s)
        gb_s[...] = jnp.zeros_like(gb_s)
        grank_s[...] = jnp.zeros_like(grank_s)

    back_part(rows, act_ref, delta_ref, gy_ref[...].astype(f32), kill_ref, rate_ref, skip_ref, dtw_ref, rank_t_ref,
              bb_ref, cc_ref, keep_ref, start_ref[...], gact_ref, gdtw_ref, gbias_ref, grate_ref, gskip_ref, *scratch)

    @pl.when(pl.program_id(0) == pl.num_programs(0) - 1)
    def _():
        fold_part(rows, rate_ref.shape[0], gproj_ref, gproj_t_ref, gb_s, gc_s, grank_s)


def conv_back_part(rows, x_ref, halo_ref, kern_ref, off_ref, mask_ref, act_ref, gact, gproj_ref,
                   gproj_t_ref, xp_ref, gxp_ref, gkern_ref, goff_ref):
    x = x_ref[...].astype(bf16).astype(f32)
    cb = x.shape[1]
    halo = halo_ref[...].astype(f32)
    kernel = kern_ref[...]
    taps = kernel.shape[0]
    masks = [wide(mask_ref[i], cb) for i in range(taps - 1)]
    pre = conv_sum(x, halo, kernel, off_ref[...], masks, rows)
    sig = sigmoid(pre)
    act16 = act_ref[...].astype(bf16)
    gxp_ref[...] = dot(gproj_t_ref[...].astype(bf16), act16)
    g_act = gact + dot(gproj_ref[...].astype(bf16), xp_ref[...])
    gpre = g_act * sig * (1.0 + pre * (1.0 - sig))
    goff_ref[...] = jnp.sum(gpre, axis=0, keepdims=True)
    length = x.shape[0] // rows
    place = lax.broadcasted_iota(jnp.int32, (length, cb), 0)
    gk = [jnp.zeros((1, cb), f32) for _ in range(taps)]
    gxs, edges = [], []
    for s in range(rows):
        here = slice(s * length, (s + 1) * length)
        g = gpre[here]
        ext = jnp.concatenate([halo[8 * s : 8 * s + 8], x[here]], axis=0)
        gk[taps - 1] = gk[taps - 1] + jnp.sum(g * x[here], axis=0, keepdims=True)
        gx = kernel[taps - 1 : taps] * g
        edge = jnp.zeros((length, cb), f32)
        for lag in range(1, taps):
            gm = g * masks[lag - 1][here]
            moved = pltpu.roll(ext, lag, 0)[8:]
            j = taps - 1 - lag
            gk[j] = gk[j] + jnp.sum(gm * moved, axis=0, keepdims=True)
            up = pltpu.roll(kernel[j : j + 1] * gm, length - lag, 0)
            inside = place < length - lag
            gx = gx + jnp.where(inside, up, 0.0)
            edge = edge + jnp.where(inside, 0.0, up)
        gxs.append(gx)
        edges.append(edge[length - 8 :])
    gkern_ref[...] = jnp.concatenate(gk, axis=0)
    return jnp.concatenate(gxs, axis=0), jnp.concatenate(edges, axis=0)


def conv_back_kernel(rows, x_ref, halo_ref, kern_ref, off_ref, mask_ref, act_ref, gact_ref, gproj_ref,
                     gproj_t_ref, xp_ref, gx_ref, edge_ref, *outs):
    gx_ref[...], edge_ref[...] = conv_back_part(
        rows, x_ref, halo_ref, kern_ref, off_ref, mask_ref, act_ref, gact_ref[...], gproj_ref, gproj_t_ref, xp_ref, *outs
    )


def col(rows, cb, shift=0):
    return pl.BlockSpec((rows, cb), lambda j: (0, j + shift))


def whole(*shape):
    return pl.BlockSpec(shape, lambda j: (0,) * len(shape))


def call(body, blocks, ins, outs, scratch, args, ident=None):
    more = {} if ident is None else dict(collective_id=ident, has_side_effects=True)
    return pl.pallas_call(
        body,
        grid=(blocks,),
        in_specs=ins,
        out_specs=[spec for spec, _, _ in outs],
        out_shape=[jax.ShapeDtypeStruct(shape, kind) for _, shape, kind in outs],
        scratch_shapes=scratch,
        compiler_params=pltpu.CompilerParams(
            dimension_semantics=("arbitrary",), vmem_limit_bytes=VMEM, **more
        ),
    )(*args)


class Mixer:
    def __init__(self, layers, rows, length, channels, ns, rank, taps):
        self.layers = layers
        self.rows, self.length, self.c, self.ns, self.rank, self.taps = rows, length, channels, ns, rank, taps
        self.tokens = rows * length
        self.chunks = length // STEPS
        self.pairs = rows * STEPS
        self.inner = self.pairs * ns
        self.width = rank + 2 * ns

    def conv(self, projected, halo, p, masks):
        t, c, cb = self.tokens, self.c, CB
        tall = (t * self.ns, 128)
        out = call(
            functools.partial(conv_kernel, self.rows, (self.rank, self.ns)), c // cb,
            [col(t, cb), col(8 * self.rows, cb), col(self.taps, cb), col(1, cb), whole(*masks.shape), col(self.width, cb)],
            [(col(t, cb), (t, c), f32), (whole(t, 2 * self.rank), (t, 2 * self.rank), bf16),
             (whole(self.rank, t), (self.rank, t), bf16), (whole(*tall), tall, f32), (whole(*tall), tall, f32),
             (whole(t, self.inner), (t, self.inner), f32)],
            [pltpu.VMEM((t, self.width), f32)], (projected, halo, p["conv_w"], p["conv_b"], masks, p["xproj"]),
        )
        m = dict(zip(("rank2", "rank_t", "bb", "cc", "cd"), out[1:]))
        m["cd"] = m["cd"].reshape(-1, STEPS, self.inner)
        return out[0], m

    def scratch3(self, cb):
        return pltpu.VMEM((self.tokens // STEPS, STEPS, cb), f32)

    def wide_scratch(self, kind, cb):
        return pltpu.VMEM((self.inner, cb), kind)

    def forward(self, i, h, gain, in_full, half, full, masks, kill, gathers, ident):
        t, c, sn, cb, nb, ns, d = self.tokens, self.c, self.rows * self.ns, CB_SCAN, CB, self.ns, h.shape[1]
        narrow, blocks = c // nb, c // cb
        front = 2 * narrow
        hn, fn = half.shape[0] // self.layers, full.shape[0] // self.layers

        def first(rows):
            return pl.BlockSpec((rows, nb), lambda j: (0, jnp.minimum(j, narrow - 1)))

        def second(rows):
            return pl.BlockSpec((rows, nb), lambda j: (0, jnp.clip(j - narrow, 0, narrow - 1)))

        def early(rows):
            return pl.BlockSpec((rows, cb), lambda j: (0, jnp.clip(j - front, 0, blocks - 1)))

        def both(rows):
            return pl.BlockSpec((rows, cb), lambda j: (0, lax.rem(jnp.maximum(j - front, 0), blocks)))

        def late(rows):
            return pl.BlockSpec((rows, cb), lambda j: (0, jnp.maximum(j - front - blocks, 0)))

        def at(spec):
            return pl.BlockSpec(spec.block_shape, lambda j: (i, spec.index_map(j)[1]))

        wx = pl.BlockSpec((nb, d), lambda j: (jnp.minimum(j, narrow - 1), 0))
        wz = pl.BlockSpec((nb, d), lambda j: (jnp.minimum(j, narrow - 1) + narrow, 0))
        n = len(gathers)
        keep = pl.BlockSpec((self.chunks, sn, cb), lambda j: (0, 0, jnp.maximum(j - front - blocks, 0)))
        sems = [pltpu.SemaphoreType.DMA((GATHER_SEMS * max(n, 1),))] * 2 + [pltpu.SemaphoreType.DMA((narrow,))] * 2
        tall = (t * ns, 128)
        hr = 8 * self.rows
        out = call(
            functools.partial(forward_kernel, self.rows, [k for _, k in gathers], (self.rank, ns, self.taps, narrow, blocks)), front + 2 * blocks,
            [whole(t, d), whole(1, d), wx, wz, at(second(fn)), at(second(hn)), whole(*masks.shape), at(early(hn)),
             whole(*kill.shape), at(both(fn)), pl.BlockSpec((fn, c), lambda j: (i, 0))] + [ANY] * n,
            [(whole(t, d), (t, d), bf16), (first(t), (t, c), bf16), (first(t), (t, c), f32), (second(hr), (hr, c), bf16),
             (second(t), (t, c), f32), (whole(self.rank, t), (self.rank, t), bf16), (whole(*tall), tall, f32),
             (whole(*tall), tall, f32), (early(t), (t, c), f32), (whole(self.rows, c), (self.rows, c), f32),
             (late(t), (t, c), bf16), (late(t), (t, c), bf16), (keep, (self.chunks, sn, c), f32)]
            + [(ANY, (2, 2, 4, 2) + g.shape[1:], g.dtype) for g, _ in gathers],
            [pltpu.VMEM((t, self.width), f32), pltpu.VMEM((narrow, t, nb), bf16), pltpu.VMEM((narrow, hr, nb), bf16),
             pltpu.VMEM((narrow, hr, nb), bf16), pltpu.VMEM((blocks, t, cb), f32), pltpu.VMEM((blocks, t, cb), f32),
             pltpu.VMEM((t, 2 * self.rank), bf16), pltpu.VMEM((t // STEPS, STEPS, self.inner), f32),
             self.scratch3(cb), self.scratch3(cb), self.wide_scratch(bf16, cb), self.wide_scratch(bf16, cb),
             self.scratch3(cb), pltpu.VMEM((blocks, t, cb), f32), pltpu.VMEM((sn, c), f32), pltpu.VMEM((sn, c), f32),
             pltpu.VMEM((self.rows, c), f32)] + exchange_scratch(self.rows, sn, c) + sems,
            (h, gain, in_full, in_full, full, half, masks, half, kill, full, full, *[g for g, _ in gathers]),
            ident,
        )
        return out[:13], [g.reshape(-1, g.shape[-1]) for g in out[13:]]

    def backward(self, i, gg, x, z, halo, y, act, delta, total, m, half, full, masks, kill, keep, sums, ident):
        t, c, sn, ns, cb, wcb = self.tokens, self.c, self.rows * self.ns, self.ns, CB_BACK, CB_ENDS
        blocks, narrow = c // wcb, c // cb

        def early(rows):
            return pl.BlockSpec((rows, wcb), lambda j: (0, jnp.minimum(j, blocks - 1)))

        def late(rows):
            return pl.BlockSpec((rows, cb), lambda j: (0, jnp.clip(j - blocks, 0, narrow - 1)))

        def last(rows):
            return pl.BlockSpec((rows, cb), lambda j: (0, jnp.maximum(j - blocks - narrow, 0)))

        def twice(rows):
            return pl.BlockSpec((rows, cb), lambda j: (0, lax.rem(jnp.maximum(j - blocks, 0), narrow)))

        def at(spec):
            return pl.BlockSpec(spec.block_shape, lambda j: (i, spec.index_map(j)[1]))

        hn, fn = half.shape[0] // self.layers, full.shape[0] // self.layers
        kept = pl.BlockSpec((self.chunks, sn, cb), lambda j: (0, 0, jnp.clip(j - blocks, 0, narrow - 1)))
        tall = m["bb"].shape
        hr = 8 * self.rows
        pack = self.width + self.rank + ns + self.taps + 3
        pack += -pack % 64
        more_in, more_out, more_scratch = reduce_parts(sums)
        sems = [pltpu.SemaphoreType.DMA((narrow,))] * 2
        out = call(
            functools.partial(backward_kernel, self.rows, len(sums), (blocks, narrow, self.rank, ns, self.taps)), blocks + 2 * narrow,
            [early(t), early(t), early(t), early(t), at(early(fn)), whole(*kill.shape), pl.BlockSpec((fn, c), lambda j: (i, 0)),
             whole(self.rows, c), twice(t), late(t), at(twice(fn)), at(twice(hn)), whole(*m["rank_t"].shape), whole(*tall),
             whole(*tall), kept, last(t), last(hr), whole(*masks.shape)] + [ANY] * len(sums),
            [(whole(t, 2 * c), (t, 2 * c), bf16), (last(pack), (pack, c), bf16)]
            + [(whole(*v.shape), v.shape, f32) for v in more_out],
            [self.scratch3(wcb)] * 2 + [pltpu.VMEM((t, c), f32), pltpu.VMEM((sn, c), f32), pltpu.VMEM((sn, c), f32)]
            + [pltpu.VMEM((t, wcb), bf16), pltpu.VMEM((narrow, t, cb), f32), pltpu.VMEM((t, self.width), f32),
               pltpu.VMEM((self.width, t), f32), pltpu.VMEM((narrow, 2 * hr, cb), f32), pltpu.VMEM((narrow, hr, cb), bf16),
               pltpu.VMEM((narrow, hr, cb), bf16)]
            + [pltpu.VMEM((narrow, k, cb), f32) for k in (self.rank, 1, ns, 1)]
            + [pltpu.VMEM((k, cb), f32) for k in (self.width, self.taps, 1)]
            + [self.scratch3(cb)] * 3 + [self.wide_scratch(f32, cb)] * 4 + [self.scratch3(cb)] * 2
            + [pltpu.VMEM(tall, f32)] * 2 + [pltpu.VMEM((t, self.rank), f32)] + exchange_scratch(self.rows, sn, c)
            + sems + more_scratch,
            (gg, z, y, delta, full, kill, full, total, act, delta, full, half, m["rank_t"], m["bb"], m["cc"], keep, x, halo,
             masks, *more_in),
            ident,
        )
        return out[:2], out[2:]

    def ends(self, act, m, p, kill):
        t, c, sn, cb = self.tokens, self.c, self.rows * self.ns, CB_ENDS
        return call(
            functools.partial(ends_kernel, self.rows), c // cb,
            [col(t, cb), whole(*m["rank2"].shape), col(self.rank, cb), col(1, cb), whole(*kill.shape), col(self.ns, cb),
             whole(*m["bb"].shape)],
            [(col(t, cb), (t, c), f32), (col(sn, cb), (sn, c), f32), (col(self.rows, cb), (self.rows, c), f32)],
            [self.scratch3(cb), self.scratch3(cb)],
            (act, m["rank2"], p["dtproj"], p["dt_b"], kill, p["rate"], m["bb"]),
        )

    def scan(self, act, delta, projected, m, p, kill, start):
        t, c, sn, cb = self.tokens, self.c, self.rows * self.ns, CB_SCAN
        keep = pl.BlockSpec((self.chunks, sn, cb), lambda j: (0, 0, j))
        return call(
            functools.partial(scan_kernel, self.rows), c // cb,
            [col(t, cb), col(t, cb), col(t, cb, c // cb), whole(*kill.shape), col(self.ns, cb), col(1, cb),
             whole(*m["bb"].shape), whole(*m["cd"].shape), col(sn, cb)],
            [(col(t, cb), (t, c), bf16), (col(t, cb), (t, c), bf16), (keep, (self.chunks, sn, c), f32)],
            [self.scratch3(cb), self.scratch3(cb), self.wide_scratch(bf16, cb), self.wide_scratch(bf16, cb),
             self.scratch3(cb)],
            (act, delta, projected, kill, p["rate"], p["skip"], m["bb"], m["cd"], start),
        )

    def back_ends(self, gg, projected, y, delta, m, p, kill):
        t, c, sn, cb = self.tokens, self.c, self.rows * self.ns, CB_ENDS
        return call(
            functools.partial(back_ends_kernel, self.rows), c // cb,
            [col(t, cb), col(t, cb, c // cb), col(t, cb), col(t, cb), whole(*kill.shape), col(self.ns, cb),
             whole(*m["cc"].shape)],
            [(col(t, cb), (t, c), bf16), (col(t, cb), (t, c), bf16), (col(sn, cb), (sn, c), f32)],
            [self.scratch3(cb), self.scratch3(cb)],
            (gg, projected, y, delta, kill, p["rate"], m["cc"]),
        )

    def back(self, act, delta, gy, m, p, kill, keep, start):
        t, c, sn, ns, cb = self.tokens, self.c, self.rows * self.ns, self.ns, CB_BACK
        kept = pl.BlockSpec((self.chunks, sn, cb), lambda j: (0, 0, j))
        tall = m["bb"].shape
        return call(
            functools.partial(back_kernel, self.rows), c // cb,
            [col(t, cb), col(t, cb), col(t, cb), whole(*kill.shape), col(ns, cb), col(1, cb), col(self.rank, cb),
             whole(*m["rank_t"].shape), whole(*tall), whole(*tall), kept, col(sn, cb)],
            [(col(t, cb), (t, c), f32), (whole(t, self.width), (t, self.width), f32),
             (whole(self.width, t), (self.width, t), f32), (col(self.rank, cb), (self.rank, c), f32),
             (col(1, cb), (1, c), f32), (col(ns, cb), (ns, c), f32), (col(1, cb), (1, c), f32)],
            [self.scratch3(cb)] * 3 + [self.wide_scratch(f32, cb)] * 4 + [self.scratch3(cb)] * 2
            + [pltpu.VMEM(tall, f32)] * 2 + [pltpu.VMEM((t, self.rank), f32)],
            (act, delta, gy, kill, p["rate"], p["skip"], p["dtproj"], m["rank_t"], m["bb"], m["cc"], keep, start),
        )

    def conv_back(self, projected, halo, p, masks, act, gact, gproj, gproj_t):
        t, c, cb = self.tokens, self.c, CB
        return call(
            functools.partial(conv_back_kernel, self.rows), c // cb,
            [col(t, cb), col(8 * self.rows, cb), col(self.taps, cb), col(1, cb), whole(*masks.shape), col(t, cb),
             col(t, cb), whole(t, self.width), whole(self.width, t), col(self.width, cb)],
            [(col(t, cb), (t, c), f32), (col(8 * self.rows, cb), (8 * self.rows, c), f32),
             (col(self.width, cb), (self.width, c), f32), (col(self.taps, cb), (self.taps, c), f32),
             (col(1, cb), (1, c), f32)],
            [], (projected, halo, p["conv_w"], p["conv_b"], masks, act, gact, gproj, gproj_t, p["xproj"]),
        )


MESH = pl.DeviceIdType.MESH
ANY = pl.BlockSpec(memory_space=pl.ANY)
INV = pl.BlockSpec(memory_space=pltpu.VMEM)


class Place:
    def __init__(self):
        r, b = lax.axis_index("rows"), lax.axis_index("bytes")
        self.y, self.x, self.z, self.c = r // 2, lax.rem(r, 2), b // 2, lax.rem(b, 2)

    def at(self, y=None, x=None, z=None, c=None):
        y = self.y if y is None else y
        x = self.x if x is None else x
        z = self.z if z is None else z
        c = self.c if c is None else c
        return (y * 2 + x, z * 2 + c)

    def over(self, k):
        return lax.rem(self.z + k, 4)

    def ring(self, step):
        b = lax.rem(self.z * 2 + self.c + 8 + step, 8)
        return self.at(z=b // 2, c=lax.rem(b, 2))

    def partners(self):
        return [self.at(c=1 - self.c), self.at(x=1 - self.x), self.at(y=1 - self.y)] + [
            self.at(z=self.over(k)) for k in (1, 2, 3)
        ]


def greet(partners):
    barrier = pltpu.get_barrier_semaphore()
    for p in partners:
        pl.semaphore_signal(barrier, inc=1, device_id=p, device_id_type=MESH)
    pl.semaphore_wait(barrier, len(partners))


def push(src, dst, send, recv, i, device):
    return pltpu.make_async_remote_copy(
        src_ref=src, dst_ref=dst, send_sem=send.at[i], recv_sem=recv.at[i], device_id=device, device_id_type=MESH
    )


GATHER_SEMS = 36
TURN = (1, 3, 2)


class Gather:
    def __init__(self, here, src, dst, send, recv, base):
        self.here, self.src, self.dst, self.send, self.recv, self.base = here, src, dst, send, recv, base
        self.h = src.shape[0] // 2
        part = functools.partial
        self.phases = [self.begin, part(self.side, 0), part(self.come, 1), part(self.come, 3), part(self.side, 1),
                       part(self.come, 2), part(self.side, 3), part(self.side, 2), self.cross, self.last]

    def source(self, k):
        return lax.rem(self.here.z + 4 - k, 4)

    def own(self):
        h = self.here
        return pltpu.make_async_copy(self.src, self.dst.at[h.y, h.x, h.z, h.c], self.send.at[self.base + 35])

    def push(self, src, dst, i, device):
        return push(src, dst, self.send, self.recv, self.base + i, device)

    def line(self, k):
        h = self.here
        return self.push(self.src, self.dst.at[h.y, h.x, h.z, h.c], k - 1, h.at(z=h.over(k)))

    def sides(self, k):
        h = self.here
        dst = self.dst.at[h.y, h.x, self.source(k), h.c]
        src = self.src if k == 0 else dst
        return [
            self.push(src, dst, 3 + k, h.at(x=1 - h.x)),
            self.push(src, dst, 7 + k, h.at(y=1 - h.y)),
        ]

    def across(self, k):
        h, z = self.here, self.source(k)
        top, low = pl.ds(0, self.h), pl.ds(self.h, self.h)
        u, v = self.dst.at[1 - h.y, h.x, z, h.c, top], self.dst.at[h.y, 1 - h.x, z, h.c, low]
        return [
            self.push(u, u, 11 + k, h.at(x=1 - h.x)),
            self.push(v, v, 15 + k, h.at(y=1 - h.y)),
        ]

    def core(self, k, part):
        h, z = self.here, self.source(k)
        y, x = ((h.y, h.x), (h.y, 1 - h.x), (1 - h.y, h.x), (1 - h.y, 1 - h.x))[part]
        dst = self.dst.at[y, x, z, h.c]
        src = self.src if (k == 0 and part == 0) else dst
        return self.push(src, dst, 19 + 4 * k + part, h.at(c=1 - h.c))

    def begin(self):
        self.own().start()
        for k in TURN:
            self.line(k).start()
        for copy in self.sides(0):
            copy.start()
        self.core(0, 0).start()

    def come(self, k):
        self.line(k).wait_recv()
        for copy in self.sides(k):
            copy.start()
        self.core(k, 0).start()

    def side(self, k):
        for copy in self.sides(k):
            copy.wait_recv()
        for copy in self.across(k):
            copy.start()
        self.core(k, 1).start()
        self.core(k, 2).start()

    def cross(self):
        for k in (0,) + TURN:
            for copy in self.across(k):
                copy.wait_recv()
            self.core(k, 3).start()

    def last(self):
        self.own().wait()
        for k in TURN:
            self.line(k).wait_send()
        for k in range(4):
            for copy in self.sides(k) + self.across(k):
                copy.wait_send()
            for part in range(4):
                self.core(k, part).wait()


class GatherBytes:
    def __init__(self, here, src, dst, send, recv, base):
        self.here, self.src, self.dst, self.send, self.recv, self.base = here, src, dst, send, recv, base
        self.w = src.shape[1]
        self.q = src.shape[0] // 4
        self.phases = [self.begin, self.second, self.third, self.fourth, self.last]

    def spot(self, z, c, q=None, n=1):
        cols = pl.ds(pl.multiple_of((z * 2 + c) * self.w, self.w), self.w)
        if q is None:
            return self.dst.at[:, cols]
        return self.dst.at[pl.ds(pl.multiple_of(q * self.q, self.q), n * self.q), cols]

    def source(self, k):
        return lax.rem(self.here.z + 4 - k, 4)

    def push(self, src, dst, i, device):
        return push(src, dst, self.send, self.recv, self.base + i, device)

    def own(self):
        h = self.here
        return pltpu.make_async_copy(self.src, self.spot(h.z, h.c), self.send.at[self.base + 13])

    def line(self, k):
        h = self.here
        q = h.y * 2 + h.x
        src = self.src.at[pl.ds(pl.multiple_of(q * self.q, self.q), self.q)]
        return self.push(src, self.spot(h.z, h.c, q), k - 1, h.at(z=h.over(k)))

    def over_x(self, k):
        h = self.here
        u = self.spot(self.source(k), h.c, h.y * 2 + h.x)
        return self.push(u, u, 2 + k, h.at(x=1 - h.x))

    def over_y(self, k):
        h = self.here
        u = self.spot(self.source(k), h.c, h.y * 2, 2)
        return self.push(u, u, 5 + k, h.at(y=1 - h.y))

    def core(self, k):
        h = self.here
        u = self.spot(self.source(k), h.c)
        src = self.src if k == 0 else u
        return self.push(src, u, 9 + k, h.at(c=1 - h.c))

    def begin(self):
        self.own().start()
        for k in TURN:
            self.line(k).start()
        self.core(0).start()

    def second(self):
        for k in TURN:
            self.line(k).wait_recv()
            self.over_x(k).start()

    def third(self):
        for k in TURN:
            self.over_x(k).wait_recv()
            self.over_y(k).start()

    def fourth(self):
        for k in TURN:
            self.over_y(k).wait_recv()
            self.core(k).start()

    def last(self):
        self.own().wait()
        for k in TURN:
            self.line(k).wait_send()
            self.over_x(k).wait_send()
            self.over_y(k).wait_send()
        for k in range(4):
            self.core(k).wait()


def run_phases(jobs, plans):
    for step in range(max(plan[-1] for plan in plans) + 1):
        for job, plan in zip(jobs, plans):
            for phase, at in zip(job.phases, plan):
                if at == step:
                    phase()


GATHER_PLAN = (0, 2, 4, 6, 8, 10, 12, 14, 16, 18)
NEXT_PLAN = (0, 3, 7, 9, 11, 13, 15, 17, 19, 20)
SMALL_PLAN = (0, 3, 6, 9, 15)
REDUCE_PLAN = (0, 1, 2, 3, 4, 5, 6, 7, 8, 9, 10, 11)
SIDES_PLAN = (8, 10)
ALL_PLAN = (6, 8, 9, 10, 11)
SMALL_REDUCE = (0, 1, 2, 2, 2, 2, 2, 5, 5, 5, 5, 7)


def gather_kernel(xp_ref, dtw_ref, rate_ref, kern_ref, off_ref, bias_ref, skip_ref, in_ref, out_ref,
                  half_ref, full_ref, win_ref, wout_ref, half_s, full_s, send, recv):
    here = Place()
    greet(here.partners())
    layers = xp_ref.shape[0]
    hn, fn = half_s.shape[0] // layers, full_s.shape[0] // layers
    for i in range(layers):
        width = xp_ref.shape[1]
        half_s[i * hn : i * hn + width, :] = xp_ref[i]
        half_s[i * hn + width : (i + 1) * hn, :] = dtw_ref[i]
        parts = [-jnp.exp(rate_ref[i]), kern_ref[i], off_ref[i : i + 1], bias_ref[i : i + 1], skip_ref[i : i + 1]]
        rest = fn - sum(v.shape[0] for v in parts)
        full_s[i * fn : (i + 1) * fn, :] = jnp.concatenate(parts + [jnp.zeros((rest, full_s.shape[1]), f32)], axis=0)
    jobs = [
        GatherBytes(here, half_s, half_ref, send, recv, 0),
        GatherBytes(here, full_s, full_ref, send, recv, GATHER_SEMS),
        Gather(here, in_ref.at[0], win_ref, send, recv, 2 * GATHER_SEMS),
        Gather(here, out_ref.at[0], wout_ref, send, recv, 3 * GATHER_SEMS),
    ]
    run_phases(jobs, [SMALL_PLAN, SMALL_PLAN, GATHER_PLAN, NEXT_PLAN])


def gather_all(xp, dtw, decay, kern, off, bias, skip, in_weight, out_weight, ident):
    layers, width, w = xp.shape
    half = (layers * (width + dtw.shape[1]), w)
    rows = decay.shape[1] + kern.shape[1] + 3
    full = (layers * (rows + -rows % 32), w)
    sems = pltpu.SemaphoreType.DMA((GATHER_SEMS * 4,))
    outs = [jax.ShapeDtypeStruct((half[0], 8 * w), bf16), jax.ShapeDtypeStruct((full[0], 8 * w), f32)]
    outs += [jax.ShapeDtypeStruct((2, 2, 4, 2) + a.shape[1:], bf16) for a in (in_weight, out_weight)]
    half, full, win, wout = pl.pallas_call(
        gather_kernel,
        out_shape=outs,
        in_specs=[INV] * 7 + [ANY] * 2,
        out_specs=[ANY] * 4,
        scratch_shapes=[pltpu.VMEM(half, bf16), pltpu.VMEM(full, f32), sems, sems],
        compiler_params=pltpu.CompilerParams(collective_id=ident, has_side_effects=True, vmem_limit_bytes=VMEM),
    )(xp, dtw, decay, kern, off, bias, skip, in_weight, out_weight)
    return half, full, win.reshape(-1, win.shape[-1]), wout.reshape(-1, wout.shape[-1])


REDUCE_SEMS = 27
FAR = (2, 1, 3, 0)


def reduce_scratch(rows, d):
    def buf(*lead, r=rows):
        return pltpu.VMEM(lead + (r, d), bf16)

    return [buf(2, 2, 4), buf(2, 2, 4), buf(4, r=rows // 2), buf(4, r=rows // 2), buf(4), buf(4), buf(3)]


class Reduce:
    def __init__(self, here, src, out, bufs, send, recv, base):
        self.here, self.src, self.out, self.send, self.recv, self.base = here, src, out, send, recv, base
        self.acc, self.rc, self.da, self.db, self.rx, self.ry, self.rz = bufs
        self.h = src.shape[4] // 2
        h = here
        self.parts = [(1 - h.y, 1 - h.x), (1 - h.y, h.x), (h.y, 1 - h.x), (h.y, h.x)]
        self.phases = (
            [self.begin, self.cross, self.pairs]
            + [functools.partial(self.side, k) for k in FAR]
            + [functools.partial(self.mine, k) for k in FAR]
            + [self.last]
        )

    def push(self, src, dst, i, device):
        return push(src, dst, self.send, self.recv, self.base + i, device)

    def own(self, part):
        y, x = self.parts[part]
        return pltpu.make_async_copy(
            self.src.at[y, x, :, self.here.c], self.acc.at[y, x], self.send.at[self.base + 23 + part]
        )

    def cores(self, part):
        y, x = self.parts[part]
        return self.push(
            self.src.at[y, x, :, 1 - self.here.c], self.rc.at[y, x], 19 + part, self.here.at(c=1 - self.here.c)
        )

    def across(self, k):
        h, z = self.here, self.here.over(k)
        block = self.acc.at[1 - h.y, 1 - h.x, z]
        return [
            self.push(block.at[pl.ds(0, self.h)], self.da.at[z], 3 + k, h.at(x=1 - h.x)),
            self.push(block.at[pl.ds(self.h, self.h)], self.db.at[z], 7 + k, h.at(y=1 - h.y)),
        ]

    def sides(self, k):
        h, z = self.here, self.here.over(k)
        return [
            self.push(self.acc.at[h.y, 1 - h.x, z], self.rx.at[z], 11 + k, h.at(x=1 - h.x)),
            self.push(self.acc.at[1 - h.y, h.x, z], self.ry.at[z], 15 + k, h.at(y=1 - h.y)),
        ]

    def line(self, k):
        h = self.here
        return self.push(self.acc.at[h.y, h.x, h.over(k)], self.rz.at[k - 1], k - 1, h.at(z=h.over(k)))

    def pair(self, part):
        y, x = self.parts[part]
        self.own(part).wait()
        self.cores(part).wait_recv()

        @pl.loop(0, 4)
        def _(z):
            self.acc[y, x, z] = self.acc[y, x, z] + self.rc[y, x, z]

    def begin(self):
        for part in range(4):
            self.cores(part).start()
            self.own(part).start()

    def cross(self):
        self.pair(0)
        for k in FAR:
            for copy in self.across(k):
                copy.start()

    def pairs(self):
        for part in (1, 2, 3):
            self.pair(part)

    def side(self, k):
        h, a, n = self.here, self.acc, self.h
        z = h.over(k)
        for copy in self.across(k):
            copy.wait_recv()
        a[1 - h.y, h.x, z, :n] = a[1 - h.y, h.x, z, :n] + self.da[z]
        a[h.y, 1 - h.x, z, n:] = a[h.y, 1 - h.x, z, n:] + self.db[z]
        for copy in self.sides(k):
            copy.start()

    def mine(self, k):
        h, a = self.here, self.acc
        z = h.over(k)
        for copy in self.sides(k):
            copy.wait_recv()
        a[h.y, h.x, z] = a[h.y, h.x, z] + self.rx[z] + self.ry[z]
        if k:
            self.line(k).start()

    def last(self):
        h = self.here
        total = self.acc[h.y, h.x, h.z].astype(f32)
        for k in (1, 3, 2):
            self.line(k).wait()
            total = total + self.rz[k - 1].astype(f32)
        self.out[...] = total
        for k in range(4):
            for copy in self.across(k) + self.sides(k):
                copy.wait_send()
            self.cores(k).wait_send()


class Reduces:
    def __init__(self, srcs, outs, scratch):
        per = len(reduce_scratch(16, 128))
        self.here = Place()
        self.jobs = [
            Reduce(self.here, src, out, scratch[per * i : per * (i + 1)], scratch[-2], scratch[-1], REDUCE_SEMS * i)
            for i, (src, out) in enumerate(zip(srcs, outs))
        ]

        self.phases = [functools.partial(self.run, i) for i in range(12)]

    def run(self, phase):
        for job in self.jobs:
            job.phases[phase]()


def reduce_parts(arrays):
    arrays = [a.reshape(2, 2, 4, 2, a.shape[0] // 32, a.shape[1]) for a in arrays]
    scratch = []
    for a in arrays:
        scratch += reduce_scratch(*a.shape[4:])
    if arrays:
        sems = pltpu.SemaphoreType.DMA((REDUCE_SEMS * len(arrays),))
        scratch += [sems, sems]
    return arrays, [jax.ShapeDtypeStruct(a.shape[4:], f32) for a in arrays], scratch


def beside(work, block, steps):
    for step in sorted(set(steps)):

        @pl.when(block == step)
        def _(step=step):
            for phase, at in enumerate(steps):
                if at == step:
                    work.phases[phase]()


SIDE_SEMS = 4


class Sides:
    def __init__(self, here, src, dst, send, recv, base):
        self.here, self.src, self.dst, self.send, self.recv, self.base = here, src, dst, send, recv, base
        self.phases = [self.begin, self.last]

    def copies(self):
        h = self.here
        dst = self.dst.at[h.y, h.x]
        to = [h.at(x=1 - h.x), h.at(y=1 - h.y), h.at(x=1 - h.x, y=1 - h.y)]
        return [push(self.src, dst, self.send, self.recv, self.base + i, p) for i, p in enumerate(to)]

    def begin(self):
        for copy in self.copies():
            copy.start()
        self.dst[self.here.y, self.here.x] = self.src[...]

    def last(self):
        for copy in self.copies():
            copy.wait()


ALL_SEMS = 6


class AllSum:
    def __init__(self, here, src, out, got, send, recv, base):
        self.here, self.src, self.out, self.got, self.send, self.recv, self.base = here, src, out, got, send, recv, base
        self.phases = [self.begin, functools.partial(self.turn, 0), functools.partial(self.turn, 1), self.along, self.last]

    def copy(self, i):
        h = self.here
        p = h.partners()[i]
        return push(self.got.at[6 + min(i, 3)], self.got.at[i], self.send, self.recv, self.base + i, p)

    def begin(self):
        self.got[6] = self.src[...]
        self.copy(0).start()

    def turn(self, i):
        self.copy(i).wait()
        self.got[7 + i] = self.got[6 + i] + self.got[i]
        self.copy(i + 1).start()

    def along(self):
        self.copy(2).wait()
        self.got[9] = self.got[8] + self.got[2]
        for i in (3, 4, 5):
            self.copy(i).start()

    def last(self):
        for i in (3, 4, 5):
            self.copy(i).wait()
        self.out[...] = self.got[9] + self.got[3] + self.got[4] + self.got[5]


def finish_kernel(cuts, small_ref, big_ref, w_ref, mixed_ref, before_ref, flow_ref, gain_ref, upper_ref,
                  flow_out, in_out, gain_out, *refs):
    outs, refs = refs[: len(cuts)], refs[len(cuts) :]
    per = len(reduce_scratch(16, 128))
    one, two, refs = refs[:per], refs[per : 2 * per], refs[2 * per :]
    w_s, gn_s, mine_s, plane_s, gains_s, got_s, send, recv, wsem = refs
    here = Place()
    greet(here.partners() + [here.at(x=1 - here.x, y=1 - here.y)])
    load = pltpu.make_async_copy(w_ref, w_s, wsem)
    load.start()
    base = 2 * REDUCE_SEMS
    small = Reduce(here, small_ref, mine_s, one, send, recv, 0)
    big = Reduce(here, big_ref, in_out, two, send, recv, REDUCE_SEMS)
    gains = AllSum(here, gains_s, gain_out, got_s, send, recv, base)
    plane = Sides(here, mine_s, plane_s, send, recv, base + ALL_SEMS)

    class Norm:
        def run(self):
            load.wait()
            depth = 512
            gn_s[...] = jnp.zeros_like(gn_s)

            @pl.loop(0, mixed_ref.shape[1] // depth)
            def _(k):
                at = pl.ds(pl.multiple_of(k * depth, depth), depth)
                gn_s[...] += dot(mixed_ref[:, at], w_s[at, :])

            gn, before, gain = gn_s[...], before_ref[...].astype(f32), gain_ref[...]
            inv = lax.rsqrt(jnp.mean(before * before, axis=1, keepdims=True) + norm_eps)
            scaled = before * inv
            gs = gn * gain
            flow_out[...] = flow_ref[...] + inv * (gs - scaled * jnp.mean(gs * scaled, axis=1, keepdims=True))
            gains_s[0:1, :] = jnp.sum(gn * scaled, axis=0, keepdims=True)
            gains_s[1:, :] = upper_ref[...]

        def __init__(self):
            self.phases = [self.run]

    run_phases(
        [small, big, Norm(), gains, plane],
        [SMALL_REDUCE, REDUCE_PLAN, (6,), ALL_PLAN, SIDES_PLAN],
    )
    rows, d = mine_s.shape
    layers = upper_ref.shape[0] + 1
    whole_sum = plane_s[...].reshape(4 * rows, d)
    per_layer = 4 * rows // layers
    for layer in range(layers):
        at = layer * per_layer
        for cut, out in zip(cuts, outs):
            v = whole_sum[at : at + cut]
            if len(out.shape) == 2:
                out[layer : layer + 1, :] = v
            else:
                out[layer] = v
            at += cut


def finish(packed, grad_in, in_full, mixed, before, flowing, gain, upper, cuts, ident):
    arrays = [a.reshape(2, 2, 4, 2, a.shape[0] // 32, a.shape[1]) for a in (packed, grad_in)]
    (rows, w), d = arrays[0].shape[4:], before.shape[1]
    layers = upper.shape[0] + 1
    outs = [jax.ShapeDtypeStruct(before.shape, f32), jax.ShapeDtypeStruct(arrays[1].shape[4:], f32),
            jax.ShapeDtypeStruct((layers, d), f32)]
    outs += [jax.ShapeDtypeStruct((layers, cut, w) if cut > 1 else (layers, w), f32) for cut in cuts]
    scratch = reduce_scratch(rows, w) + reduce_scratch(*arrays[1].shape[4:])
    scratch += [pltpu.VMEM(in_full.shape, bf16), pltpu.VMEM(before.shape, f32), pltpu.VMEM((rows, w), f32),
                pltpu.VMEM((2, 2, rows, w), f32), pltpu.VMEM((layers, d), f32), pltpu.VMEM((10, layers, d), f32)]
    sems = pltpu.SemaphoreType.DMA((REDUCE_SEMS * 2 + ALL_SEMS + SIDE_SEMS,))
    return pl.pallas_call(
        functools.partial(finish_kernel, cuts),
        out_shape=outs,
        in_specs=[ANY] * 3 + [INV] * 5,
        out_specs=[INV] * len(outs),
        scratch_shapes=scratch + [sems, sems, pltpu.SemaphoreType.DMA],
        compiler_params=pltpu.CompilerParams(collective_id=ident, has_side_effects=True, vmem_limit_bytes=VMEM),
    )(*arrays, in_full, mixed, before, flowing, gain, upper)


EXCHANGE_SEMS = 10


def exchange_scratch(rows, sn, c):
    h = c // 2
    sems = pltpu.SemaphoreType.DMA((EXCHANGE_SEMS,))
    return [pltpu.VMEM((sn, h), bf16)] * 4 + [
        pltpu.VMEM((rows, h), f32), pltpu.VMEM((1, rows, h), f32), pltpu.VMEM((4, sn, h), bf16),
        pltpu.VMEM((4, rows, h), f32), sems, sems,
    ]


def exchange(here, backward, rows, end_ref, sum_ref, rate_ref, out_ref, scratch):
    sent, back, got, late, gsum, msum, line, lsum, send, recv = scratch
    half = end_ref.shape[1] // 2
    mine = pl.ds(pl.multiple_of(here.c * half, half), half)
    theirs = pl.ds(pl.multiple_of((1 - here.c) * half, half), half)
    other = here.at(c=1 - here.c)
    sent[...] = end_ref[:, theirs].astype(bf16)
    msum[0] = sum_ref[:, theirs]
    one = [push(sent, got, send, recv, 0, other), push(msum.at[0], gsum, send, recv, 1, other)]
    for copy in one:
        copy.start()
    rate = rate_ref[:, mine]

    def fade(total):
        return jnp.concatenate([jnp.exp(rate * total[s : s + 1]) for s in range(rows)], axis=0)

    for copy in one:
        copy.wait()
    e_me, d_me = end_ref[:, mine], sum_ref[:, mine]
    e_it, d_it = got[...].astype(f32), gsum[...]
    first = here.c == 0
    e0, e1 = jnp.where(first, e_me, e_it), jnp.where(first, e_it, e_me)
    d0, d1 = jnp.where(first, d_me, d_it), jnp.where(first, d_it, d_me)
    chip = e0 + fade(d0) * e1 if backward else fade(d1) * e0 + e1
    line[3] = chip.astype(bf16)
    lsum[3] = d0 + d1
    two = []
    for k in (1, 2, 3):
        two.append(push(line.at[3], line.at[k - 1], send, recv, 2 + 2 * k, here.at(z=here.over(k))))
        two.append(push(lsum.at[3], lsum.at[k - 1], send, recv, 3 + 2 * k, here.at(z=here.over(k))))
    for copy in two:
        copy.start()
    for copy in two:
        copy.wait()
    state = jnp.zeros_like(chip)
    for k in (1, 2, 3) if backward else (3, 2, 1):
        at = lax.rem(here.z + 4 - k, 4)
        e, d = line[k - 1].astype(f32), lsum[k - 1]
        use = at > here.z if backward else at < here.z
        state = jnp.where(use, fade(d) * state + e, state)
    if backward:
        s1, s0 = state, e1 + fade(d1) * state
    else:
        s0, s1 = state, fade(d0) * state + e0
    out_ref[:, mine] = jnp.where(first, s0, s1)
    back[...] = jnp.where(first, s1, s0).astype(bf16)
    three = push(back, late, send, recv, 2, other)
    three.start()
    three.wait()
    out_ref[:, theirs] = late[...].astype(f32)


def carried_in(ends, sums, rate, axis, backward):
    n = lax.axis_size(axis)
    rows = sums.shape[0]
    ns = rate.shape[0]

    def fade(total):
        return jnp.exp(total[:, None, :] * rate[None])

    def moved(v, shift):
        if backward:
            pairs = [(i, i - shift) for i in range(shift, n)]
        else:
            pairs = [(i, i + shift) for i in range(n - shift)]
        return lax.ppermute(v, axis, pairs)

    def shifted(e, s, shift):
        return moved(e.astype(bf16), shift).astype(f32), moved(s, shift)

    ends = ends.reshape(rows, ns, -1)
    ends, sums = shifted(ends, sums, 1)
    shift = 1
    while shift < n - 1:
        e, s = shifted(ends, sums, shift)
        ends = fade(sums) * e + ends
        sums = sums + s
        shift *= 2
    return ends.reshape(rows * ns, -1)


def body(
    tokens, boundaries, norm_gain, in_weight, out_weight, conv_weight, conv_bias, xproj_weight,
    dtproj_weight, dt_bias, decay_log, skip_gain, cotangent,
):
    rows, length, d = tokens.shape
    layers = norm_gain.shape[0]
    both = ("rows", "bytes")
    n = rows * length
    place = lax.axis_index("bytes") * length + jnp.arange(length, dtype=jnp.int32)
    reached = boundaries[:, None, :] <= place[None, :, None]
    starts = jnp.max(jnp.where(reached, boundaries[:, None, :], 0), axis=2)
    renewed = jnp.any(boundaries[:, None, :] == place[None, :, None], axis=2)
    kill = jnp.broadcast_to(jnp.where(renewed, KILL, 0.0).reshape(n, 1), (n, 128)).astype(f32)
    taps = conv_weight.shape[1]
    masks = jnp.stack(
        [
            jnp.broadcast_to((place[None, :] - lag >= starts).astype(f32).reshape(n, 1), (n, 128))
            for lag in range(1, taps)
        ]
    )
    fast = (lax.axis_size("rows"), lax.axis_size("bytes")) == (4, 8)
    if fast:
        half, full, first_in, first_out = gather_all(
            xproj_weight.transpose(0, 2, 1), dtproj_weight, decay_log, conv_weight, conv_bias, dt_bias, skip_gain, in_weight, out_weight, 1
        )
    else:
        half = jnp.concatenate([xproj_weight.transpose(0, 2, 1), dtproj_weight], axis=1)
        full = jnp.concatenate(
            [-jnp.exp(decay_log), conv_weight, conv_bias[:, None], dt_bias[:, None], skip_gain[:, None]], axis=1
        )
        half = lax.all_gather(half, "bytes", axis=2, tiled=True)
        full = lax.all_gather(full, "bytes", axis=2, tiled=True)
    ns = decay_log.shape[1]
    rank = dtproj_weight.shape[1]
    width = xproj_weight.shape[2]
    channels = full.shape[-1]
    mixer = Mixer(layers, rows, length, channels, ns, rank, taps)
    params = []
    for i in range(0 if fast else layers):
        rest = full[i, ns + taps :]
        params.append(
            dict(
                xproj=half[i, :width], dtproj=half[i, width:], conv_w=full[i, ns : ns + taps], conv_b=rest[:1],
                dt_b=rest[1:2], skip=rest[2:3], rate=full[i, :ns],
            )
        )
    if fast:
        in_fulls, out_fulls = {0: first_in}, {0: first_out}
    else:
        in_fulls = {i: lax.all_gather(in_weight[i], both, axis=0, tiled=True) for i in range(layers)}
        out_fulls = {i: lax.all_gather(out_weight[i], both, axis=0, tiled=True) for i in range(layers)}
    size = lax.axis_size("bytes")
    ahead = [(i, i + 1) for i in range(size - 1)]
    behind = [(i + 1, i) for i in range(size - 1)]
    current = tokens.astype(f32).reshape(n, d)
    saved = []
    for i in range(layers):
        p = None if fast else params[i]
        if fast:
            (normed, x, z, halo, act, rank_t, bb, cc, delta, total, y, gated, keep), whole_w = mixer.forward(
                i, current if i else tokens.reshape(n, d), norm_gain[i][None], in_fulls[i], half, full, masks, kill,
                ([(out_weight, i)] if i else []) + [(in_weight, j) for j in range(i + 1, min(i + 2, layers))], 2 + i,
            )
            m = dict(rank_t=rank_t, bb=bb, cc=cc)
            if i:
                out_fulls[i] = whole_w[0]
            if i + 1 < layers:
                in_fulls[i + 1] = whole_w[-1]
        else:
            normed = (
                current * lax.rsqrt(jnp.mean(current * current, axis=-1, keepdims=True) + norm_eps) * norm_gain[i]
            ).astype(bf16)
            projected = dot_nt(normed, in_fulls[i])
            tail = projected.reshape(rows, length, -1)[:, length - 8 :, :channels].astype(bf16)
            halo = lax.ppermute(tail, "bytes", ahead).reshape(8 * rows, channels)
            act, m = mixer.conv(projected, halo, p, masks)
            delta, end, total = mixer.ends(act, m, p, kill)
            start = carried_in(end, total, p["rate"], "bytes", False)
            y, gated, keep = mixer.scan(act, delta, projected, m, p, kill, start)
            x = z = projected
        saved.append((current, normed, x, z, halo, act, m, delta, total, y, gated, keep))
        current = current + dot(gated, out_fulls[i])
    flowing = cotangent.astype(f32).reshape(n, d)
    big, small, gains = [], [], []
    waiting, ready = [], []
    for i in reversed(range(layers)):
        p = None if fast else params[i]
        in_full, out_full = in_fulls[i], out_fulls[i]
        before, normed, x, z, halo, act, m, delta, total, y, gated, keep = saved[i]
        down = flowing.astype(bf16)
        grad_out = lax.dot_general(gated, down, (((0,), (0,)), ((), ())), preferred_element_type=f32).astype(bf16)
        gg = dot_nt(down, out_full)
        if fast:
            waiting.append(grad_out)
            (mixed, pieces), done = mixer.backward(
                i, gg, x, z, halo, y, act, delta, total, m, half, full, masks, kill, keep, waiting, 10 + i
            )
            ready += done
        else:
            gy, gz, gend = mixer.back_ends(gg, z, y, delta, m, p, kill)
            gstart = carried_in(gend, total, p["rate"], "bytes", True)
            gact, gproj, gproj_t, gdtw, gbias, grate, gskip = mixer.back(act, delta, gy, m, p, kill, keep, gstart)
            gx, edge, gxp, gkern, goff = mixer.conv_back(x, halo, p, masks, act, gact, gproj, gproj_t)
            late = lax.ppermute(edge.astype(bf16), "bytes", behind).astype(f32).reshape(rows, 8, channels)
            gx = (
                (gx.reshape(rows, length, channels) + jnp.pad(late, ((0, 0), (length - 8, 0), (0, 0))))
                .reshape(n, channels)
                .astype(bf16)
            )
            mixed = jnp.concatenate([gx, gz], axis=1)
            pieces = jnp.concatenate([gxp, gdtw, grate, gkern, goff, gbias, gskip], axis=0)
        grad_in = lax.dot_general(mixed, normed, (((0,), (0,)), ((), ())), preferred_element_type=f32).astype(bf16)
        small.append(pieces)
        waiting = [grad_in]
        if fast and i == 0:
            break
        gn = dot(mixed, in_full)
        inv = lax.rsqrt(jnp.mean(before * before, axis=-1, keepdims=True) + norm_eps)
        scaled = before * inv
        gains.append(jnp.sum(gn * scaled, axis=0))
        gs = gn * norm_gain[i]
        flowing = flowing + inv * (gs - scaled * jnp.mean(gs * scaled, axis=-1, keepdims=True))
        if not fast:
            big.append([lax.psum_scatter(g, both, scatter_dimension=0, tiled=True).astype(f32) for g in (grad_in, grad_out)])
    cuts = [width, rank, ns, taps, 1, 1, 1]
    if fast:
        packed = jnp.stack(small[::-1])
        packed = packed.reshape(4, layers * packed.shape[1] // 4, size, channels // size).transpose(0, 2, 1, 3)
        flowing, last_in, gain_total, *parts = finish(
            packed.reshape(-1, channels // size), grad_in, in_full, mixed, tokens.reshape(n, d), flowing, norm_gain[0][None],
            jnp.stack(gains[::-1]), cuts, 9,
        )
        ready.append(last_in)
        big = [(ready[2 * i + 1], ready[2 * i]) for i in range(layers)]
    else:
        packed = jnp.stack(small[::-1]).astype(bf16)
        packed = lax.psum_scatter(packed, "bytes", scatter_dimension=2, tiled=True)
        packed = lax.psum(packed, "rows").astype(f32)
        gain_total = lax.psum(jnp.stack(gains[::-1]), both)
        parts, at = [], 0
        for cut in cuts:
            parts.append(packed[:, at] if cut == 1 else packed[:, at : at + cut])
            at += cut
    big = big[::-1]
    return (
        current.reshape(rows, length, d),
        flowing.reshape(rows, length, d),
        gain_total,
        jnp.stack([b[0] for b in big]),
        jnp.stack([b[1] for b in big]),
        parts[3],
        parts[4],
        parts[0].transpose(0, 2, 1),
        parts[1],
        parts[5],
        parts[2],
        parts[6],
    )


def solution(mesh):
    split = P("rows", "bytes", None)
    shared = P(None, ("rows", "bytes"), None)
    in_specs = (
        split, P("rows", None), P(), shared, shared, P(None, None, "bytes"), P(None, "bytes"),
        P(None, "bytes", None), P(None, None, "bytes"), P(None, "bytes"), P(None, None, "bytes"),
        P(None, "bytes"), split,
    )
    out_specs = (
        split, split, P(), shared, shared, P(None, None, "bytes"), P(None, "bytes"), P(None, "bytes", None),
        P(None, None, "bytes"), P(None, "bytes"), P(None, None, "bytes"), P(None, "bytes"),
    )
    return jax.shard_map(body, mesh=mesh, in_specs=in_specs, out_specs=out_specs, check_vma=False)
```

```python
import functools

import jax
import jax.numpy as jnp
from jax import lax
from jax.experimental import pallas as pl
from jax.experimental.pallas import tpu as pltpu
from jax.sharding import PartitionSpec as P

norm_eps = 1e-05
f32 = jnp.float32
bf16 = jnp.bfloat16
STEPS = 8
CB = 256
CB_ENDS = 512
CB_SCAN = 512
CB_BACK = 512
KILL = 1e30
LOG2E = 1.4426950408889634
VMEM = 58 * 2**20
FORWARD_ONE = (8, 15, 16, 17, 18, 18, 19, 20, 21)
FORWARD_EARLY = (8, 16, 17, 19, 20, 20, 20, 22, 23)
BACKWARD_STEPS = (0, 2, 4, 4, 4, 4, 4, 5, 6, 7, 8)

NT = (((1,), (1,)), ((), ()))


def dot(a, b):
    return jnp.dot(a, b, preferred_element_type=f32)


def dot_nt(a, b):
    return lax.dot_general(a, b, NT, preferred_element_type=f32)


def halves(v):
    high = v.astype(bf16)
    return high, (v - high.astype(f32)).astype(bf16)


def wide(v, width):
    return jnp.concatenate([v] * (width // v.shape[1]), axis=1)


def sigmoid(v):
    return 1.0 / (1.0 + jnp.exp(-v))


def conv_sum(x, halo, kernel, offset, masks, rows):
    length = x.shape[0] // rows
    taps = kernel.shape[0]
    outs = []
    for s in range(rows):
        ext = jnp.concatenate([halo[8 * s : 8 * s + 8], x[s * length : (s + 1) * length]], axis=0)
        total = offset + kernel[taps - 1 : taps] * ext[8:]
        for lag in range(1, taps):
            moved = pltpu.roll(ext, lag, 0)[8:]
            m = masks[lag - 1][s * length : (s + 1) * length]
            total = total + kernel[taps - 1 - lag : taps - lag] * moved * m
        outs.append(total)
    return jnp.concatenate(outs, axis=0)


class Packed:
    def __init__(self, rank, ns, taps):
        self.rank, self.ns, self.taps = rank, ns, taps
        self.width = rank + 2 * ns

    def rate(self, ref):
        return ref.at[0 : self.ns]

    def kernel(self, ref):
        return ref.at[self.ns : self.ns + self.taps]

    def row(self, ref, i):
        return ref.at[self.ns + self.taps + i : self.ns + self.taps + i + 1]

    def offset(self, ref):
        return self.row(ref, 0)

    def bias(self, ref):
        return self.row(ref, 1)

    def skip(self, ref):
        return self.row(ref, 2)

    def xproj(self, ref):
        return ref.at[0 : self.width]

    def dtproj(self, ref):
        return ref.at[self.width : self.width + self.rank]


def maps_part(rows, rank, ns, proj, rank2_ref, rank_t_ref, bb_ref, cc_ref, cd_ref):
    tokens = proj.shape[0]
    high, low = halves(proj[:, :rank])
    rank2_ref[...] = jnp.concatenate([high, low], axis=1)
    turned = proj.T
    rank_t_ref[...] = turned[:rank].astype(bf16)
    per = tokens // rows // STEPS
    for s in range(rows):
        for k in range(per):
            for t in range(STEPS):
                tok = (s * per + k) * STEPS + t
                at = ((k * rows + s) * STEPS + t) * ns
                bb_ref[at : at + ns, :] = jnp.broadcast_to(turned[rank : rank + ns, tok : tok + 1], (ns, 128))
                cc_ref[at : at + ns, :] = jnp.broadcast_to(turned[rank + ns :, tok : tok + 1], (ns, 128))
    inner = cd_ref.shape[-1]
    tile = (
        lax.broadcasted_iota(jnp.int32, (ns, inner), 0) == lax.broadcasted_iota(jnp.int32, (ns, inner), 1) % ns
    ).astype(bf16)
    spread = dot(proj[:, rank + ns :].astype(bf16), tile)
    tok = lax.broadcasted_iota(jnp.int32, (tokens, inner), 0)
    own = (tok // (tokens // rows)) * STEPS + tok % STEPS
    cd = jnp.where(own == lax.broadcasted_iota(jnp.int32, (tokens, inner), 1) // ns, spread, 0.0)
    cd_ref[...] = cd.reshape(cd_ref.shape)


def conv_part(rows, x, halo, kern_ref, off_ref, mask_ref, xp_ref, proj_s):
    cb = x.shape[1]
    masks = [wide(mask_ref[i], cb) for i in range(mask_ref.shape[0])]
    pre = conv_sum(x, halo, kern_ref[...], off_ref[...], masks, rows)
    act = pre * sigmoid(pre)
    high, low = halves(act)
    weight = xp_ref[...]
    proj_s[...] += dot_nt(high, weight) + dot_nt(low, weight)
    return act


def conv_kernel(rows, sizes, x_ref, halo_ref, kern_ref, off_ref, mask_ref, xp_ref,
                act_ref, rank2_ref, rank_t_ref, bb_ref, cc_ref, cd_ref, proj_s):
    block = pl.program_id(0)

    @pl.when(block == 0)
    def _():
        proj_s[...] = jnp.zeros_like(proj_s)

    act_ref[...] = conv_part(
        rows, x_ref[...].astype(bf16).astype(f32), halo_ref[...].astype(f32), kern_ref, off_ref, mask_ref, xp_ref, proj_s
    )

    @pl.when(block == pl.num_programs(0) - 1)
    def _():
        maps_part(rows, *sizes, proj_s[...], rank2_ref, rank_t_ref, bb_ref, cc_ref, cd_ref)


def step_sizes(rank2_ref, dtw_ref, bias_ref):
    weight = dtw_ref[...]
    pre = dot(rank2_ref[...], jnp.concatenate([weight, weight], axis=0)) + bias_ref[...]
    return jnp.maximum(pre, 0.0) + jnp.log1p(jnp.exp(-jnp.abs(pre)))


def chunked(v):
    return v.reshape(v.shape[0] // STEPS, STEPS, v.shape[1])


def tile_rows(ref, k, at, ns, inner, cb):
    v = ref[pl.ds(pl.multiple_of(k * inner, inner) + at, ns), :]
    return jnp.concatenate([v] * (cb // v.shape[1]), axis=1)


def lane_sum(v):
    out = v[:, :128]
    for i in range(1, v.shape[1] // 128):
        out = out + v[:, 128 * i : 128 * (i + 1)]
    return out


def ends_part(rows, act, rank2_ref, dtw_ref, bias_ref, kill_ref, rate_ref, bb_ref, eff_s, u_s):
    delta = step_sizes(rank2_ref, dtw_ref, bias_ref)
    cb = delta.shape[1]
    eff = delta + wide(kill_ref[...], cb)
    eff_s[...] = chunked(eff)
    u_s[...] = chunked(delta * act)
    length = eff.shape[0] // rows
    sums = jnp.concatenate(
        [jnp.sum(eff[s * length : (s + 1) * length], axis=0, keepdims=True) for s in range(rows)], axis=0
    )
    rate = rate_ref[...] * LOG2E
    ns = rate.shape[0]
    chunks = length // STEPS
    inner = rows * STEPS * ns

    def chunk(k, state):
        state = list(state)
        for t in range(STEPS):
            for s in range(rows):
                fade = jnp.exp2(rate * eff_s[s * chunks + k, t : t + 1, :])
                drive = u_s[s * chunks + k, t : t + 1, :] * tile_rows(bb_ref, k, (s * STEPS + t) * ns, ns, inner, cb)
                state[s] = fade * state[s] + drive
        return tuple(state)

    zero = jnp.zeros((ns, cb), f32)
    state = lax.fori_loop(0, chunks, chunk, (zero,) * rows)
    return delta, sums, jnp.concatenate(state, axis=0)


def scan_part(rows, delta, act, z, kill_ref, rate_ref, skip_ref, bb_ref, cd_ref, start,
              y_ref, gated_ref, keep_ref, eff_s, u_s, sa, sb, y_s):
    cb = delta.shape[1]
    eff_s[...] = chunked(delta + wide(kill_ref[...], cb))
    u_s[...] = chunked(delta * act)
    rate = rate_ref[...] * LOG2E
    ns = rate.shape[0]
    length = delta.shape[0] // rows
    chunks = length // STEPS
    inner = rows * STEPS * ns

    def scan(k, state, held):
        state = list(state)
        for s in range(rows):
            keep_ref[k, s * ns : (s + 1) * ns, :] = state[s]
        for t in range(STEPS):
            for s in range(rows):
                at = (s * STEPS + t) * ns
                fade = jnp.exp2(rate * eff_s[s * chunks + k, t : t + 1, :])
                drive = u_s[s * chunks + k, t : t + 1, :] * tile_rows(bb_ref, k, at, ns, inner, cb)
                state[s] = fade * state[s] + drive
                held[at : at + ns, :] = state[s].astype(bf16)
        return tuple(state)

    def leave(k, held):
        left = jnp.concatenate([cd_ref[s * chunks + k] for s in range(rows)], axis=0).astype(bf16)
        y = dot(left, held[...])
        for s in range(rows):
            y_s[s * chunks + k] = y[s * STEPS : (s + 1) * STEPS]

    sb[...] = jnp.zeros_like(sb)

    def two(i, state):
        k = 2 * i
        leave(jnp.maximum(k - 1, 0), sb)
        state = scan(k, state, sa)
        leave(k, sa)
        return scan(k + 1, state, sb)

    lax.fori_loop(0, chunks // 2, two, tuple(start[s * ns : (s + 1) * ns] for s in range(rows)))
    leave(chunks - 1, sb)
    y = (y_s[...].reshape(delta.shape) + skip_ref[...] * act).astype(bf16)
    y_ref[...] = y
    gated_ref[...] = (y.astype(f32) * (z * sigmoid(z))).astype(bf16)


def forward_kernel(rows, layer_of, sizes, *refs):
    n = len(layer_of)
    rank, ns, taps, narrow, blocks = sizes
    (h_ref, gain_ref, wx_ref, wz_ref, full_n, half_n, mask_ref, half_w, kill_ref, full_w, full_ref), refs = refs[:11], refs[11:]
    cut = Packed(rank, ns, taps)
    kern_ref, off_ref, xp_ref = cut.kernel(full_n), cut.offset(full_n), cut.xproj(half_n)
    dtw_ref, bias_ref, rate_ref = cut.dtproj(half_w), cut.bias(full_w), cut.rate(full_w)
    skip_ref, rates_ref = cut.skip(full_w), cut.rate(full_ref)
    srcs, refs = refs[:n], refs[n:]
    (normed_ref, x_ref, z_ref, halo_ref, act_ref, rank_t_ref, bb_ref, cc_ref, delta_ref, sum_ref, y_ref, gated_ref,
     keep_ref), refs = refs[:13], refs[13:]
    dsts, refs = refs[:n], refs[n:]
    (proj_s, x_s, tail_s, halo_s, act_s, z_s, rank2_s, cd_s, eff_s, u_s, sa, sb, y_s, delta_s, end_s, start_s,
     sum_s), refs = refs[:17], refs[17:]
    exch, (send, recv, hsend, hrecv) = refs[:20], refs[20:]
    here = Place()
    block = pl.program_id(0)
    front = 2 * narrow
    nb, cb = x_s.shape[2], eff_s.shape[2]
    per = cb // nb

    def halo(j):
        return push(tail_s.at[j], halo_s.at[j], hsend, hrecv, j, here.ring(1))

    @pl.when(block == 0)
    def _():
        greet(here.partners() + [here.ring(1), here.ring(-1)])
        proj_s[...] = jnp.zeros_like(proj_s)
        h = h_ref[...].astype(f32)
        normed_ref[...] = (
            h * lax.rsqrt(jnp.mean(h * h, axis=1, keepdims=True) + norm_eps) * gain_ref[...]
        ).astype(bf16)

    exchanges(here, False, rows, end_s, sum_s, rates_ref, start_s, exch, block, front + blocks // 2)
    jobs = [
        Gather(here, src.at[layer], dst, send, recv, GATHER_SEMS * i)
        for i, (src, dst, layer) in enumerate(zip(srcs, dsts, layer_of))
    ]
    plans = [FORWARD_ONE if src.shape[1] * 32 < h_ref.shape[1] * 4 else FORWARD_EARLY for src in srcs]
    for job, plan in zip(jobs, plans):
        beside(job, block, plan)

    @pl.when(block < narrow)
    def _():
        normed = normed_ref[...]
        x = dot_nt(normed, wx_ref[...])
        z = dot_nt(normed, wz_ref[...])
        z_ref[...] = z
        z_s[block // per, :, pl.ds(pl.multiple_of(lax.rem(block, per) * nb, nb), nb)] = z
        x16 = x.astype(bf16)
        x_ref[...] = x16
        x_s[block] = x16
        length = x.shape[0] // rows
        tail_s[block] = jnp.concatenate([x[(s + 1) * length - 8 : (s + 1) * length] for s in range(rows)], axis=0).astype(bf16)
        halo(block).start()

    @pl.when((block >= narrow) & (block < front))
    def _():
        j = block - narrow
        halo(j).wait()
        before = halo_s[j]
        halo_ref[...] = before
        act = conv_part(
            rows, x_s[j].astype(f32), before.astype(f32), kern_ref, off_ref, mask_ref, xp_ref, proj_s
        )
        act_ref[...] = act
        act_s[j // per, :, pl.ds(pl.multiple_of(lax.rem(j, per) * nb, nb), nb)] = act

    @pl.when(block == front - 1)
    def _():
        maps_part(rows, rank, ns, proj_s[...], rank2_s, rank_t_ref, bb_ref, cc_ref, cd_s)

    @pl.when((block >= front) & (block < front + blocks))
    def _():
        j = block - front
        delta, sums, ends = ends_part(
            rows, act_s[j], rank2_s, dtw_ref, bias_ref, kill_ref, rate_ref, bb_ref, eff_s, u_s
        )
        cols = pl.ds(pl.multiple_of(j * cb, cb), cb)
        delta_ref[...] = delta
        delta_s[j] = delta
        sum_s[:, cols] = sums
        end_s[:, cols] = ends

    @pl.when(block == front + blocks - 1)
    def _():
        sum_ref[...] = sum_s[...]

    @pl.when(block >= front + blocks)
    def _():
        j = block - front - blocks
        cols = pl.ds(pl.multiple_of(j * cb, cb), cb)
        scan_part(rows, delta_s[j], act_s[j], z_s[j], kill_ref, rate_ref, skip_ref, bb_ref, cd_s,
                  start_s[:, cols], y_ref, gated_ref, keep_ref, eff_s, u_s, sa, sb, y_s)

    @pl.when(block == pl.num_programs(0) - 1)
    def _():
        for job, plan in reversed(list(zip(jobs, plans))):
            for phase in job.phases[len(plan) :]:
                phase()


def back_ends_part(rows, gg_ref, z_ref, y_ref, delta_ref, kill_ref, rate_ref, cc_ref, gz_ref, eff_s, gy_s):
    z = z_ref[...]
    gg = gg_ref[...]
    sig = sigmoid(z)
    gy = (gg * z * sig).astype(bf16)
    gz_ref[...] = (gg * y_ref[...].astype(f32) * sig * (1.0 + z * (1.0 - sig))).astype(bf16)
    cb = z.shape[1]
    eff_s[...] = chunked(delta_ref[...] + wide(kill_ref[...], cb))
    gy_s[...] = chunked(gy.astype(f32))
    rate = rate_ref[...] * LOG2E
    ns = rate.shape[0]
    length = z.shape[0] // rows
    chunks = length // STEPS
    inner = rows * STEPS * ns

    def chunk(i, flow):
        k = chunks - 1 - i
        flow = list(flow)
        for t in reversed(range(STEPS)):
            for s in range(rows):
                fade = jnp.exp2(rate * eff_s[s * chunks + k, t : t + 1, :])
                push = gy_s[s * chunks + k, t : t + 1, :] * tile_rows(cc_ref, k, (s * STEPS + t) * ns, ns, inner, cb)
                flow[s] = fade * (flow[s] + push)
        return tuple(flow)

    zero = jnp.zeros((ns, cb), f32)
    flow = lax.fori_loop(0, chunks, chunk, (zero,) * rows)
    return gy, jnp.concatenate(flow, axis=0)


def back_part(rows, act_ref, delta_ref, gy, kill_ref, rate_ref, skip_ref, dtw_ref, rank_t_ref, bb_ref, cc_ref, keep_ref,
              start, gact_ref, gdtw_ref, gbias_ref, grate_ref, gskip_ref,
              eff_s, u_s, gy_s, fade_s, held_s, sa, sb, gu_s, gd_s, gb_s, gc_s, grank_s):
    delta = delta_ref[...]
    act = act_ref[...]
    cb = delta.shape[1]
    eff_s[...] = chunked(delta + wide(kill_ref[...], cb))
    u_s[...] = chunked(delta * act)
    gy_s[...] = chunked(gy)
    rate_n = rate_ref[...]
    rate = rate_n * LOG2E
    ns = rate.shape[0]
    length = delta.shape[0] // rows
    chunks = length // STEPS
    pairs = rows * STEPS
    inner = pairs * ns
    half = ns // 2
    side = pairs * half
    pick = (
        lax.broadcasted_iota(jnp.int32, (2 * pairs, 2 * side), 0)
        == lax.broadcasted_iota(jnp.int32, (2 * pairs, 2 * side), 1) // half
    ).astype(bf16)

    def scan(k, carry, sums):
        flow, total = list(carry[0]), carry[1]
        state = [keep_ref[k, s * ns : (s + 1) * ns, :] for s in range(rows)]
        base = pl.multiple_of(k * inner, inner)
        for t in range(STEPS):
            for s in range(rows):
                at = (s * STEPS + t) * ns
                fade = jnp.exp2(rate * eff_s[s * chunks + k, t : t + 1, :])
                held = fade * state[s]
                fade_s[at : at + ns, :] = fade
                held_s[at : at + ns, :] = held
                drive = u_s[s * chunks + k, t : t + 1, :] * tile_rows(bb_ref, k, at, ns, inner, cb)
                state[s] = held + drive
                gc_s[pl.ds(base + at, ns), :] += lane_sum(state[s] * gy_s[s * chunks + k, t : t + 1, :])
        for t in reversed(range(STEPS)):
            for s in range(rows):
                at = (s * STEPS + t) * ns
                push = gy_s[s * chunks + k, t : t + 1, :] * tile_rows(cc_ref, k, at, ns, inner, cb)
                grad = flow[s] + push
                gb_s[pl.ds(base + at, ns), :] += lane_sum(grad * u_s[s * chunks + k, t : t + 1, :])
                w = grad * held_s[at : at + ns, :]
                total = total + w * eff_s[s * chunks + k, t : t + 1, :]
                gu = grad * tile_rows(bb_ref, k, at, ns, inner, cb)
                wa = w * rate_n
                low = (s * STEPS + t) * half
                sums[low : low + half, :] = gu[:half] + gu[half:]
                sums[side + low : side + low + half, :] = wa[:half] + wa[half:]
                flow[s] = fade_s[at : at + ns, :] * grad
        return tuple(flow), total

    def leave(k, sums):
        out = dot(pick, sums[...].astype(bf16))
        for s in range(rows):
            gu_s[s * chunks + k] = out[s * STEPS : (s + 1) * STEPS]
            gd_s[s * chunks + k] = out[pairs + s * STEPS : pairs + (s + 1) * STEPS]

    sb[...] = jnp.zeros_like(sb)

    def two(i, carry):
        k = chunks - 1 - 2 * i
        leave(jnp.minimum(k + 1, chunks - 1), sb)
        carry = scan(k, carry, sa)
        leave(k, sa)
        return scan(k - 1, carry, sb)

    first = tuple(start[s * ns : (s + 1) * ns] for s in range(rows))
    _, total = lax.fori_loop(0, chunks // 2, two, (first, jnp.zeros((ns, cb), f32)))
    leave(0, sb)
    grate_ref[...] = total * rate_n
    gu = gu_s[...].reshape(delta.shape)
    gact_ref[...] = gu * delta + skip_ref[...] * gy
    gskip_ref[...] = jnp.sum(gy * act, axis=0, keepdims=True)
    gpre = (gu * act + gd_s[...].reshape(delta.shape)) * (1.0 - jnp.exp(-delta))
    gbias_ref[...] = jnp.sum(gpre, axis=0, keepdims=True)
    gpre16 = gpre.astype(bf16)
    gdtw_ref[...] = dot(rank_t_ref[...], gpre16)
    grank_s[...] += dot_nt(gpre16, dtw_ref[...])


def fold_part(rows, ns, gproj_ref, gproj_t_ref, gb_s, gc_s, grank_s):
    pairs = rows * STEPS
    inner = pairs * ns
    chunks = gb_s.shape[0] // inner
    ones = jnp.ones((128, 128), bf16)
    lane = lax.broadcasted_iota(jnp.int32, (pairs, ns, 128), 2)
    spot = lax.broadcasted_iota(jnp.int32, (pairs, ns, 128), 1)
    rank = grank_s.shape[1]

    def fold(ref, k):
        high, low = halves(ref[k * inner : (k + 1) * inner, :])
        v = (dot(high, ones) + dot(low, ones)).reshape(pairs, ns, 128)
        return jnp.sum(jnp.where(lane == spot, v, 0.0), axis=1)[:, :ns]

    for k in range(chunks):
        gb, gc = fold(gb_s, k), fold(gc_s, k)
        for s in range(rows):
            here = slice((s * chunks + k) * STEPS, (s * chunks + k + 1) * STEPS)
            mine = slice(s * STEPS, (s + 1) * STEPS)
            gproj_ref[here, :] = jnp.concatenate([grank_s[here, :], gb[mine], gc[mine]], axis=1)
    gproj_t_ref[...] = gproj_ref[...].T


def backward_kernel(rows, n, sizes, *refs):
    blocks, narrow, rank, ns, taps = sizes
    (gg_ref, z_ref, y_ref, wdelta_ref, full_w, kill_ref, full_ref, sum_ref, act_ref, delta_ref, full_n,
     half_n, rank_t_ref, bb_ref, cc_ref, keep_ref, x_ref, halo_ref, mask_ref) = refs[:19]
    refs = refs[19:]
    cut = Packed(rank, ns, taps)
    wrate_ref, rates_ref, rate_ref, skip_ref = cut.rate(full_w), cut.rate(full_ref), cut.rate(full_n), cut.skip(full_n)
    dtw_ref, xp_ref, kern_ref, off_ref = cut.dtproj(half_n), cut.xproj(half_n), cut.kernel(full_n), cut.offset(full_n)
    srcs, refs = refs[:n], refs[n:]
    (mixed_ref, packed_ref), refs = refs[:2], refs[2:]
    sums, refs = refs[:n], refs[n:]
    (weff_s, wgy_s, gyall_s, end_s, start_s, gz_s, gact_s, gproj_s, gproj_t_s, gend_s, edge_s, late_s, gdtw_s, gbias_s, grate_s,
     gskip_s, gxp_s, gkern_s, goff_s), refs = refs[:19], refs[19:]
    (eff_s, u_s, gy_s, fade_s, held_s, sa, sb, gu_s, gd_s, gb_s, gc_s, grank_s), refs = refs[:12], refs[12:]
    exch, (esend, erecv), refs = refs[:20], refs[20:22], refs[22:]
    here = Place()
    block = pl.program_id(0)
    wide_cb, cb = gg_ref.shape[1], act_ref.shape[1]
    c = wide_cb * blocks

    def edge(j):
        return push(edge_s.at[j], late_s.at[j], esend, erecv, j, here.ring(-1))

    @pl.when(block == 0)
    def _():
        greet(here.partners() + [here.ring(1), here.ring(-1)])
        gc_s[...] = jnp.zeros_like(gc_s)
        gb_s[...] = jnp.zeros_like(gb_s)
        grank_s[...] = jnp.zeros_like(grank_s)

    exchanges(here, True, rows, end_s, sum_ref, rates_ref, start_s, exch, block, blocks // 2)
    beside(Reduces(srcs, sums, refs), block, BACKWARD_STEPS)

    @pl.when(block < blocks)
    def _():
        gy, flow = back_ends_part(
            rows, gg_ref, z_ref, y_ref, wdelta_ref, kill_ref, wrate_ref, cc_ref, gz_s, weff_s, wgy_s
        )
        cols = pl.ds(pl.multiple_of(block * wide_cb, wide_cb), wide_cb)
        mixed_ref[:, pl.ds(pl.multiple_of(c + block * wide_cb, wide_cb), wide_cb)] = gz_s[...]
        gyall_s[:, cols] = gy.astype(f32)
        end_s[:, cols] = flow

    @pl.when((block >= blocks) & (block < blocks + narrow))
    def _():
        j = block - blocks
        cols = pl.ds(pl.multiple_of(j * cb, cb), cb)
        back_part(rows, act_ref, delta_ref, gyall_s[:, cols], kill_ref, rate_ref, skip_ref, dtw_ref, rank_t_ref,
                  bb_ref, cc_ref, keep_ref, start_s[:, cols], gact_s.at[j], gdtw_s.at[j], gbias_s.at[j], grate_s.at[j], gskip_s.at[j],
                  eff_s, u_s, gy_s, fade_s, held_s, sa, sb, gu_s, gd_s, gb_s, gc_s, grank_s)

    @pl.when(block == blocks + narrow - 1)
    def _():
        fold_part(rows, rate_ref.shape[0], gproj_s, gproj_t_s, gb_s, gc_s, grank_s)

    @pl.when(block >= blocks + narrow)
    def _():
        j = block - blocks - narrow
        cols = pl.ds(pl.multiple_of(j * cb, cb), cb)
        gx, edges = conv_back_part(
            rows, x_ref, halo_ref, kern_ref, off_ref, mask_ref, act_ref, gact_s[j], gproj_s, gproj_t_s, xp_ref,
            gxp_s, gkern_s, goff_s
        )
        rows_of = [gxp_s[...], gdtw_s[j], grate_s[j], gkern_s[...], goff_s[...], gbias_s[j], gskip_s[j]]
        count = sum(v.shape[0] for v in rows_of)
        rows_of.append(jnp.zeros((packed_ref.shape[0] - count, cb), f32))
        packed_ref[...] = jnp.concatenate(rows_of, axis=0).astype(bf16)
        edge_s[j] = edges.astype(bf16)
        edge(j).start()
        mixed_ref[:, cols] = gx.astype(bf16)
        length = gx.shape[0] // rows
        gend_s[j] = jnp.concatenate([gx[(s + 1) * length - 16 : (s + 1) * length] for s in range(rows)], axis=0)

    @pl.when(block == pl.num_programs(0) - 1)
    def _():
        more = jnp.where((here.z == 3) & (here.c == 1), 0.0, 1.0)
        length = mixed_ref.shape[0] // rows
        for j in range(narrow):
            edge(j).wait()
            late = late_s[j].astype(f32) * more
            for s in range(rows):
                end = gend_s[j, 16 * s : 16 * s + 16]
                fixed = jnp.concatenate([end[:8], end[8:] + late[8 * s : 8 * s + 8]], axis=0)
                mixed_ref[(s + 1) * length - 16 : (s + 1) * length, j * cb : (j + 1) * cb] = fixed.astype(bf16)
        Reduces(srcs, sums, refs).run(-1)


def ends_kernel(rows, act_ref, rank2_ref, dtw_ref, bias_ref, kill_ref, rate_ref, bb_ref,
                delta_ref, end_ref, sum_ref, eff_s, u_s):
    delta_ref[...], sum_ref[...], end_ref[...] = ends_part(
        rows, act_ref[...], rank2_ref, dtw_ref, bias_ref, kill_ref, rate_ref, bb_ref, eff_s, u_s
    )


def scan_kernel(rows, act_ref, delta_ref, z_ref, kill_ref, rate_ref, skip_ref, bb_ref, cd_ref, start_ref, *refs):
    scan_part(rows, delta_ref[...], act_ref[...], z_ref[...], kill_ref, rate_ref, skip_ref, bb_ref, cd_ref, start_ref[...], *refs)


def back_ends_kernel(rows, gg_ref, z_ref, y_ref, delta_ref, kill_ref, rate_ref, cc_ref,
                     gy_ref, gz_ref, end_ref, eff_s, gy_s):
    gy_ref[...], end_ref[...] = back_ends_part(
        rows, gg_ref, z_ref, y_ref, delta_ref, kill_ref, rate_ref, cc_ref, gz_ref, eff_s, gy_s
    )


def back_kernel(rows, act_ref, delta_ref, gy_ref, kill_ref, rate_ref, skip_ref, dtw_ref, rank_t_ref,
                bb_ref, cc_ref, keep_ref, start_ref,
                gact_ref, gproj_ref, gproj_t_ref, gdtw_ref, gbias_ref, grate_ref, gskip_ref, *scratch):
    gb_s, gc_s, grank_s = scratch[-3:]

    @pl.when(pl.program_id(0) == 0)
    def _():
        gc_s[...] = jnp.zeros_like(gc_s)
        gb_s[...] = jnp.zeros_like(gb_s)
        grank_s[...] = jnp.zeros_like(grank_s)

    back_part(rows, act_ref, delta_ref, gy_ref[...].astype(f32), kill_ref, rate_ref, skip_ref, dtw_ref, rank_t_ref,
              bb_ref, cc_ref, keep_ref, start_ref[...], gact_ref, gdtw_ref, gbias_ref, grate_ref, gskip_ref, *scratch)

    @pl.when(pl.program_id(0) == pl.num_programs(0) - 1)
    def _():
        fold_part(rows, rate_ref.shape[0], gproj_ref, gproj_t_ref, gb_s, gc_s, grank_s)


def conv_back_part(rows, x_ref, halo_ref, kern_ref, off_ref, mask_ref, act_ref, gact, gproj_ref,
                   gproj_t_ref, xp_ref, gxp_ref, gkern_ref, goff_ref):
    x = x_ref[...].astype(bf16).astype(f32)
    cb = x.shape[1]
    halo = halo_ref[...].astype(f32)
    kernel = kern_ref[...]
    taps = kernel.shape[0]
    masks = [wide(mask_ref[i], cb) for i in range(taps - 1)]
    pre = conv_sum(x, halo, kernel, off_ref[...], masks, rows)
    sig = sigmoid(pre)
    act16 = act_ref[...].astype(bf16)
    gxp_ref[...] = dot(gproj_t_ref[...].astype(bf16), act16)
    g_act = gact + dot(gproj_ref[...].astype(bf16), xp_ref[...])
    gpre = g_act * sig * (1.0 + pre * (1.0 - sig))
    goff_ref[...] = jnp.sum(gpre, axis=0, keepdims=True)
    length = x.shape[0] // rows
    place = lax.broadcasted_iota(jnp.int32, (length, cb), 0)
    gk = [jnp.zeros((1, cb), f32) for _ in range(taps)]
    gxs, edges = [], []
    for s in range(rows):
        here = slice(s * length, (s + 1) * length)
        g = gpre[here]
        ext = jnp.concatenate([halo[8 * s : 8 * s + 8], x[here]], axis=0)
        gk[taps - 1] = gk[taps - 1] + jnp.sum(g * x[here], axis=0, keepdims=True)
        gx = kernel[taps - 1 : taps] * g
        edge = jnp.zeros((length, cb), f32)
        for lag in range(1, taps):
            gm = g * masks[lag - 1][here]
            moved = pltpu.roll(ext, lag, 0)[8:]
            j = taps - 1 - lag
            gk[j] = gk[j] + jnp.sum(gm * moved, axis=0, keepdims=True)
            up = pltpu.roll(kernel[j : j + 1] * gm, length - lag, 0)
            inside = place < length - lag
            gx = gx + jnp.where(inside, up, 0.0)
            edge = edge + jnp.where(inside, 0.0, up)
        gxs.append(gx)
        edges.append(edge[length - 8 :])
    gkern_ref[...] = jnp.concatenate(gk, axis=0)
    return jnp.concatenate(gxs, axis=0), jnp.concatenate(edges, axis=0)


def conv_back_kernel(rows, x_ref, halo_ref, kern_ref, off_ref, mask_ref, act_ref, gact_ref, gproj_ref,
                     gproj_t_ref, xp_ref, gx_ref, edge_ref, *outs):
    gx_ref[...], edge_ref[...] = conv_back_part(
        rows, x_ref, halo_ref, kern_ref, off_ref, mask_ref, act_ref, gact_ref[...], gproj_ref, gproj_t_ref, xp_ref, *outs
    )


def col(rows, cb, shift=0):
    return pl.BlockSpec((rows, cb), lambda j: (0, j + shift))


def whole(*shape):
    return pl.BlockSpec(shape, lambda j: (0,) * len(shape))


def call(body, blocks, ins, outs, scratch, args, ident=None):
    more = {} if ident is None else dict(collective_id=ident, has_side_effects=True)
    return pl.pallas_call(
        body,
        grid=(blocks,),
        in_specs=ins,
        out_specs=[spec for spec, _, _ in outs],
        out_shape=[jax.ShapeDtypeStruct(shape, kind) for _, shape, kind in outs],
        scratch_shapes=scratch,
        compiler_params=pltpu.CompilerParams(
            dimension_semantics=("arbitrary",), vmem_limit_bytes=VMEM, **more
        ),
    )(*args)


class Mixer:
    def __init__(self, layers, rows, length, channels, ns, rank, taps):
        self.layers = layers
        self.rows, self.length, self.c, self.ns, self.rank, self.taps = rows, length, channels, ns, rank, taps
        self.tokens = rows * length
        self.chunks = length // STEPS
        self.pairs = rows * STEPS
        self.inner = self.pairs * ns
        self.width = rank + 2 * ns

    def conv(self, projected, halo, p, masks):
        t, c, cb = self.tokens, self.c, CB
        tall = (t * self.ns, 128)
        out = call(
            functools.partial(conv_kernel, self.rows, (self.rank, self.ns)), c // cb,
            [col(t, cb), col(8 * self.rows, cb), col(self.taps, cb), col(1, cb), whole(*masks.shape), col(self.width, cb)],
            [(col(t, cb), (t, c), f32), (whole(t, 2 * self.rank), (t, 2 * self.rank), bf16),
             (whole(self.rank, t), (self.rank, t), bf16), (whole(*tall), tall, f32), (whole(*tall), tall, f32),
             (whole(t, self.inner), (t, self.inner), f32)],
            [pltpu.VMEM((t, self.width), f32)], (projected, halo, p["conv_w"], p["conv_b"], masks, p["xproj"]),
        )
        m = dict(zip(("rank2", "rank_t", "bb", "cc", "cd"), out[1:]))
        m["cd"] = m["cd"].reshape(-1, STEPS, self.inner)
        return out[0], m

    def scratch3(self, cb):
        return pltpu.VMEM((self.tokens // STEPS, STEPS, cb), f32)

    def wide_scratch(self, kind, cb):
        return pltpu.VMEM((self.inner, cb), kind)

    def forward(self, i, h, gain, in_full, half, full, masks, kill, gathers, ident):
        t, c, sn, cb, nb, ns, d = self.tokens, self.c, self.rows * self.ns, CB_SCAN, CB, self.ns, h.shape[1]
        narrow, blocks = c // nb, c // cb
        front = 2 * narrow
        hn, fn = half.shape[0] // self.layers, full.shape[0] // self.layers

        def first(rows):
            return pl.BlockSpec((rows, nb), lambda j: (0, jnp.minimum(j, narrow - 1)))

        def second(rows):
            return pl.BlockSpec((rows, nb), lambda j: (0, jnp.clip(j - narrow, 0, narrow - 1)))

        def early(rows):
            return pl.BlockSpec((rows, cb), lambda j: (0, jnp.clip(j - front, 0, blocks - 1)))

        def both(rows):
            return pl.BlockSpec((rows, cb), lambda j: (0, lax.rem(jnp.maximum(j - front, 0), blocks)))

        def late(rows):
            return pl.BlockSpec((rows, cb), lambda j: (0, jnp.maximum(j - front - blocks, 0)))

        def at(spec):
            return pl.BlockSpec(spec.block_shape, lambda j: (i, spec.index_map(j)[1]))

        wx = pl.BlockSpec((nb, d), lambda j: (jnp.minimum(j, narrow - 1), 0))
        wz = pl.BlockSpec((nb, d), lambda j: (jnp.minimum(j, narrow - 1) + narrow, 0))
        n = len(gathers)
        keep = pl.BlockSpec((self.chunks, sn, cb), lambda j: (0, 0, jnp.maximum(j - front - blocks, 0)))
        sems = [pltpu.SemaphoreType.DMA((GATHER_SEMS * max(n, 1),))] * 2 + [pltpu.SemaphoreType.DMA((narrow,))] * 2
        tall = (t * ns, 128)
        hr = 8 * self.rows
        out = call(
            functools.partial(forward_kernel, self.rows, [k for _, k in gathers], (self.rank, ns, self.taps, narrow, blocks)), front + 2 * blocks,
            [whole(t, d), whole(1, d), wx, wz, at(second(fn)), at(second(hn)), whole(*masks.shape), at(early(hn)),
             whole(*kill.shape), at(both(fn)), pl.BlockSpec((fn, c), lambda j: (i, 0))] + [ANY] * n,
            [(whole(t, d), (t, d), bf16), (first(t), (t, c), bf16), (first(t), (t, c), f32), (second(hr), (hr, c), bf16),
             (second(t), (t, c), f32), (whole(self.rank, t), (self.rank, t), bf16), (whole(*tall), tall, f32),
             (whole(*tall), tall, f32), (early(t), (t, c), f32), (whole(self.rows, c), (self.rows, c), f32),
             (late(t), (t, c), bf16), (late(t), (t, c), bf16), (keep, (self.chunks, sn, c), f32)]
            + [(ANY, (2, 2, 4, 2) + g.shape[1:], g.dtype) for g, _ in gathers],
            [pltpu.VMEM((t, self.width), f32), pltpu.VMEM((narrow, t, nb), bf16), pltpu.VMEM((narrow, hr, nb), bf16),
             pltpu.VMEM((narrow, hr, nb), bf16), pltpu.VMEM((blocks, t, cb), f32), pltpu.VMEM((blocks, t, cb), f32),
             pltpu.VMEM((t, 2 * self.rank), bf16), pltpu.VMEM((t // STEPS, STEPS, self.inner), f32),
             self.scratch3(cb), self.scratch3(cb), self.wide_scratch(bf16, cb), self.wide_scratch(bf16, cb),
             self.scratch3(cb), pltpu.VMEM((blocks, t, cb), f32), pltpu.VMEM((sn, c), f32), pltpu.VMEM((sn, c), f32),
             pltpu.VMEM((self.rows, c), f32)] + exchange_scratch(self.rows, sn, c // 2) * 2 + sems,
            (h, gain, in_full, in_full, full, half, masks, half, kill, full, full, *[g for g, _ in gathers]),
            ident,
        )
        return out[:13], [g.reshape(-1, g.shape[-1]) for g in out[13:]]

    def backward(self, i, gg, x, z, halo, y, act, delta, total, m, half, full, masks, kill, keep, sums, ident):
        t, c, sn, ns, cb, wcb = self.tokens, self.c, self.rows * self.ns, self.ns, CB_BACK, CB_ENDS
        blocks, narrow = c // wcb, c // cb

        def early(rows):
            return pl.BlockSpec((rows, wcb), lambda j: (0, jnp.minimum(j, blocks - 1)))

        def late(rows):
            return pl.BlockSpec((rows, cb), lambda j: (0, jnp.clip(j - blocks, 0, narrow - 1)))

        def last(rows):
            return pl.BlockSpec((rows, cb), lambda j: (0, jnp.maximum(j - blocks - narrow, 0)))

        def twice(rows):
            return pl.BlockSpec((rows, cb), lambda j: (0, lax.rem(jnp.maximum(j - blocks, 0), narrow)))

        def at(spec):
            return pl.BlockSpec(spec.block_shape, lambda j: (i, spec.index_map(j)[1]))

        hn, fn = half.shape[0] // self.layers, full.shape[0] // self.layers
        kept = pl.BlockSpec((self.chunks, sn, cb), lambda j: (0, 0, jnp.clip(j - blocks, 0, narrow - 1)))
        tall = m["bb"].shape
        hr = 8 * self.rows
        pack = self.width + self.rank + ns + self.taps + 3
        pack += -pack % 64
        more_in, more_out, more_scratch = reduce_parts(sums)
        sems = [pltpu.SemaphoreType.DMA((narrow,))] * 2
        out = call(
            functools.partial(backward_kernel, self.rows, len(sums), (blocks, narrow, self.rank, ns, self.taps)), blocks + 2 * narrow,
            [early(t), early(t), early(t), early(t), at(early(fn)), whole(*kill.shape), pl.BlockSpec((fn, c), lambda j: (i, 0)),
             whole(self.rows, c), twice(t), late(t), at(twice(fn)), at(twice(hn)), whole(*m["rank_t"].shape), whole(*tall),
             whole(*tall), kept, last(t), last(hr), whole(*masks.shape)] + [ANY] * len(sums),
            [(whole(t, 2 * c), (t, 2 * c), bf16), (last(pack), (pack, c), bf16)]
            + [(whole(*v.shape), v.shape, f32) for v in more_out],
            [self.scratch3(wcb)] * 2 + [pltpu.VMEM((t, c), f32), pltpu.VMEM((sn, c), f32), pltpu.VMEM((sn, c), f32)]
            + [pltpu.VMEM((t, wcb), bf16), pltpu.VMEM((narrow, t, cb), f32), pltpu.VMEM((t, self.width), f32),
               pltpu.VMEM((self.width, t), f32), pltpu.VMEM((narrow, 2 * hr, cb), f32), pltpu.VMEM((narrow, hr, cb), bf16),
               pltpu.VMEM((narrow, hr, cb), bf16)]
            + [pltpu.VMEM((narrow, k, cb), f32) for k in (self.rank, 1, ns, 1)]
            + [pltpu.VMEM((k, cb), f32) for k in (self.width, self.taps, 1)]
            + [self.scratch3(cb)] * 3 + [self.wide_scratch(f32, cb)] * 4 + [self.scratch3(cb)] * 2
            + [pltpu.VMEM(tall, f32)] * 2 + [pltpu.VMEM((t, self.rank), f32)] + exchange_scratch(self.rows, sn, c // 2) * 2
            + sems + more_scratch,
            (gg, z, y, delta, full, kill, full, total, act, delta, full, half, m["rank_t"], m["bb"], m["cc"], keep, x, halo,
             masks, *more_in),
            ident,
        )
        return out[:2], out[2:]

    def ends(self, act, m, p, kill):
        t, c, sn, cb = self.tokens, self.c, self.rows * self.ns, CB_ENDS
        return call(
            functools.partial(ends_kernel, self.rows), c // cb,
            [col(t, cb), whole(*m["rank2"].shape), col(self.rank, cb), col(1, cb), whole(*kill.shape), col(self.ns, cb),
             whole(*m["bb"].shape)],
            [(col(t, cb), (t, c), f32), (col(sn, cb), (sn, c), f32), (col(self.rows, cb), (self.rows, c), f32)],
            [self.scratch3(cb), self.scratch3(cb)],
            (act, m["rank2"], p["dtproj"], p["dt_b"], kill, p["rate"], m["bb"]),
        )

    def scan(self, act, delta, projected, m, p, kill, start):
        t, c, sn, cb = self.tokens, self.c, self.rows * self.ns, CB_SCAN
        keep = pl.BlockSpec((self.chunks, sn, cb), lambda j: (0, 0, j))
        return call(
            functools.partial(scan_kernel, self.rows), c // cb,
            [col(t, cb), col(t, cb), col(t, cb, c // cb), whole(*kill.shape), col(self.ns, cb), col(1, cb),
             whole(*m["bb"].shape), whole(*m["cd"].shape), col(sn, cb)],
            [(col(t, cb), (t, c), bf16), (col(t, cb), (t, c), bf16), (keep, (self.chunks, sn, c), f32)],
            [self.scratch3(cb), self.scratch3(cb), self.wide_scratch(bf16, cb), self.wide_scratch(bf16, cb),
             self.scratch3(cb)],
            (act, delta, projected, kill, p["rate"], p["skip"], m["bb"], m["cd"], start),
        )

    def back_ends(self, gg, projected, y, delta, m, p, kill):
        t, c, sn, cb = self.tokens, self.c, self.rows * self.ns, CB_ENDS
        return call(
            functools.partial(back_ends_kernel, self.rows), c // cb,
            [col(t, cb), col(t, cb, c // cb), col(t, cb), col(t, cb), whole(*kill.shape), col(self.ns, cb),
             whole(*m["cc"].shape)],
            [(col(t, cb), (t, c), bf16), (col(t, cb), (t, c), bf16), (col(sn, cb), (sn, c), f32)],
            [self.scratch3(cb), self.scratch3(cb)],
            (gg, projected, y, delta, kill, p["rate"], m["cc"]),
        )

    def back(self, act, delta, gy, m, p, kill, keep, start):
        t, c, sn, ns, cb = self.tokens, self.c, self.rows * self.ns, self.ns, CB_BACK
        kept = pl.BlockSpec((self.chunks, sn, cb), lambda j: (0, 0, j))
        tall = m["bb"].shape
        return call(
            functools.partial(back_kernel, self.rows), c // cb,
            [col(t, cb), col(t, cb), col(t, cb), whole(*kill.shape), col(ns, cb), col(1, cb), col(self.rank, cb),
             whole(*m["rank_t"].shape), whole(*tall), whole(*tall), kept, col(sn, cb)],
            [(col(t, cb), (t, c), f32), (whole(t, self.width), (t, self.width), f32),
             (whole(self.width, t), (self.width, t), f32), (col(self.rank, cb), (self.rank, c), f32),
             (col(1, cb), (1, c), f32), (col(ns, cb), (ns, c), f32), (col(1, cb), (1, c), f32)],
            [self.scratch3(cb)] * 3 + [self.wide_scratch(f32, cb)] * 4 + [self.scratch3(cb)] * 2
            + [pltpu.VMEM(tall, f32)] * 2 + [pltpu.VMEM((t, self.rank), f32)],
            (act, delta, gy, kill, p["rate"], p["skip"], p["dtproj"], m["rank_t"], m["bb"], m["cc"], keep, start),
        )

    def conv_back(self, projected, halo, p, masks, act, gact, gproj, gproj_t):
        t, c, cb = self.tokens, self.c, CB
        return call(
            functools.partial(conv_back_kernel, self.rows), c // cb,
            [col(t, cb), col(8 * self.rows, cb), col(self.taps, cb), col(1, cb), whole(*masks.shape), col(t, cb),
             col(t, cb), whole(t, self.width), whole(self.width, t), col(self.width, cb)],
            [(col(t, cb), (t, c), f32), (col(8 * self.rows, cb), (8 * self.rows, c), f32),
             (col(self.width, cb), (self.width, c), f32), (col(self.taps, cb), (self.taps, c), f32),
             (col(1, cb), (1, c), f32)],
            [], (projected, halo, p["conv_w"], p["conv_b"], masks, act, gact, gproj, gproj_t, p["xproj"]),
        )


MESH = pl.DeviceIdType.MESH
ANY = pl.BlockSpec(memory_space=pl.ANY)
INV = pl.BlockSpec(memory_space=pltpu.VMEM)


class Place:
    def __init__(self):
        r, b = lax.axis_index("rows"), lax.axis_index("bytes")
        self.y, self.x, self.z, self.c = r // 2, lax.rem(r, 2), b // 2, lax.rem(b, 2)

    def at(self, y=None, x=None, z=None, c=None):
        y = self.y if y is None else y
        x = self.x if x is None else x
        z = self.z if z is None else z
        c = self.c if c is None else c
        return (y * 2 + x, z * 2 + c)

    def over(self, k):
        return lax.rem(self.z + k, 4)

    def ring(self, step):
        b = lax.rem(self.z * 2 + self.c + 8 + step, 8)
        return self.at(z=b // 2, c=lax.rem(b, 2))

    def partners(self):
        return [self.at(c=1 - self.c), self.at(x=1 - self.x), self.at(y=1 - self.y)] + [
            self.at(z=self.over(k)) for k in (1, 2, 3)
        ]


def greet(partners):
    barrier = pltpu.get_barrier_semaphore()
    for p in partners:
        pl.semaphore_signal(barrier, inc=1, device_id=p, device_id_type=MESH)
    pl.semaphore_wait(barrier, len(partners))


def push(src, dst, send, recv, i, device):
    return pltpu.make_async_remote_copy(
        src_ref=src, dst_ref=dst, send_sem=send.at[i], recv_sem=recv.at[i], device_id=device, device_id_type=MESH
    )


GATHER_SEMS = 36
TURN = (1, 3, 2)


class Gather:
    def __init__(self, here, src, dst, send, recv, base):
        self.here, self.src, self.dst, self.send, self.recv, self.base = here, src, dst, send, recv, base
        self.h = src.shape[0] // 2
        part = functools.partial
        self.phases = [self.begin, part(self.side, 0), part(self.come, 1), part(self.come, 3), part(self.side, 1),
                       part(self.come, 2), part(self.side, 3), part(self.side, 2), self.cross, self.last]

    def source(self, k):
        return lax.rem(self.here.z + 4 - k, 4)

    def own(self):
        h = self.here
        return pltpu.make_async_copy(self.src, self.dst.at[h.y, h.x, h.z, h.c], self.send.at[self.base + 35])

    def push(self, src, dst, i, device):
        return push(src, dst, self.send, self.recv, self.base + i, device)

    def line(self, k):
        h = self.here
        return self.push(self.src, self.dst.at[h.y, h.x, h.z, h.c], k - 1, h.at(z=h.over(k)))

    def sides(self, k):
        h = self.here
        dst = self.dst.at[h.y, h.x, self.source(k), h.c]
        src = self.src if k == 0 else dst
        return [
            self.push(src, dst, 3 + k, h.at(x=1 - h.x)),
            self.push(src, dst, 7 + k, h.at(y=1 - h.y)),
        ]

    def across(self, k):
        h, z = self.here, self.source(k)
        top, low = pl.ds(0, self.h), pl.ds(self.h, self.h)
        u, v = self.dst.at[1 - h.y, h.x, z, h.c, top], self.dst.at[h.y, 1 - h.x, z, h.c, low]
        return [
            self.push(u, u, 11 + k, h.at(x=1 - h.x)),
            self.push(v, v, 15 + k, h.at(y=1 - h.y)),
        ]

    def core(self, k, part):
        h, z = self.here, self.source(k)
        y, x = ((h.y, h.x), (h.y, 1 - h.x), (1 - h.y, h.x), (1 - h.y, 1 - h.x))[part]
        dst = self.dst.at[y, x, z, h.c]
        src = self.src if (k == 0 and part == 0) else dst
        return self.push(src, dst, 19 + 4 * k + part, h.at(c=1 - h.c))

    def begin(self):
        self.own().start()
        for k in TURN:
            self.line(k).start()
        for copy in self.sides(0):
            copy.start()
        self.core(0, 0).start()

    def come(self, k):
        self.line(k).wait_recv()
        for copy in self.sides(k):
            copy.start()
        self.core(k, 0).start()

    def side(self, k):
        for copy in self.sides(k):
            copy.wait_recv()
        for copy in self.across(k):
            copy.start()
        self.core(k, 1).start()
        self.core(k, 2).start()

    def cross(self):
        for k in (0,) + TURN:
            for copy in self.across(k):
                copy.wait_recv()
            self.core(k, 3).start()

    def last(self):
        self.own().wait()
        for k in TURN:
            self.line(k).wait_send()
        for k in range(4):
            for copy in self.sides(k) + self.across(k):
                copy.wait_send()
            for part in range(4):
                self.core(k, part).wait()


class GatherBytes:
    def __init__(self, here, src, dst, send, recv, base):
        self.here, self.src, self.dst, self.send, self.recv, self.base = here, src, dst, send, recv, base
        self.w = src.shape[1]
        self.q = src.shape[0] // 4
        self.phases = [self.begin, self.second, self.third, self.fourth, self.last]

    def spot(self, z, c, q=None, n=1):
        cols = pl.ds(pl.multiple_of((z * 2 + c) * self.w, self.w), self.w)
        if q is None:
            return self.dst.at[:, cols]
        return self.dst.at[pl.ds(pl.multiple_of(q * self.q, self.q), n * self.q), cols]

    def source(self, k):
        return lax.rem(self.here.z + 4 - k, 4)

    def push(self, src, dst, i, device):
        return push(src, dst, self.send, self.recv, self.base + i, device)

    def own(self):
        h = self.here
        return pltpu.make_async_copy(self.src, self.spot(h.z, h.c), self.send.at[self.base + 13])

    def line(self, k):
        h = self.here
        q = h.y * 2 + h.x
        src = self.src.at[pl.ds(pl.multiple_of(q * self.q, self.q), self.q)]
        return self.push(src, self.spot(h.z, h.c, q), k - 1, h.at(z=h.over(k)))

    def over_x(self, k):
        h = self.here
        u = self.spot(self.source(k), h.c, h.y * 2 + h.x)
        return self.push(u, u, 2 + k, h.at(x=1 - h.x))

    def over_y(self, k):
        h = self.here
        u = self.spot(self.source(k), h.c, h.y * 2, 2)
        return self.push(u, u, 5 + k, h.at(y=1 - h.y))

    def core(self, k):
        h = self.here
        u = self.spot(self.source(k), h.c)
        src = self.src if k == 0 else u
        return self.push(src, u, 9 + k, h.at(c=1 - h.c))

    def begin(self):
        self.own().start()
        for k in TURN:
            self.line(k).start()
        self.core(0).start()

    def second(self):
        for k in TURN:
            self.line(k).wait_recv()
            self.over_x(k).start()

    def third(self):
        for k in TURN:
            self.over_x(k).wait_recv()
            self.over_y(k).start()

    def fourth(self):
        for k in TURN:
            self.over_y(k).wait_recv()
            self.core(k).start()

    def last(self):
        self.own().wait()
        for k in TURN:
            self.line(k).wait_send()
            self.over_x(k).wait_send()
            self.over_y(k).wait_send()
        for k in range(4):
            self.core(k).wait()


def run_phases(jobs, plans):
    for step in range(max(plan[-1] for plan in plans) + 1):
        for job, plan in zip(jobs, plans):
            for phase, at in zip(job.phases, plan):
                if at == step:
                    phase()


GATHER_PLAN = (0, 2, 4, 6, 8, 10, 12, 14, 16, 18)
NEXT_PLAN = (0, 3, 7, 9, 11, 13, 15, 17, 19, 20)
SMALL_PLAN = (0, 3, 6, 9, 15)
REDUCE_PLAN = (0, 1, 2, 3, 4, 5, 6, 7, 8, 9, 10, 11)
SIDES_PLAN = (8, 10)
ALL_PLAN = (6, 8, 9, 10, 11)
SMALL_REDUCE = (0, 1, 2, 2, 2, 2, 2, 5, 5, 5, 5, 7)


def gather_kernel(xp_ref, dtw_ref, rate_ref, kern_ref, off_ref, bias_ref, skip_ref, in_ref, out_ref,
                  half_ref, full_ref, win_ref, wout_ref, half_s, full_s, send, recv):
    here = Place()
    greet(here.partners())
    layers = xp_ref.shape[0]
    hn, fn = half_s.shape[0] // layers, full_s.shape[0] // layers
    for i in range(layers):
        width = xp_ref.shape[1]
        half_s[i * hn : i * hn + width, :] = xp_ref[i]
        half_s[i * hn + width : (i + 1) * hn, :] = dtw_ref[i]
        parts = [-jnp.exp(rate_ref[i]), kern_ref[i], off_ref[i : i + 1], bias_ref[i : i + 1], skip_ref[i : i + 1]]
        rest = fn - sum(v.shape[0] for v in parts)
        full_s[i * fn : (i + 1) * fn, :] = jnp.concatenate(parts + [jnp.zeros((rest, full_s.shape[1]), f32)], axis=0)
    jobs = [
        GatherBytes(here, half_s, half_ref, send, recv, 0),
        GatherBytes(here, full_s, full_ref, send, recv, GATHER_SEMS),
        Gather(here, in_ref.at[0], win_ref, send, recv, 2 * GATHER_SEMS),
        Gather(here, out_ref.at[0], wout_ref, send, recv, 3 * GATHER_SEMS),
    ]
    run_phases(jobs, [SMALL_PLAN, SMALL_PLAN, GATHER_PLAN, NEXT_PLAN])


def gather_all(xp, dtw, decay, kern, off, bias, skip, in_weight, out_weight, ident):
    layers, width, w = xp.shape
    half = (layers * (width + dtw.shape[1]), w)
    rows = decay.shape[1] + kern.shape[1] + 3
    full = (layers * (rows + -rows % 32), w)
    sems = pltpu.SemaphoreType.DMA((GATHER_SEMS * 4,))
    outs = [jax.ShapeDtypeStruct((half[0], 8 * w), bf16), jax.ShapeDtypeStruct((full[0], 8 * w), f32)]
    outs += [jax.ShapeDtypeStruct((2, 2, 4, 2) + a.shape[1:], bf16) for a in (in_weight, out_weight)]
    half, full, win, wout = pl.pallas_call(
        gather_kernel,
        out_shape=outs,
        in_specs=[INV] * 7 + [ANY] * 2,
        out_specs=[ANY] * 4,
        scratch_shapes=[pltpu.VMEM(half, bf16), pltpu.VMEM(full, f32), sems, sems],
        compiler_params=pltpu.CompilerParams(collective_id=ident, has_side_effects=True, vmem_limit_bytes=VMEM),
    )(xp, dtw, decay, kern, off, bias, skip, in_weight, out_weight)
    return half, full, win.reshape(-1, win.shape[-1]), wout.reshape(-1, wout.shape[-1])


REDUCE_SEMS = 27
FAR = (2, 1, 3, 0)


def reduce_scratch(rows, d):
    def buf(*lead, r=rows):
        return pltpu.VMEM(lead + (r, d), bf16)

    return [buf(2, 2, 4), buf(2, 2, 4), buf(4, r=rows // 2), buf(4, r=rows // 2), buf(4), buf(4), buf(3)]


class Reduce:
    def __init__(self, here, src, out, bufs, send, recv, base):
        self.here, self.src, self.out, self.send, self.recv, self.base = here, src, out, send, recv, base
        self.acc, self.rc, self.da, self.db, self.rx, self.ry, self.rz = bufs
        self.h = src.shape[4] // 2
        h = here
        self.parts = [(1 - h.y, 1 - h.x), (1 - h.y, h.x), (h.y, 1 - h.x), (h.y, h.x)]
        self.phases = (
            [self.begin, self.cross, self.pairs]
            + [functools.partial(self.side, k) for k in FAR]
            + [functools.partial(self.mine, k) for k in FAR]
            + [self.last]
        )

    def push(self, src, dst, i, device):
        return push(src, dst, self.send, self.recv, self.base + i, device)

    def own(self, part):
        y, x = self.parts[part]
        return pltpu.make_async_copy(
            self.src.at[y, x, :, self.here.c], self.acc.at[y, x], self.send.at[self.base + 23 + part]
        )

    def cores(self, part):
        y, x = self.parts[part]
        return self.push(
            self.src.at[y, x, :, 1 - self.here.c], self.rc.at[y, x], 19 + part, self.here.at(c=1 - self.here.c)
        )

    def across(self, k):
        h, z = self.here, self.here.over(k)
        block = self.acc.at[1 - h.y, 1 - h.x, z]
        return [
            self.push(block.at[pl.ds(0, self.h)], self.da.at[z], 3 + k, h.at(x=1 - h.x)),
            self.push(block.at[pl.ds(self.h, self.h)], self.db.at[z], 7 + k, h.at(y=1 - h.y)),
        ]

    def sides(self, k):
        h, z = self.here, self.here.over(k)
        return [
            self.push(self.acc.at[h.y, 1 - h.x, z], self.rx.at[z], 11 + k, h.at(x=1 - h.x)),
            self.push(self.acc.at[1 - h.y, h.x, z], self.ry.at[z], 15 + k, h.at(y=1 - h.y)),
        ]

    def line(self, k):
        h = self.here
        return self.push(self.acc.at[h.y, h.x, h.over(k)], self.rz.at[k - 1], k - 1, h.at(z=h.over(k)))

    def pair(self, part):
        y, x = self.parts[part]
        self.own(part).wait()
        self.cores(part).wait_recv()

        @pl.loop(0, 4)
        def _(z):
            self.acc[y, x, z] = self.acc[y, x, z] + self.rc[y, x, z]

    def begin(self):
        for part in range(4):
            self.cores(part).start()
            self.own(part).start()

    def cross(self):
        self.pair(0)
        for k in FAR:
            for copy in self.across(k):
                copy.start()

    def pairs(self):
        for part in (1, 2, 3):
            self.pair(part)

    def side(self, k):
        h, a, n = self.here, self.acc, self.h
        z = h.over(k)
        for copy in self.across(k):
            copy.wait_recv()
        a[1 - h.y, h.x, z, :n] = a[1 - h.y, h.x, z, :n] + self.da[z]
        a[h.y, 1 - h.x, z, n:] = a[h.y, 1 - h.x, z, n:] + self.db[z]
        for copy in self.sides(k):
            copy.start()

    def mine(self, k):
        h, a = self.here, self.acc
        z = h.over(k)
        for copy in self.sides(k):
            copy.wait_recv()
        a[h.y, h.x, z] = a[h.y, h.x, z] + self.rx[z] + self.ry[z]
        if k:
            self.line(k).start()

    def last(self):
        h = self.here
        total = self.acc[h.y, h.x, h.z].astype(f32)
        for k in (1, 3, 2):
            self.line(k).wait()
            total = total + self.rz[k - 1].astype(f32)
        self.out[...] = total
        for k in range(4):
            for copy in self.across(k) + self.sides(k):
                copy.wait_send()
            self.cores(k).wait_send()


class Reduces:
    def __init__(self, srcs, outs, scratch):
        per = len(reduce_scratch(16, 128))
        self.here = Place()
        self.jobs = [
            Reduce(self.here, src, out, scratch[per * i : per * (i + 1)], scratch[-2], scratch[-1], REDUCE_SEMS * i)
            for i, (src, out) in enumerate(zip(srcs, outs))
        ]

        self.phases = [functools.partial(self.run, i) for i in range(12)]

    def run(self, phase):
        for job in self.jobs:
            job.phases[phase]()


def reduce_parts(arrays):
    arrays = [a.reshape(2, 2, 4, 2, a.shape[0] // 32, a.shape[1]) for a in arrays]
    scratch = []
    for a in arrays:
        scratch += reduce_scratch(*a.shape[4:])
    if arrays:
        sems = pltpu.SemaphoreType.DMA((REDUCE_SEMS * len(arrays),))
        scratch += [sems, sems]
    return arrays, [jax.ShapeDtypeStruct(a.shape[4:], f32) for a in arrays], scratch


def beside(work, block, steps):
    for step in sorted(set(steps)):

        @pl.when(block == step)
        def _(step=step):
            for phase, at in enumerate(steps):
                if at == step:
                    work.phases[phase]()


SIDE_SEMS = 4


class Sides:
    def __init__(self, here, src, dst, send, recv, base):
        self.here, self.src, self.dst, self.send, self.recv, self.base = here, src, dst, send, recv, base
        self.phases = [self.begin, self.last]

    def copies(self):
        h = self.here
        dst = self.dst.at[h.y, h.x]
        to = [h.at(x=1 - h.x), h.at(y=1 - h.y), h.at(x=1 - h.x, y=1 - h.y)]
        return [push(self.src, dst, self.send, self.recv, self.base + i, p) for i, p in enumerate(to)]

    def begin(self):
        for copy in self.copies():
            copy.start()
        self.dst[self.here.y, self.here.x] = self.src[...]

    def last(self):
        for copy in self.copies():
            copy.wait()


ALL_SEMS = 6


class AllSum:
    def __init__(self, here, src, out, got, send, recv, base):
        self.here, self.src, self.out, self.got, self.send, self.recv, self.base = here, src, out, got, send, recv, base
        self.phases = [self.begin, functools.partial(self.turn, 0), functools.partial(self.turn, 1), self.along, self.last]

    def copy(self, i):
        h = self.here
        p = h.partners()[i]
        return push(self.got.at[6 + min(i, 3)], self.got.at[i], self.send, self.recv, self.base + i, p)

    def begin(self):
        self.got[6] = self.src[...]
        self.copy(0).start()

    def turn(self, i):
        self.copy(i).wait()
        self.got[7 + i] = self.got[6 + i] + self.got[i]
        self.copy(i + 1).start()

    def along(self):
        self.copy(2).wait()
        self.got[9] = self.got[8] + self.got[2]
        for i in (3, 4, 5):
            self.copy(i).start()

    def last(self):
        for i in (3, 4, 5):
            self.copy(i).wait()
        self.out[...] = self.got[9] + self.got[3] + self.got[4] + self.got[5]


def finish_kernel(cuts, small_ref, big_ref, w_ref, mixed_ref, before_ref, flow_ref, gain_ref, upper_ref,
                  flow_out, in_out, gain_out, *refs):
    outs, refs = refs[: len(cuts)], refs[len(cuts) :]
    per = len(reduce_scratch(16, 128))
    one, two, refs = refs[:per], refs[per : 2 * per], refs[2 * per :]
    w_s, gn_s, mine_s, plane_s, gains_s, got_s, send, recv, wsem = refs
    here = Place()
    greet(here.partners() + [here.at(x=1 - here.x, y=1 - here.y)])
    load = pltpu.make_async_copy(w_ref, w_s, wsem)
    load.start()
    base = 2 * REDUCE_SEMS
    small = Reduce(here, small_ref, mine_s, one, send, recv, 0)
    big = Reduce(here, big_ref, in_out, two, send, recv, REDUCE_SEMS)
    gains = AllSum(here, gains_s, gain_out, got_s, send, recv, base)
    plane = Sides(here, mine_s, plane_s, send, recv, base + ALL_SEMS)

    class Norm:
        def run(self):
            load.wait()
            depth = 512
            gn_s[...] = jnp.zeros_like(gn_s)

            @pl.loop(0, mixed_ref.shape[1] // depth)
            def _(k):
                at = pl.ds(pl.multiple_of(k * depth, depth), depth)
                gn_s[...] += dot(mixed_ref[:, at], w_s[at, :])

            gn, before, gain = gn_s[...], before_ref[...].astype(f32), gain_ref[...]
            inv = lax.rsqrt(jnp.mean(before * before, axis=1, keepdims=True) + norm_eps)
            scaled = before * inv
            gs = gn * gain
            flow_out[...] = flow_ref[...] + inv * (gs - scaled * jnp.mean(gs * scaled, axis=1, keepdims=True))
            gains_s[0:1, :] = jnp.sum(gn * scaled, axis=0, keepdims=True)
            gains_s[1:, :] = upper_ref[...]

        def __init__(self):
            self.phases = [self.run]

    run_phases(
        [small, big, Norm(), gains, plane],
        [SMALL_REDUCE, REDUCE_PLAN, (6,), ALL_PLAN, SIDES_PLAN],
    )
    rows, d = mine_s.shape
    layers = upper_ref.shape[0] + 1
    whole_sum = plane_s[...].reshape(4 * rows, d)
    per_layer = 4 * rows // layers
    for layer in range(layers):
        at = layer * per_layer
        for cut, out in zip(cuts, outs):
            v = whole_sum[at : at + cut]
            if len(out.shape) == 2:
                out[layer : layer + 1, :] = v
            else:
                out[layer] = v
            at += cut


def finish(packed, grad_in, in_full, mixed, before, flowing, gain, upper, cuts, ident):
    arrays = [a.reshape(2, 2, 4, 2, a.shape[0] // 32, a.shape[1]) for a in (packed, grad_in)]
    (rows, w), d = arrays[0].shape[4:], before.shape[1]
    layers = upper.shape[0] + 1
    outs = [jax.ShapeDtypeStruct(before.shape, f32), jax.ShapeDtypeStruct(arrays[1].shape[4:], f32),
            jax.ShapeDtypeStruct((layers, d), f32)]
    outs += [jax.ShapeDtypeStruct((layers, cut, w) if cut > 1 else (layers, w), f32) for cut in cuts]
    scratch = reduce_scratch(rows, w) + reduce_scratch(*arrays[1].shape[4:])
    scratch += [pltpu.VMEM(in_full.shape, bf16), pltpu.VMEM(before.shape, f32), pltpu.VMEM((rows, w), f32),
                pltpu.VMEM((2, 2, rows, w), f32), pltpu.VMEM((layers, d), f32), pltpu.VMEM((10, layers, d), f32)]
    sems = pltpu.SemaphoreType.DMA((REDUCE_SEMS * 2 + ALL_SEMS + SIDE_SEMS,))
    return pl.pallas_call(
        functools.partial(finish_kernel, cuts),
        out_shape=outs,
        in_specs=[ANY] * 3 + [INV] * 5,
        out_specs=[INV] * len(outs),
        scratch_shapes=scratch + [sems, sems, pltpu.SemaphoreType.DMA],
        compiler_params=pltpu.CompilerParams(collective_id=ident, has_side_effects=True, vmem_limit_bytes=VMEM),
    )(*arrays, in_full, mixed, before, flowing, gain, upper)


EXCHANGE_SEMS = 10


def exchange_scratch(rows, sn, c):
    h = c // 2
    sems = pltpu.SemaphoreType.DMA((EXCHANGE_SEMS,))
    return [pltpu.VMEM((sn, h), bf16)] * 4 + [
        pltpu.VMEM((rows, h), f32), pltpu.VMEM((1, rows, h), f32), pltpu.VMEM((4, sn, h), bf16),
        pltpu.VMEM((4, rows, h), f32), sems, sems,
    ]


class Exchange:
    def __init__(self, here, backward, rows, end_ref, sum_ref, rate_ref, out_ref, scratch, off, width):
        self.here, self.backward, self.rows = here, backward, rows
        self.end, self.sum, self.out = end_ref, sum_ref, out_ref
        self.sent, self.back, self.got, self.late, self.gsum, self.msum, self.line, self.lsum, self.send, self.recv = scratch
        half = width // 2
        self.mine = pl.ds(pl.multiple_of(off + here.c * half, half), half)
        self.theirs = pl.ds(pl.multiple_of(off + (1 - here.c) * half, half), half)
        self.other = here.at(c=1 - here.c)
        self.rate = rate_ref
        self.phases = [self.begin, self.second, self.third, self.last]

    def one(self):
        return [push(self.sent, self.got, self.send, self.recv, 0, self.other),
                push(self.msum.at[0], self.gsum, self.send, self.recv, 1, self.other)]

    def two(self):
        out = []
        for k in (1, 2, 3):
            to = self.here.at(z=self.here.over(k))
            out.append(push(self.line.at[3], self.line.at[k - 1], self.send, self.recv, 2 + 2 * k, to))
            out.append(push(self.lsum.at[3], self.lsum.at[k - 1], self.send, self.recv, 3 + 2 * k, to))
        return out

    def three(self):
        return push(self.back, self.late, self.send, self.recv, 2, self.other)

    def fade(self, total):
        rate = self.rate[:, self.mine]
        return jnp.concatenate([jnp.exp(rate * total[s : s + 1]) for s in range(self.rows)], axis=0)

    def pair(self):
        e_me, d_me = self.end[:, self.mine], self.sum[:, self.mine]
        e_it, d_it = self.got[...].astype(f32), self.gsum[...]
        first = self.here.c == 0
        return (jnp.where(first, e_me, e_it), jnp.where(first, e_it, e_me),
                jnp.where(first, d_me, d_it), jnp.where(first, d_it, d_me))

    def begin(self):
        self.sent[...] = self.end[:, self.theirs].astype(bf16)
        self.msum[0] = self.sum[:, self.theirs]
        for copy in self.one():
            copy.start()

    def second(self):
        for copy in self.one():
            copy.wait()
        e0, e1, d0, d1 = self.pair()
        chip = e0 + self.fade(d0) * e1 if self.backward else self.fade(d1) * e0 + e1
        self.line[3] = chip.astype(bf16)
        self.lsum[3] = d0 + d1
        for copy in self.two():
            copy.start()

    def third(self):
        for copy in self.two():
            copy.wait()
        e0, e1, d0, d1 = self.pair()
        state = jnp.zeros_like(e0)
        z = self.here.z
        for k in (1, 2, 3) if self.backward else (3, 2, 1):
            at = lax.rem(z + 4 - k, 4)
            e, d = self.line[k - 1].astype(f32), self.lsum[k - 1]
            use = at > z if self.backward else at < z
            state = jnp.where(use, self.fade(d) * state + e, state)
        if self.backward:
            s1, s0 = state, e1 + self.fade(d1) * state
        else:
            s0, s1 = state, self.fade(d0) * state + e0
        first = self.here.c == 0
        self.out[:, self.mine] = jnp.where(first, s0, s1)
        self.back[...] = jnp.where(first, s1, s0).astype(bf16)
        self.three().start()

    def last(self):
        self.three().wait()
        self.out[:, self.theirs] = self.late[...].astype(f32)


def exchanges(here, backward, rows, end_ref, sum_ref, rate_ref, out_ref, scratch, block, first):
    width = end_ref.shape[1] // 2
    for i in range(2):
        work = Exchange(here, backward, rows, end_ref, sum_ref, rate_ref, out_ref, scratch[10 * i : 10 * i + 10],
                        i * width, width)
        at = first + 2 * i
        beside(work, block, (at, at + 1, at + 2, at + 2))


def carried_in(ends, sums, rate, axis, backward):
    n = lax.axis_size(axis)
    rows = sums.shape[0]
    ns = rate.shape[0]

    def fade(total):
        return jnp.exp(total[:, None, :] * rate[None])

    def moved(v, shift):
        if backward:
            pairs = [(i, i - shift) for i in range(shift, n)]
        else:
            pairs = [(i, i + shift) for i in range(n - shift)]
        return lax.ppermute(v, axis, pairs)

    def shifted(e, s, shift):
        return moved(e.astype(bf16), shift).astype(f32), moved(s, shift)

    ends = ends.reshape(rows, ns, -1)
    ends, sums = shifted(ends, sums, 1)
    shift = 1
    while shift < n - 1:
        e, s = shifted(ends, sums, shift)
        ends = fade(sums) * e + ends
        sums = sums + s
        shift *= 2
    return ends.reshape(rows * ns, -1)


def body(
    tokens, boundaries, norm_gain, in_weight, out_weight, conv_weight, conv_bias, xproj_weight,
    dtproj_weight, dt_bias, decay_log, skip_gain, cotangent,
):
    rows, length, d = tokens.shape
    layers = norm_gain.shape[0]
    both = ("rows", "bytes")
    n = rows * length
    place = lax.axis_index("bytes") * length + jnp.arange(length, dtype=jnp.int32)
    reached = boundaries[:, None, :] <= place[None, :, None]
    starts = jnp.max(jnp.where(reached, boundaries[:, None, :], 0), axis=2)
    renewed = jnp.any(boundaries[:, None, :] == place[None, :, None], axis=2)
    kill = jnp.broadcast_to(jnp.where(renewed, KILL, 0.0).reshape(n, 1), (n, 128)).astype(f32)
    taps = conv_weight.shape[1]
    masks = jnp.stack(
        [
            jnp.broadcast_to((place[None, :] - lag >= starts).astype(f32).reshape(n, 1), (n, 128))
            for lag in range(1, taps)
        ]
    )
    fast = (lax.axis_size("rows"), lax.axis_size("bytes")) == (4, 8)
    if fast:
        half, full, first_in, first_out = gather_all(
            xproj_weight.transpose(0, 2, 1), dtproj_weight, decay_log, conv_weight, conv_bias, dt_bias, skip_gain, in_weight, out_weight, 1
        )
    else:
        half = jnp.concatenate([xproj_weight.transpose(0, 2, 1), dtproj_weight], axis=1)
        full = jnp.concatenate(
            [-jnp.exp(decay_log), conv_weight, conv_bias[:, None], dt_bias[:, None], skip_gain[:, None]], axis=1
        )
        half = lax.all_gather(half, "bytes", axis=2, tiled=True)
        full = lax.all_gather(full, "bytes", axis=2, tiled=True)
    ns = decay_log.shape[1]
    rank = dtproj_weight.shape[1]
    width = xproj_weight.shape[2]
    channels = full.shape[-1]
    mixer = Mixer(layers, rows, length, channels, ns, rank, taps)
    params = []
    for i in range(0 if fast else layers):
        rest = full[i, ns + taps :]
        params.append(
            dict(
                xproj=half[i, :width], dtproj=half[i, width:], conv_w=full[i, ns : ns + taps], conv_b=rest[:1],
                dt_b=rest[1:2], skip=rest[2:3], rate=full[i, :ns],
            )
        )
    if fast:
        in_fulls, out_fulls = {0: first_in}, {0: first_out}
    else:
        in_fulls = {i: lax.all_gather(in_weight[i], both, axis=0, tiled=True) for i in range(layers)}
        out_fulls = {i: lax.all_gather(out_weight[i], both, axis=0, tiled=True) for i in range(layers)}
    size = lax.axis_size("bytes")
    ahead = [(i, i + 1) for i in range(size - 1)]
    behind = [(i + 1, i) for i in range(size - 1)]
    current = tokens.astype(f32).reshape(n, d)
    saved = []
    for i in range(layers):
        p = None if fast else params[i]
        if fast:
            (normed, x, z, halo, act, rank_t, bb, cc, delta, total, y, gated, keep), whole_w = mixer.forward(
                i, current if i else tokens.reshape(n, d), norm_gain[i][None], in_fulls[i], half, full, masks, kill,
                ([(out_weight, i)] if i else []) + [(in_weight, j) for j in range(i + 1, min(i + 2, layers))], 2 + i,
            )
            m = dict(rank_t=rank_t, bb=bb, cc=cc)
            if i:
                out_fulls[i] = whole_w[0]
            if i + 1 < layers:
                in_fulls[i + 1] = whole_w[-1]
        else:
            normed = (
                current * lax.rsqrt(jnp.mean(current * current, axis=-1, keepdims=True) + norm_eps) * norm_gain[i]
            ).astype(bf16)
            projected = dot_nt(normed, in_fulls[i])
            tail = projected.reshape(rows, length, -1)[:, length - 8 :, :channels].astype(bf16)
            halo = lax.ppermute(tail, "bytes", ahead).reshape(8 * rows, channels)
            act, m = mixer.conv(projected, halo, p, masks)
            delta, end, total = mixer.ends(act, m, p, kill)
            start = carried_in(end, total, p["rate"], "bytes", False)
            y, gated, keep = mixer.scan(act, delta, projected, m, p, kill, start)
            x = z = projected
        saved.append((current, normed, x, z, halo, act, m, delta, total, y, gated, keep))
        current = current + dot(gated, out_fulls[i])
    flowing = cotangent.astype(f32).reshape(n, d)
    big, small, gains = [], [], []
    waiting, ready = [], []
    for i in reversed(range(layers)):
        p = None if fast else params[i]
        in_full, out_full = in_fulls[i], out_fulls[i]
        before, normed, x, z, halo, act, m, delta, total, y, gated, keep = saved[i]
        down = flowing.astype(bf16)
        grad_out = lax.dot_general(gated, down, (((0,), (0,)), ((), ())), preferred_element_type=f32).astype(bf16)
        gg = dot_nt(down, out_full)
        if fast:
            waiting.append(grad_out)
            (mixed, pieces), done = mixer.backward(
                i, gg, x, z, halo, y, act, delta, total, m, half, full, masks, kill, keep, waiting, 10 + i
            )
            ready += done
        else:
            gy, gz, gend = mixer.back_ends(gg, z, y, delta, m, p, kill)
            gstart = carried_in(gend, total, p["rate"], "bytes", True)
            gact, gproj, gproj_t, gdtw, gbias, grate, gskip = mixer.back(act, delta, gy, m, p, kill, keep, gstart)
            gx, edge, gxp, gkern, goff = mixer.conv_back(x, halo, p, masks, act, gact, gproj, gproj_t)
            late = lax.ppermute(edge.astype(bf16), "bytes", behind).astype(f32).reshape(rows, 8, channels)
            gx = (
                (gx.reshape(rows, length, channels) + jnp.pad(late, ((0, 0), (length - 8, 0), (0, 0))))
                .reshape(n, channels)
                .astype(bf16)
            )
            mixed = jnp.concatenate([gx, gz], axis=1)
            pieces = jnp.concatenate([gxp, gdtw, grate, gkern, goff, gbias, gskip], axis=0)
        grad_in = lax.dot_general(mixed, normed, (((0,), (0,)), ((), ())), preferred_element_type=f32).astype(bf16)
        small.append(pieces)
        waiting = [grad_in]
        if fast and i == 0:
            break
        gn = dot(mixed, in_full)
        inv = lax.rsqrt(jnp.mean(before * before, axis=-1, keepdims=True) + norm_eps)
        scaled = before * inv
        gains.append(jnp.sum(gn * scaled, axis=0))
        gs = gn * norm_gain[i]
        flowing = flowing + inv * (gs - scaled * jnp.mean(gs * scaled, axis=-1, keepdims=True))
        if not fast:
            big.append([lax.psum_scatter(g, both, scatter_dimension=0, tiled=True).astype(f32) for g in (grad_in, grad_out)])
    cuts = [width, rank, ns, taps, 1, 1, 1]
    if fast:
        packed = jnp.stack(small[::-1])
        packed = packed.reshape(4, layers * packed.shape[1] // 4, size, channels // size).transpose(0, 2, 1, 3)
        flowing, last_in, gain_total, *parts = finish(
            packed.reshape(-1, channels // size), grad_in, in_full, mixed, tokens.reshape(n, d), flowing, norm_gain[0][None],
            jnp.stack(gains[::-1]), cuts, 9,
        )
        ready.append(last_in)
        big = [(ready[2 * i + 1], ready[2 * i]) for i in range(layers)]
    else:
        packed = jnp.stack(small[::-1]).astype(bf16)
        packed = lax.psum_scatter(packed, "bytes", scatter_dimension=2, tiled=True)
        packed = lax.psum(packed, "rows").astype(f32)
        gain_total = lax.psum(jnp.stack(gains[::-1]), both)
        parts, at = [], 0
        for cut in cuts:
            parts.append(packed[:, at] if cut == 1 else packed[:, at : at + cut])
            at += cut
    big = big[::-1]
    return (
        current.reshape(rows, length, d),
        flowing.reshape(rows, length, d),
        gain_total,
        jnp.stack([b[0] for b in big]),
        jnp.stack([b[1] for b in big]),
        parts[3],
        parts[4],
        parts[0].transpose(0, 2, 1),
        parts[1],
        parts[5],
        parts[2],
        parts[6],
    )


def solution(mesh):
    split = P("rows", "bytes", None)
    shared = P(None, ("rows", "bytes"), None)
    in_specs = (
        split, P("rows", None), P(), shared, shared, P(None, None, "bytes"), P(None, "bytes"),
        P(None, "bytes", None), P(None, None, "bytes"), P(None, "bytes"), P(None, None, "bytes"),
        P(None, "bytes"), split,
    )
    out_specs = (
        split, split, P(), shared, shared, P(None, None, "bytes"), P(None, "bytes"), P(None, "bytes", None),
        P(None, None, "bytes"), P(None, "bytes"), P(None, None, "bytes"), P(None, "bytes"),
    )
    return jax.shard_map(body, mesh=mesh, in_specs=in_specs, out_specs=out_specs, check_vma=False)
```
